32 devices in a mesh: dp: 4 (over z), fsdp: 8 (over y, x, core).
Axes of the slice: x: 2, y: 2, z: 4, core: 2. Of those that a mesh axis runs over, the one named last changes fastest.
Arguments:
- tokens: bfloat16 [98304, 512], P(('dp', 'fsdp')), may hold values from -6 to 6
- lengths: int32 [96], P(('dp', 'fsdp')), may hold values from 256 to 1024, as said below
- w_query: bfloat16 [512, 512], P(None, ('dp', 'fsdp')), may hold values from -0.25 to 0.25
- w_key: bfloat16 [512, 512], P(None, ('dp', 'fsdp')), may hold values from -0.25 to 0.25
- w_value: bfloat16 [512, 512], P(None, ('dp', 'fsdp')), may hold values from -0.25 to 0.25
- w_out: bfloat16 [512, 512], P(None, ('dp', 'fsdp')), may hold values from -6 to 6
- w_up: bfloat16 [512, 2048], P(None, ('dp', 'fsdp')), may hold values from -0.25 to 0.25
- w_down: bfloat16 [2048, 512], P(None, ('dp', 'fsdp')), may hold values from -0.125 to 0.125
- bias_up: bfloat16 [2048], P(('dp', 'fsdp')), may hold values from -3 to 3
- bias_down: bfloat16 [512], P(('dp', 'fsdp')), may hold values from -4 to 4
- gain_attn: bfloat16 [512], P(('dp', 'fsdp')), may hold values from 0.099609375 to 1.8984375
- shift_attn: bfloat16 [512], P(('dp', 'fsdp')), may hold values from -3 to 3
- gain_ffn: bfloat16 [512], P(('dp', 'fsdp')), may hold values from 0.099609375 to 1.8984375
- shift_ffn: bfloat16 [512], P(('dp', 'fsdp')), may hold values from -3 to 3
- cotangent: bfloat16 [98304, 512], P(('dp', 'fsdp')), may hold values from -0.0390625 to 0.0390625
Outputs:
- output: bfloat16 [98304, 512], P(('dp', 'fsdp'))
- grad_tokens: bfloat16 [98304, 512], P(('dp', 'fsdp'))
- grad_w_query: float32 [512, 512], P(None, ('dp', 'fsdp'))
- grad_w_key: float32 [512, 512], P(None, ('dp', 'fsdp'))
- grad_w_value: float32 [512, 512], P(None, ('dp', 'fsdp'))
- grad_w_out: float32 [512, 512], P(None, ('dp', 'fsdp'))
- grad_w_up: float32 [512, 2048], P(None, ('dp', 'fsdp'))
- grad_w_down: float32 [2048, 512], P(None, ('dp', 'fsdp'))
- grad_bias_up: float32 [2048], P(('dp', 'fsdp'))
- grad_bias_down: float32 [512], P(('dp', 'fsdp'))
- grad_gain_attn: float32 [512], P(('dp', 'fsdp'))
- grad_shift_attn: float32 [512], P(('dp', 'fsdp'))
- grad_gain_ffn: float32 [512], P(('dp', 'fsdp'))
- grad_shift_ffn: float32 [512], P(('dp', 'fsdp'))
The draws below stay inside these ranges and needn't reach their ends.
Inputs may be any that keep to these rules, and one draw needn't show every extreme that they name: `lengths`: each entry is the number of real tokens at the start of a sequence slot of 1024; the rest of the slot is padding. Both ends of the range are taken in every draw.
All inputs are finite; a program needn't handle non-finite values.
Results may differ from the reference program's by a relative error of at most 0.03.
Values may be sent and summed in bfloat16 or wider, within the bound.
No kernel may reach another device: no remote copies, remote signals or barrier semaphores. Data moves between devices by JAX's collectives and lax.ppermute only.
A program may use at most 512 MiB of HBM per device.

```python
import jax
import jax.numpy as jnp
from jax import lax

D = 512
H = 8
DH = 64
FF = 2048
BLOCK = 16
LEVELS = 6
SEQ_DEV = 3
LEN = 1024
SEQS = 96
TOKENS = 98304


def draw_lengths(key, part):
    values = jax.random.randint(key, (SEQS,), LEN // 4, LEN + 1)
    values = values.at[0].set(LEN).at[1].set(LEN // 4)
    return values.astype(jnp.int32)


def with_spikes(values, own_key, source, target, shards_of, factor):
    def block_of(position):
        return (jnp.arange(values.shape[position]) // (values.shape[position] // shards_of)).reshape((-1,) + (1,) * (values.ndim - 1 - position))

    first = jax.random.permutation(own_key, shards_of)[block_of(target)]
    other_side = (block_of(target) + shards_of // 2) % shards_of
    return jnp.where((block_of(source) == first) | (block_of(source) == other_side), factor * values, values)


def block_levels(own_key, extent, cuts, smallest, largest):
    level, own = 1.0, jax.random.fold_in(own_key, 6)
    for dim, blocks in cuts:
        heights = jnp.exp(jax.random.uniform(jax.random.fold_in(own, dim), (blocks,), jnp.float32, smallest / len(cuts), largest / len(cuts)))
        level = level * jnp.repeat(heights, extent[dim] // blocks).reshape([-1 if axis == dim else 1 for axis in range(len(extent))])
    return level


def normal_values(stream_key, extent, scale, most, pieces=(), held_as=jnp.bfloat16):
    values = scale * jax.random.normal(stream_key, extent, jnp.float32)
    if pieces:
        values = values * block_levels(stream_key, extent, pieces, -0.22, 0.18)
    return jnp.clip(values, -most, most).astype(held_as)


def bell_draw_with(rng, dims, deviation, reach, split, heavy, kind=jnp.bfloat16):
    entries = deviation * jax.random.normal(rng, dims, jnp.float32)
    if split:
        entries = entries * block_levels(rng, dims, split, -0.22, 0.18)
    return jnp.clip(with_spikes(entries, jax.random.fold_in(rng, 3), *heavy), -reach, reach).astype(kind)


def setup_inputs(seed: int = 0) -> dict:
    seeds = jax.random.split(jax.random.key(seed), 16)
    tokens = normal_values(seeds[0], (TOKENS, D), 1.0, 6.0, ((0, 32),))
    lengths = draw_lengths(jax.random.fold_in(seeds[15], 71), 0)
    w_query = normal_values(seeds[2], (D, D), D ** -0.5, 0.25, ((1, 32),))
    w_key = normal_values(seeds[3], (D, D), D ** -0.5, 0.25, ((1, 32),))
    w_value = normal_values(seeds[4], (D, D), D ** -0.5, 0.25, ((1, 32),))
    w_out = normal_values(seeds[5], (D, D), (max(D // LEN, 1)) ** -0.5, 6.0, ((1, 32),))
    w_up = normal_values(seeds[6], (D, FF), D ** -0.5, 0.25, ((1, 32),))
    w_down = normal_values(seeds[7], (FF, D), FF ** -0.5, 0.125, ((1, 32),))
    bias_up = normal_values(seeds[8], (FF,), 0.5, 3.0, ((0, 32),))
    bias_down = normal_values(seeds[9], (D,), 1.0, 4.0, ((0, 32),))
    gain_attn = jnp.clip(1.0 + 0.18 * jax.random.normal(seeds[10], (D,), jnp.float32), 0.099609375, 1.8984375).astype(jnp.bfloat16)
    shift_attn = normal_values(seeds[11], (D,), 0.5, 3.0, ((0, 32),))
    gain_ffn = jnp.clip(1.0 + 0.18 * jax.random.normal(seeds[12], (D,), jnp.float32), 0.099609375, 1.8984375).astype(jnp.bfloat16)
    shift_ffn = normal_values(seeds[13], (D,), 0.5, 3.0, ((0, 32),))
    cotangent = bell_draw_with(seeds[14], (TOKENS, D), (TOKENS ** -0.5), 0.0390625, ((0, 32),), (0, 1, 32, 2.75))
    return {"tokens": tokens, "lengths": lengths, "w_query": w_query, "w_key": w_key, "w_value": w_value, "w_out": w_out, "w_up": w_up, "w_down": w_down, "bias_up": bias_up, "bias_down": bias_down, "gain_attn": gain_attn, "shift_attn": shift_attn, "gain_ffn": gain_ffn, "shift_ffn": shift_ffn, "cotangent": cotangent}


@jax.custom_vjp
def low(v):
    return lax.optimization_barrier(v.astype(jnp.bfloat16)).astype(jnp.float32)

@jax.custom_vjp
def low_back(v):
    return v

def low_keep(v):
    return (low(v), None)

def low_pass(kept, grad):
    return (grad,)

def back_keep(v):
    return (v, None)

def back_low(kept, grad):
    return (low(grad),)
low.defvjp(low_keep, low_pass)
low_back.defvjp(back_keep, back_low)
highest = lax.Precision.HIGHEST

def neighbours(values):
    widths = [(0, 0), (1, 1)] + [(0, 0)] * (values.ndim - 2)
    padded = jnp.pad(values, widths)
    return jnp.concatenate([padded[:, :-2], padded[:, 1:-1], padded[:, 2:]], axis=2)

def pair_mask(level_index, width):
    if level_index == 0:
        return jnp.ones((width, 3 * width), jnp.float32)
    rows_pos = lax.broadcasted_iota(jnp.int32, (width, 3 * width), 0)
    cols_pos = lax.broadcasted_iota(jnp.int32, (width, 3 * width), 1)
    query_half = 2 * rows_pos // width
    key_half = 2 * (cols_pos // width) - 2 + 2 * (cols_pos % width) // width
    return jnp.where(jnp.abs(query_half - key_half) > 1, 1.0, 0.0).astype(jnp.float32)

def halve_mean(values):
    return (values[:, 0::2] + values[:, 1::2]) * 0.5

def halve_sum(values):
    return values[:, 0::2] + values[:, 1::2]

def hier_attend(query, keys, vals, valid):
    seq_count = query.shape[0]
    score_scale = DH ** (-0.5)
    query_now = query
    keys_now = keys
    vals_now = vals * valid[:, :, None, None]
    valid_now = valid
    numer_list = []
    totals_list = []
    for level_index in range(LEVELS):
        if level_index > 0:
            query_now = halve_mean(query_now)
            keys_now = halve_mean(keys_now)
            vals_now = halve_sum(vals_now)
            valid_now = halve_sum(valid_now)
        length = query_now.shape[1]
        blocks = length // BLOCK
        query_low = low(query_now).reshape(seq_count, blocks, BLOCK, H, DH)
        keys_near = neighbours(low(keys_now).reshape(seq_count, blocks, BLOCK, H, DH))
        vals_near = neighbours(low(vals_now).reshape(seq_count, blocks, BLOCK, H, DH))
        valid_near = neighbours(valid_now.reshape(seq_count, blocks, BLOCK))
        allowed = pair_mask(level_index, BLOCK)
        weight = allowed[None, None, None] * valid_near[:, :, None, None, :]
        scores = low_back(jnp.einsum('snbhd,snchd->snhbc', query_low, keys_near, precision=highest) * score_scale)
        exp_scores = jnp.exp(scores)
        totals = lax.optimization_barrier(jnp.sum(exp_scores * weight, axis=-1))
        numerator = low_back(jnp.einsum('snhbc,snchd->snbhd', low(exp_scores * allowed), vals_near, precision=highest))
        numer_list.append(numerator.reshape(seq_count, length, H, DH))
        totals_list.append(jnp.transpose(totals, (0, 1, 3, 2)).reshape(seq_count, length, H))
    numer_all = numer_list[-1]
    totals_all = totals_list[-1]
    for level_index in range(LEVELS - 2, -1, -1):
        numer_all = jnp.repeat(numer_all, 2, axis=1) + numer_list[level_index]
        totals_all = jnp.repeat(totals_all, 2, axis=1) + totals_list[level_index]
    return numer_all / totals_all[:, :, :, None]

def layer_norm(values, gain, shift):
    centred = values - lax.optimization_barrier(jnp.mean(values, axis=-1, keepdims=True))
    normed = centred * lax.rsqrt(lax.optimization_barrier(jnp.mean(centred * centred, axis=-1, keepdims=True)) + 1e-05)
    return normed * gain + shift

def block_forward(params, rows, seq_lengths):
    w_query, w_key, w_value, w_out, w_up, w_down, bias_up, bias_down, gain_attn, shift_attn, gain_ffn, shift_ffn = params
    seq_count = seq_lengths.shape[0]
    valid = (lax.broadcasted_iota(jnp.int32, (seq_count, LEN), 1) < seq_lengths[:, None]).astype(jnp.float32)
    normed_attn = low(layer_norm(rows, gain_attn, shift_attn))
    query = low(low_back(jnp.dot(normed_attn, w_query, precision=highest)))
    keys = low(low_back(jnp.dot(normed_attn, w_key, precision=highest)))
    vals = low(low_back(jnp.dot(normed_attn, w_value, precision=highest)))
    shape_heads = (seq_count, LEN, H, DH)
    attn = hier_attend(query.reshape(shape_heads), keys.reshape(shape_heads), vals.reshape(shape_heads), valid)
    attn = low(low_back(attn.reshape(seq_count * LEN, D)))
    middle = rows + low_back(jnp.dot(attn, w_out, precision=highest))
    normed_ffn = low(layer_norm(middle, gain_ffn, shift_ffn))
    hidden = low_back(jnp.dot(normed_ffn, w_up, precision=highest) + bias_up)
    active = low(hidden * jax.nn.sigmoid(hidden))
    return middle + low_back(jnp.dot(active, w_down, precision=highest) + bias_down)

def reference(tokens, lengths, w_query, w_key, w_value, w_out, w_up, w_down, bias_up, bias_down, gain_attn, shift_attn, gain_ffn, shift_ffn, cotangent):
    params = (w_query.astype(jnp.float32), w_key.astype(jnp.float32), w_value.astype(jnp.float32), w_out.astype(jnp.float32), w_up.astype(jnp.float32), w_down.astype(jnp.float32), bias_up.astype(jnp.float32), bias_down.astype(jnp.float32), gain_attn.astype(jnp.float32), shift_attn.astype(jnp.float32), gain_ffn.astype(jnp.float32), shift_ffn.astype(jnp.float32))
    group_count = SEQS // SEQ_DEV
    rows = tokens.astype(jnp.float32).reshape(group_count, SEQ_DEV * LEN, D)
    grouped_lengths = lengths.reshape(group_count, SEQ_DEV)
    step_fn = jax.checkpoint(block_forward)

    def forward(params_in, rows_in):
        return lax.map(lambda grouped_item: step_fn(params_in, grouped_item[0], grouped_item[1]), (rows_in, grouped_lengths))
    result, pullback = jax.vjp(forward, params, rows)
    param_grads, row_grads = pullback(cotangent.astype(jnp.float32).reshape(group_count, SEQ_DEV * LEN, D))
    return (result.reshape(TOKENS, D).astype(jnp.bfloat16), row_grads.reshape(TOKENS, D).astype(jnp.bfloat16), param_grads[0], param_grads[1], param_grads[2], param_grads[3], param_grads[4], param_grads[5], param_grads[6], param_grads[7], param_grads[8], param_grads[9], param_grads[10], param_grads[11])
```

```python
import functools

import jax
import jax.numpy as jnp
import numpy as np
from jax import lax
from jax.experimental import pallas as pl
from jax.experimental.pallas import tpu as pltpu
from jax.sharding import PartitionSpec as P

D = 512
H = 8
DH = 64
FF = 2048
BLOCK = 16
LEVELS = 6
LEN = 1024
AXES = ("dp", "fsdp")
BF16 = jnp.bfloat16
F32 = jnp.float32

STARTS = (32, 1072, 1600, 1872, 2016, 2096)
SIZES = tuple(LEN >> level for level in range(LEVELS))
ROWS = 2192
GAPS = ((0, 32), (1056, 16), (1584, 16), (1856, 16), (2000, 16), (2080, 16), (2128, 64))
WINDOWS = 32
QUERIES = 64
KEYS = 128
UNROLL = 8
POOL_CHUNK = 256
SHARE = 16
FIRST_ROWS = 3 * SHARE + 8
SECOND_ROWS = 9 * SHARE + 8
SCORE = 0.125 * 1.4426950408889634


def nn(left, right):
    return lax.dot_general(left, right, (((1,), (0,)), ((), ())), preferred_element_type=F32)


def nt(left, right):
    return lax.dot_general(left, right, (((1,), (1,)), ((), ())), preferred_element_type=F32)


def tn(left, right):
    return lax.dot_general(left, right, (((0,), (0,)), ((), ())), preferred_element_type=F32)


def score_bias():
    query = (np.arange(2 * QUERIES) % QUERIES)[:, None]
    key = np.arange(KEYS)[None, :] - 32
    near = np.abs(query // 16 - key // 16) <= 1
    apart = np.abs(query // 8 - key // 8) > 1
    return np.where(np.stack([near, near & apart]), 0.0, -1e30).astype(np.float32)


def pool_matrix():
    matrix = np.zeros((POOL_CHUNK, POOL_CHUNK), np.float32)
    first = 0
    for level in range(1, LEVELS):
        count = POOL_CHUNK >> level
        for row in range(count):
            matrix[first + row, row << level : (row + 1) << level] = 0.5**level
        first += count
    return matrix


def halves():
    lane = np.arange(128)
    return np.stack([lane < DH, lane >= DH]).astype(np.float32)


def window_row(window):
    gaps = sum((window >= first).astype(jnp.int32) for first in (16, 24, 28, 30, 31))
    return pl.multiple_of(STARTS[0] + QUERIES * window + 16 * gaps, 16)


def window_loop(step, unroll=UNROLL):
    def body(index, carry):
        for inner in range(unroll):
            window = index * unroll + inner
            row = window_row(window)
            step(
                pl.ds(row, QUERIES),
                pl.ds(pl.multiple_of(row - 32, 16), KEYS),
                pl.ds(pl.multiple_of(window * 2 * QUERIES, 128), 2 * QUERIES),
                jnp.where(window >= 16, 1, 0),
            )
        return carry

    lax.fori_loop(0, WINDOWS // unroll, body, 0)


def row_loop(total, size, step, unroll=1):
    def body(index, carry):
        for inner in range(unroll):
            step(pl.multiple_of((index * unroll + inner) * size, size))
        return carry

    lax.fori_loop(0, total // (size * unroll), body, 0)


def pair_lanes(pair):
    return slice(128 * pair, 128 * pair + 128)


def by_head(values, half):
    return jnp.concatenate([values * half[0:1, :], values * half[1:2, :]], axis=0)


def joined_heads(values, low_head):
    return jnp.where(low_head, values[:QUERIES], values[QUERIES:])


def fill_counts(counts, length):
    clear_gaps(counts)
    for level in range(LEVELS):
        place = lax.broadcasted_iota(jnp.int32, (SIZES[level], 128), 0)
        span = 1 << level
        number = jnp.clip(length - place * span, 0, span).astype(F32)
        counts[STARTS[level] : STARTS[level] + SIZES[level], :] = number.astype(BF16)


def block_places(place, plain, sign):
    for half in range(2):
        for block in range(16):
            if plain:
                yield half, block, half * 16 + block
            else:
                column = place[1] ^ (half + 2 * (block // 4))
                row = (place[0] + 4 + sign * (block % 4)) % 4
                yield half, block, row * 8 + column


def sixteen(device):
    return pl.ds(pl.multiple_of(device * SHARE, SHARE), SHARE)


def sixty_four(device):
    return pl.ds(pl.multiple_of(device * 4 * SHARE, 4 * SHARE), 4 * SHARE)


def load_first(place, plain, blocks, weights, vectors):
    total = jnp.zeros((8, D), F32)
    for half, block, device in block_places(place, plain, -1):
        source = blocks[half]
        for part in range(3):
            rows = pl.ds(pl.multiple_of(part * D + device * SHARE, SHARE), SHARE)
            weights[rows, :] = source[block, part * SHARE : part * SHARE + SHARE, :]
        total = total + source[block, 3 * SHARE : 3 * SHARE + 8, :].astype(F32)
    vectors[...] = total


def load_second(place, plain, blocks, w_out, w_up, w_down, vectors):
    total = jnp.zeros((8, D), F32)
    for half, block, device in block_places(place, plain, -1):
        source = blocks[half]
        w_out[sixteen(device), :] = source[block, 0:SHARE, :]
        w_up[sixty_four(device), :] = source[block, SHARE : 5 * SHARE, :]
        for part in range(4):
            at = (5 + part) * SHARE
            w_down[sixteen(device), D * part : D * part + D] = source[block, at : at + SHARE, :]
        total = total + source[block, 9 * SHARE : 9 * SHARE + 8, :].astype(F32)
    vectors[...] = total


def layer_norm(values):
    mean = jnp.mean(values, axis=-1, keepdims=True)
    centred = values - mean
    inverse = lax.rsqrt(jnp.mean(centred * centred, axis=-1, keepdims=True) + 1e-05)
    return centred * inverse, inverse


def norm_back(gradient, normed, inverse, gain):
    scaled = gradient * gain
    return inverse * (
        scaled
        - jnp.mean(scaled, axis=-1, keepdims=True)
        - normed * jnp.mean(scaled * normed, axis=-1, keepdims=True)
    )


def clear_gaps(ref):
    for first, count in GAPS:
        ref[first : first + count, :] = jnp.zeros((count, ref.shape[1]), ref.dtype)


def spread_up(ref, factor):
    for level in range(LEVELS - 2, -1, -1):
        count = SIZES[level + 1]
        size = min(count, 64)

        def step(first, level=level, size=size):
            for pair in range(4):
                above = ref[pair, pl.ds(STARTS[level + 1] + first, size), :]
                if factor != 1.0:
                    above = above * factor
                for odd in (0, 1):
                    below = pl.ds(STARTS[level] + 2 * first + odd, size, stride=2)
                    ref[pair, below, :] = ref[pair, below, :] + above

        row_loop(count, size, step)


def attend_kernel(
    plain,
    lengths,
    place,
    tokens,
    near_blocks,
    far_blocks,
    bias,
    pool,
    half,
    query,
    key,
    value,
    probs,
    attn,
    total,
    weights,
    vectors,
    normed,
    joined,
    top,
    counts,
    numer,
    denom,
):
    @pl.when(pl.program_id(0) == 0)
    def _():
        load_first(place, plain, (near_blocks, far_blocks), weights, vectors)

    length = lengths[pl.program_id(0)]
    gain = vectors[0:1, :]
    shift = vectors[1:2, :]

    def norm_step(first):
        rows = pl.ds(first, 64)
        values, _ = layer_norm(tokens[rows, :].astype(F32))
        normed[rows, :] = (values * gain + shift).astype(BF16)

    row_loop(LEN, 64, norm_step, 4)
    for ref in (query, key, value):
        clear_gaps(ref)
    fill_counts(counts, length)
    targets = ((query, 0), (key, D), (value, 2 * D))
    for first in range(0, LEN, POOL_CHUNK):
        rows = slice(first, first + POOL_CHUNK)
        chunk = first // POOL_CHUNK
        values = nt(normed[rows, :], weights[...])
        valid = (lax.broadcasted_iota(jnp.int32, (POOL_CHUNK, 1), 0) + first < length).astype(F32)
        joined[rows, : 2 * D] = values[:, : 2 * D].astype(BF16)
        joined[rows, 2 * D :] = (values[:, 2 * D :] * valid).astype(BF16)
        pooled = nn(pool[...], joined[rows, :])
        for ref, lane in targets:
            start = STARTS[0] + first
            ref[start : start + POOL_CHUNK, :] = joined[rows, lane : lane + D]
            at = 0
            for level in range(1, LEVELS):
                count = POOL_CHUNK >> level
                part = pooled[at : at + count, lane : lane + D]
                at += count
                if ref is value:
                    part = part * float(1 << level)
                if level < LEVELS - 1:
                    start = STARTS[level] + chunk * count
                    ref[start : start + count, :] = part.astype(BF16)
                else:
                    top[chunk * count : chunk * count + count, lane : lane + D] = part
    for ref, lane in targets:
        ref[STARTS[-1] : STARTS[-1] + SIZES[-1], :] = top[:, lane : lane + D].astype(BF16)

    def score_step(rows, near, flat, kind):
        allowed = bias[kind]
        for pair in range(4):
            lanes = pair_lanes(pair)
            scores = nt(by_head(query[rows, lanes], half), key[near, lanes])
            probs[flat, lanes] = jnp.exp2(scores * SCORE + allowed).astype(BF16)

    window_loop(score_step)
    low_head = lax.broadcasted_iota(jnp.int32, (QUERIES, 128), 1) < DH

    def value_step(rows, near, flat, kind):
        number = counts[near, :]
        for pair in range(4):
            lanes = pair_lanes(pair)
            both = nn(probs[flat, lanes], jnp.concatenate([value[near, lanes], number], axis=1))
            numer[pair, rows, :] = joined_heads(both[:, :128], low_head)
            denom[pair, rows, :] = joined_heads(both[:, 128:], low_head)

    window_loop(value_step)
    spread_up(numer, 1.0)
    spread_up(denom, 1.0)

    def join_step(first):
        rows = pl.ds(first, 64)
        inner = pl.ds(STARTS[0] + first, 64)
        for pair in range(4):
            lanes = pair_lanes(pair)
            below = denom[pair, inner, :]
            attn[rows, lanes] = (numer[pair, inner, :] / below).astype(BF16)
            total[rows, lanes] = below

    row_loop(LEN, 64, join_step, 2)


def feed_kernel(
    plain,
    place,
    tokens,
    attn,
    total,
    cotangent,
    near_blocks,
    far_blocks,
    output,
    middle_grad,
    numer_grad,
    total_grad,
    near_grads,
    far_grads,
    w_out,
    w_up,
    w_down,
    vectors,
    middle,
    normed,
    inverse,
    normed_low,
    hidden,
    result,
    active,
    back,
    sums,
    acc_out,
    acc_up,
    acc_down,
):
    @pl.when(pl.program_id(0) == 0)
    def _():
        acc_out[...] = jnp.zeros_like(acc_out)
        acc_up[...] = jnp.zeros_like(acc_up)
        acc_down[...] = jnp.zeros_like(acc_down)
        sums[...] = jnp.zeros_like(sums)
        load_second(place, plain, (near_blocks, far_blocks), w_out, w_up, w_down, vectors)

    gain = vectors[0:1, :]
    shift = vectors[1:2, :]
    bias_down = vectors[2:3, :]
    middle[...] = nt(attn[...], w_out[...])

    def norm_step(first):
        rows = pl.ds(first, 64)
        values = middle[rows, :] + tokens[rows, :].astype(F32)
        middle[rows, :] = values
        norm, factor = layer_norm(values)
        normed[rows, :] = norm
        inverse[rows, :] = jnp.broadcast_to(factor, (64, 128))
        normed_low[rows, :] = (norm * gain + shift).astype(BF16)

    row_loop(LEN, 64, norm_step, 4)
    for part in range(FF // D):
        lanes = slice(D * part, D * part + D)
        hidden[...] = nt(normed_low[...], w_up[lanes, :])
        result[...] = nn(cotangent[...], w_down[:, lanes])
        bias_up = vectors[3 + part : 4 + part, :]

        def act_step(first, bias_up=bias_up, part=part):
            rows = pl.ds(first, 64)
            value = hidden[rows, :] + bias_up
            gate = 0.5 * jnp.tanh(0.5 * value) + 0.5
            active[rows, :] = (value * gate).astype(BF16)
            slope = gate * (1.0 + value * (1.0 - gate))
            gradient = (result[rows, :] * slope).astype(BF16)
            back[rows, :] = gradient
            at = 8 * (3 + part)
            sums[at : at + 8, :] += jnp.sum(gradient.astype(F32).reshape(8, 8, D), axis=0)

        row_loop(LEN, 64, act_step)
        acc_down[:, lanes] += tn(cotangent[...], active[...])
        acc_up[lanes, :] += tn(back[...], normed_low[...])
        middle[...] += nt(active[...], w_down[:, lanes])
        down = nn(back[...], w_up[lanes, :])
        gathered = down if part == 0 else gathered + down
    result[...] = gathered

    def back_step(first):
        rows = pl.ds(first, 64)
        output[rows, :] = (middle[rows, :] + bias_down).astype(BF16)
        gradient = result[rows, :]
        norm = normed[rows, :]
        value = cotangent[rows, :].astype(F32)
        sums[0:8, :] += jnp.sum((gradient * norm).reshape(8, 8, D), axis=0)
        sums[8:16, :] += jnp.sum(gradient.reshape(8, 8, D), axis=0)
        sums[16:24, :] += jnp.sum(value.reshape(8, 8, D), axis=0)
        value = value + norm_back(gradient, norm, inverse[rows, 0:1], gain)
        middle_grad[rows, :] = value.astype(BF16)

    row_loop(LEN, 64, back_step, 4)
    acc_out[...] += tn(middle_grad[...], attn[...])
    result[...] = nn(middle_grad[...], w_out[...])

    def numer_step(first):
        rows = pl.ds(first, 64)
        gradient = result[rows, :].astype(BF16).astype(F32) / total[rows, :]
        numer_grad[rows, :] = gradient.astype(BF16)
        total_grad[rows, :] = (-gradient * attn[rows, :].astype(F32)).astype(BF16)

    row_loop(LEN, 64, numer_step, 2)

    @pl.when(pl.program_id(0) == pl.num_programs(0) - 1)
    def _():
        small = jnp.sum(sums[...].reshape(7, 8, D), axis=1)
        small = jnp.concatenate([small, jnp.zeros((1, D), F32)], axis=0).astype(BF16)
        for half, block, device in block_places(place, plain, 1):
            target = (near_grads, far_grads)[half]
            target[block, 0:SHARE, :] = acc_out[sixteen(device), :].astype(BF16)
            target[block, SHARE : 5 * SHARE, :] = acc_up[sixty_four(device), :].astype(BF16)
            for part in range(4):
                at = (5 + part) * SHARE
                grads = acc_down[sixteen(device), D * part : D * part + D]
                target[block, at : at + SHARE, :] = grads.astype(BF16)
            target[block, 9 * SHARE : 9 * SHARE + 8, :] = small


def attend_back_kernel(
    plain,
    lengths,
    place,
    tokens,
    middle_grad,
    numer_grad,
    total_grad,
    query,
    key,
    value,
    probs,
    near_blocks,
    far_blocks,
    pool,
    half,
    grad_tokens,
    near_grads,
    far_grads,
    weights,
    vectors,
    numer,
    denom,
    score_grad,
    total,
    joined,
    normed,
    counts,
    top,
    sums,
    acc,
    result,
):
    step_index = pl.program_id(0)
    length = lengths[step_index]

    @pl.when(step_index == 0)
    def _():
        acc[...] = jnp.zeros_like(acc)
        sums[...] = jnp.zeros_like(sums)
        load_first(place, plain, (near_blocks, far_blocks), weights, vectors)

    gain = vectors[0:1, :]
    shift = vectors[1:2, :]
    clear_gaps(numer)
    clear_gaps(denom)
    fill_counts(counts, length)
    for source, target in ((numer_grad, numer), (total_grad, denom)):
        target[STARTS[0] : STARTS[0] + LEN, :] = source[...]
        for first in range(0, LEN, POOL_CHUNK):
            chunk = first // POOL_CHUNK
            pooled = nn(pool[...], source[first : first + POOL_CHUNK, :])
            at = 0
            for level in range(1, LEVELS):
                count = POOL_CHUNK >> level
                part = pooled[at : at + count] * float(1 << level)
                at += count
                if level < LEVELS - 1:
                    start = STARTS[level] + chunk * count
                    target[start : start + count, :] = part.astype(BF16)
                else:
                    top[chunk * count : chunk * count + count, :] = part
        target[STARTS[-1] : STARTS[-1] + SIZES[-1], :] = top[...].astype(BF16)

    def score_step(rows, near, flat, kind):
        number = counts[near, :]
        for pair in range(4):
            lanes = pair_lanes(pair)
            left = jnp.concatenate(
                [by_head(numer[rows, lanes], half), by_head(denom[rows, lanes], half)], axis=1
            )
            right = jnp.concatenate([value[near, lanes], number], axis=1)
            score_grad[flat, lanes] = (nt(left, right) * probs[flat, lanes].astype(F32)).astype(BF16)

    window_loop(score_step)
    low_head = lax.broadcasted_iota(jnp.int32, (QUERIES, 128), 1) < DH

    def query_step(rows, near, flat, kind):
        for pair in range(4):
            lanes = pair_lanes(pair)
            both = nn(score_grad[flat, lanes], key[near, lanes])
            total[pair, rows, :] = joined_heads(both, low_head)

    window_loop(query_step)
    spread_up(total, 0.5)

    def take(at, scale, masked):
        def take_step(first):
            rows = pl.ds(first, 64)
            if masked:
                place = lax.broadcasted_iota(jnp.int32, (64, 1), 0) + first
                valid = (place < length).astype(F32)
            for pair in range(4):
                values = total[pair, pl.ds(STARTS[0] + first, 64), :]
                if scale != 1.0:
                    values = values * scale
                if masked:
                    values = values * valid
                joined[rows, at + 128 * pair : at + 128 * pair + 128] = values.astype(BF16)

        row_loop(LEN, 64, take_step, 2)

    take(0, 0.125, False)
    for at, left, right, factor, scale, masked in (
        (D, score_grad, query, 0.5, 0.125, False),
        (2 * D, probs, numer, 1.0, 1.0, True),
    ):
        total[...] = jnp.zeros_like(total)

        def near_step(rows, near, flat, kind, left=left, right=right):
            for pair in range(4):
                lanes = pair_lanes(pair)
                total[pair, near, :] += tn(left[flat, lanes], by_head(right[rows, lanes], half))

        window_loop(near_step)
        spread_up(total, factor)
        take(at, scale, masked)

    def norm_step(first):
        rows = pl.ds(first, 64)
        values, _ = layer_norm(tokens[rows, :].astype(F32))
        normed[rows, :] = (values * gain + shift).astype(BF16)

    row_loop(LEN, 64, norm_step, 4)
    acc[...] += tn(joined[...], normed[...])
    result[...] = nn(joined[...], weights[...])

    def back_step(first):
        rows = pl.ds(first, 64)
        norm, inverse = layer_norm(tokens[rows, :].astype(F32))
        gradient = result[rows, :]
        sums[0:8, :] += jnp.sum((gradient * norm).reshape(8, 8, D), axis=0)
        sums[8:16, :] += jnp.sum(gradient.reshape(8, 8, D), axis=0)
        value = middle_grad[rows, :].astype(F32) + norm_back(gradient, norm, inverse, gain)
        grad_tokens[rows, :] = value.astype(BF16)

    row_loop(LEN, 64, back_step, 4)

    @pl.when(step_index == pl.num_programs(0) - 1)
    def _():
        small = jnp.sum(sums[...].reshape(2, 8, D), axis=1)
        small = jnp.concatenate([small, jnp.zeros((6, D), F32)], axis=0).astype(BF16)
        for side, block, device in block_places(place, plain, 1):
            target = (near_grads, far_grads)[side]
            for part in range(3):
                rows = pl.ds(pl.multiple_of(part * D + device * SHARE, SHARE), SHARE)
                target[block, part * SHARE : part * SHARE + SHARE, :] = acc[rows, :].astype(BF16)
            target[block, 3 * SHARE : 3 * SHARE + 8, :] = small


SMEM = pl.BlockSpec(memory_space=pltpu.SMEM)


def whole(*shape):
    return pl.BlockSpec(shape, lambda i: (0,) * len(shape), pipeline_mode=pl.Buffered(1))


def per_sequence(rows, columns):
    return pl.BlockSpec((rows, columns), lambda i: (i, 0))


def vmem(rows, columns, dtype):
    return pltpu.VMEM((rows, columns), dtype)


def shape_of(rows, columns, dtype):
    return jax.ShapeDtypeStruct((rows, columns), dtype)


PARAMS = pltpu.CompilerParams(
    dimension_semantics=("arbitrary",), vmem_limit_bytes=63 * 1024 * 1024
)


def cost(microseconds):
    return pl.CostEstimate(
        flops=int(microseconds * 1.0e9), bytes_accessed=int(microseconds * 1.0e6), transcendentals=0
    )


def attend(lengths, place, plain, tokens, blocks):
    count = lengths.shape[0]
    levels = shape_of(count * ROWS, D, BF16)
    one = per_sequence(LEN, D)
    all_levels = per_sequence(ROWS, D)
    flat = WINDOWS * 2 * QUERIES
    return pl.pallas_call(
        functools.partial(attend_kernel, plain),
        grid=(count,),
        in_specs=[
            SMEM,
            SMEM,
            one,
            whole(16, FIRST_ROWS, D),
            whole(16, FIRST_ROWS, D),
            whole(2, 2 * QUERIES, KEYS),
            whole(POOL_CHUNK, POOL_CHUNK),
            whole(2, 128),
        ],
        out_specs=[all_levels] * 3 + [per_sequence(flat, D), one, one],
        out_shape=[levels] * 3
        + [
            shape_of(count * flat, D, BF16),
            shape_of(count * LEN, D, BF16),
            shape_of(count * LEN, D, F32),
        ],
        scratch_shapes=[
            vmem(3 * D, D, BF16),
            vmem(8, D, F32),
            vmem(LEN, D, BF16),
            vmem(LEN, 3 * D, BF16),
            vmem(SIZES[-1], 3 * D, F32),
            vmem(ROWS, 128, BF16),
            pltpu.VMEM((4, ROWS, 128), F32),
            pltpu.VMEM((4, ROWS, 128), F32),
        ],
        compiler_params=PARAMS,
        cost_estimate=cost(40),
        name="attend",
    )(
        lengths,
        place,
        tokens,
        *blocks,
        jnp.asarray(score_bias()),
        jnp.asarray(pool_matrix(), BF16),
        jnp.asarray(halves(), BF16),
    )


def feed(place, plain, tokens, attn, total, cotangent, blocks):
    rows = tokens.shape[0]
    one = per_sequence(LEN, D)
    low = shape_of(rows, D, BF16)
    grads = whole(16, SECOND_ROWS, D)
    return pl.pallas_call(
        functools.partial(feed_kernel, plain),
        grid=(rows // LEN,),
        in_specs=[SMEM] + [one] * 4 + [whole(16, SECOND_ROWS, D)] * 2,
        out_specs=[one] * 4 + [grads, grads],
        out_shape=[low] * 4 + [jax.ShapeDtypeStruct((16, SECOND_ROWS, D), BF16)] * 2,
        scratch_shapes=[
            vmem(D, D, BF16),
            vmem(FF, D, BF16),
            vmem(D, FF, BF16),
            vmem(8, D, F32),
            vmem(LEN, D, F32),
            vmem(LEN, D, F32),
            vmem(LEN, 128, F32),
            vmem(LEN, D, BF16),
            vmem(LEN, D, F32),
            vmem(LEN, D, F32),
            vmem(LEN, D, BF16),
            vmem(LEN, D, BF16),
            vmem(56, D, F32),
            vmem(D, D, F32),
            vmem(FF, D, F32),
            vmem(D, FF, F32),
        ],
        compiler_params=PARAMS,
        cost_estimate=cost(75),
        name="feed",
    )(place, tokens, attn, total, cotangent, *blocks)


def attend_back(lengths, place, plain, tokens, middle_grad, numer_grad, total_grad, kept, blocks):
    count = lengths.shape[0]
    one = per_sequence(LEN, D)
    all_levels = per_sequence(ROWS, D)
    flat = WINDOWS * 2 * QUERIES
    grads = whole(16, FIRST_ROWS, D)
    return pl.pallas_call(
        functools.partial(attend_back_kernel, plain),
        grid=(count,),
        in_specs=[SMEM, SMEM]
        + [one] * 4
        + [all_levels] * 3
        + [per_sequence(flat, D)]
        + [whole(16, FIRST_ROWS, D)] * 2
        + [whole(POOL_CHUNK, POOL_CHUNK), whole(2, 128)],
        out_specs=[one, grads, grads],
        out_shape=[shape_of(count * LEN, D, BF16)]
        + [jax.ShapeDtypeStruct((16, FIRST_ROWS, D), BF16)] * 2,
        scratch_shapes=[
            vmem(3 * D, D, BF16),
            vmem(8, D, F32),
            vmem(ROWS, D, BF16),
            vmem(ROWS, D, BF16),
            vmem(flat, D, BF16),
            pltpu.VMEM((4, ROWS, 128), F32),
            vmem(LEN, 3 * D, BF16),
            vmem(LEN, D, BF16),
            vmem(ROWS, 128, BF16),
            vmem(SIZES[-1], D, F32),
            vmem(16, D, F32),
            vmem(3 * D, D, F32),
            vmem(LEN, D, F32),
        ],
        compiler_params=PARAMS,
        cost_estimate=cost(60),
        name="attend_back",
    )(
        lengths,
        place,
        tokens,
        middle_grad,
        numer_grad,
        total_grad,
        *kept,
        *blocks,
        jnp.asarray(pool_matrix(), BF16),
        jnp.asarray(halves(), BF16),
    )


def pack_first_kernel(place, w_query, w_key, w_value, small, packed):
    for part, ref in enumerate((w_query, w_key, w_value)):
        packed[part * SHARE : part * SHARE + SHARE, :] = ref[...].astype(F32).T.astype(BF16)
    device = place[0] * 8 + place[1]
    lane = lax.broadcasted_iota(jnp.int32, (SHARE, D), 1)
    mine = lane == lax.broadcasted_iota(jnp.int32, (SHARE, D), 0) + device * SHARE
    packed[3 * SHARE :, :] = nn(small[...], mine.astype(F32).astype(BF16)).astype(BF16)


def pack_second_kernel(place, w_out, w_up, w_down, small, bias_up, packed):
    packed[0:SHARE, :] = w_out[...].astype(F32).T.astype(BF16)
    packed[SHARE : 5 * SHARE, :] = w_up[...].astype(F32).T.astype(BF16)
    for part in range(4):
        at = (5 + part) * SHARE
        rows = slice(D * part, D * part + D)
        packed[at : at + SHARE, :] = w_down[rows, :].astype(F32).T.astype(BF16)
    device = place[0] * 8 + place[1]
    lane = lax.broadcasted_iota(jnp.int32, (SHARE, D), 1)
    mine = lane == lax.broadcasted_iota(jnp.int32, (SHARE, D), 0) + device * SHARE
    vectors = nn(small[...], mine.astype(F32).astype(BF16))
    lane = lax.broadcasted_iota(jnp.int32, (4 * SHARE, D), 1)
    mine = lane == lax.broadcasted_iota(jnp.int32, (4 * SHARE, D), 0) + (device % 8) * 4 * SHARE
    wide = nn(bias_up[...], mine.astype(F32).astype(BF16))
    row = lax.broadcasted_iota(jnp.int32, (8, D), 0)
    vectors = vectors + jnp.where(row == 3 + device // 8, wide, 0.0)
    packed[9 * SHARE :, :] = vectors.astype(BF16)


def pack(kernel, rows, name, place, *operands):
    return pl.pallas_call(
        kernel,
        in_specs=[SMEM] + [pl.BlockSpec(memory_space=pltpu.VMEM)] * len(operands),
        out_specs=pl.BlockSpec(memory_space=pltpu.VMEM),
        out_shape=shape_of(rows, D, BF16),
        cost_estimate=cost(2),
        name=name,
    )(place, *operands)


def across(values, bits):
    return lax.ppermute(values, "fsdp", [(i, i ^ bits) for i in range(8)])


def along(values, step):
    return lax.ppermute(values, "dp", [(i, (i + step) % 4) for i in range(4)])


def gather_rows(packed):
    return jnp.stack([packed] + [along(packed, step) for step in (1, 2, 3)])


def scatter_rows(blocks):
    parts = [blocks[0]] + [along(blocks[step], step) for step in (1, 2, 3)]
    return sum(part.astype(F32) for part in parts)


def spread(vector, index, devices):
    share = vector.shape[0]
    full = jnp.tile(vector, devices)
    mine = lax.broadcasted_iota(jnp.int32, full.shape, 0) // share == index
    return jnp.where(mine, full, jnp.zeros_like(full)).reshape(-1, D)


def stack_vectors(vectors):
    rows = jnp.stack(vectors)
    return jnp.concatenate([rows, jnp.zeros((8 - len(vectors), rows.shape[1]), rows.dtype)])


def exchange_permutes(place, tokens, lengths, weights, vectors, cotangent):
    w_query, w_key, w_value, w_out, w_up, w_down = weights
    bias_up, bias_down, gain_attn, shift_attn, gain_ffn, shift_ffn = vectors
    small = stack_vectors([gain_attn, shift_attn])
    first = pack(pack_first_kernel, FIRST_ROWS, "pack_first", place, w_query, w_key, w_value, small)
    small = stack_vectors([gain_ffn, shift_ffn, bias_down])
    second = pack(
        pack_second_kernel,
        SECOND_ROWS,
        "pack_second",
        place,
        w_out,
        w_up,
        w_down,
        small,
        bias_up.reshape(1, -1),
    )
    rows = gather_rows(first)
    in_x, in_y = across(rows, 2), across(rows, 4)
    diagonal = jnp.concatenate([across(in_x[:2], 4), across(in_y[2:], 2)])
    near = jnp.concatenate([rows, in_x, in_y, diagonal])
    first_blocks = (near, across(near, 1))
    second_rows = gather_rows(second)
    others = [across(second_rows, bits) for bits in (2, 4, 6)]
    *kept, attn, total = attend(lengths, place, False, tokens, first_blocks)
    near = jnp.concatenate([second_rows] + others)
    second_blocks = (near, across(near, 1))
    output, middle_grad, numer_grad, total_grad, near, far = feed(
        place, False, tokens, attn, total, cotangent, second_blocks
    )
    mine = (near.astype(F32) + across(far, 1).astype(F32)).astype(BF16).reshape(4, 4, SECOND_ROWS, D)
    others = [across(mine[block], bits) for block, bits in ((1, 2), (2, 4), (3, 6))]
    grad_tokens, near, far = attend_back(
        lengths, place, False, tokens, middle_grad, numer_grad, total_grad, kept, first_blocks
    )
    mine = sum(part.astype(F32) for part in [mine[0]] + others).astype(BF16)
    second_share = scatter_rows(mine)
    mine = (near.astype(F32) + across(far, 1).astype(F32)).astype(BF16).reshape(4, 4, FIRST_ROWS, D)
    mine = (mine[:2].astype(F32) + across(mine[2:], 4).astype(F32)).astype(BF16)
    mine = (mine[0].astype(F32) + across(mine[1], 2).astype(F32)).astype(BF16)
    first_share = scatter_rows(mine)
    return output, grad_tokens, first_share, second_share


def exchange_plain(index, devices, tokens, lengths, weights, vectors, cotangent):
    w_query, w_key, w_value, w_out, w_up, w_down = weights
    bias_up, bias_down, gain_attn, shift_attn, gain_ffn, shift_ffn = vectors
    share = D // devices

    def gathered(rows):
        return lax.all_gather(rows, AXES, axis=0, tiled=True).reshape(32, SHARE, D)

    def vector_rows(parts):
        rows = jnp.concatenate([spread(part, index, devices) for part in parts])
        rows = lax.psum(rows, AXES)
        pad = jnp.zeros((8 - rows.shape[0], D), rows.dtype)
        rows = jnp.concatenate([rows, pad])[None]
        return jnp.concatenate([rows, jnp.zeros((31, 8, D), rows.dtype)])

    def halved(parts):
        blocks = jnp.concatenate(parts, axis=1)
        return blocks[:16], blocks[16:]

    place = jnp.zeros((2,), jnp.int32)
    first_blocks = halved(
        [gathered(w.T) for w in (w_query, w_key, w_value)]
        + [vector_rows([gain_attn, shift_attn])]
    )
    up = lax.all_gather(w_up.T, AXES, axis=0, tiled=True).reshape(32, 4 * SHARE, D)
    down = lax.all_gather(w_down.T, AXES, axis=0, tiled=True).reshape(32, SHARE, 4, D)
    down = jnp.transpose(down, (0, 2, 1, 3)).reshape(32, 4 * SHARE, D)
    second_blocks = halved(
        [gathered(w_out.T), up, down, vector_rows([gain_ffn, shift_ffn, bias_down, bias_up])]
    )
    *kept, attn, total = attend(lengths, place, True, tokens, first_blocks)
    output, middle_grad, numer_grad, total_grad, near, far = feed(
        place, True, tokens, attn, total, cotangent, second_blocks
    )
    second = jnp.concatenate([near, far])
    grad_tokens, near, far = attend_back(
        lengths, place, True, tokens, middle_grad, numer_grad, total_grad, kept, first_blocks
    )
    first = jnp.concatenate([near, far])

    def scattered(rows):
        rows = rows.reshape(devices, -1, D)
        return lax.psum_scatter(rows, AXES, scatter_dimension=0, tiled=False).astype(F32)

    down = second[:, 5 * SHARE : 9 * SHARE].reshape(32, 4, SHARE, D)
    down = scattered(jnp.transpose(down, (0, 2, 1, 3)).reshape(32, 4 * SHARE, D))
    down = jnp.transpose(down.reshape(share, 4, D), (1, 0, 2)).reshape(4 * share, D)
    first_vectors = lax.psum(first[0, 3 * SHARE :].astype(F32), AXES)
    second_vectors = lax.psum(second[0, 9 * SHARE :].astype(F32), AXES)
    first_share = [scattered(first[:, p * SHARE : p * SHARE + SHARE]) for p in range(3)]
    second_share = [scattered(second[:, :SHARE]), scattered(second[:, SHARE : 5 * SHARE]), down]
    return (
        output,
        grad_tokens,
        jnp.concatenate(first_share + [first_vectors]),
        jnp.concatenate(second_share + [second_vectors]),
    )


def on_device(sizes, tokens, lengths, *rest):
    weights, vectors, cotangent = rest[:6], rest[6:12], rest[12]
    devices = sizes[0] * sizes[1]
    share = D // devices
    index = lax.axis_index(AXES)
    if sizes == (4, 8):
        place = jnp.stack([lax.axis_index("dp"), lax.axis_index("fsdp")]).astype(jnp.int32)
        output, grad_tokens, first, second = exchange_permutes(
            place, tokens, lengths, weights, vectors, cotangent
        )
    else:
        output, grad_tokens, first, second = exchange_plain(
            index, devices, tokens, lengths, weights, vectors, cotangent
        )

    def own(row):
        return lax.dynamic_slice(row, (index * share,), (share,))

    first_vectors = first[3 * share :]
    second_vectors = second[9 * share :]
    down = jnp.transpose(second[5 * share : 9 * share].reshape(4, share, D), (0, 2, 1))
    return (
        output,
        grad_tokens,
        first[:share].T,
        first[share : 2 * share].T,
        first[2 * share : 3 * share].T,
        second[:share].T,
        second[share : 5 * share].T,
        down.reshape(FF, share),
        lax.dynamic_slice(second_vectors[3:7].reshape(FF), (index * 4 * share,), (4 * share,)),
        own(second_vectors[2]),
        own(first_vectors[0]),
        own(first_vectors[1]),
        own(second_vectors[0]),
        own(second_vectors[1]),
    )


def solution(mesh):
    rows = P(AXES, None)
    columns = P(None, AXES)
    vector = P(AXES)
    sizes = (mesh.shape["dp"], mesh.shape["fsdp"])
    return jax.shard_map(
        functools.partial(on_device, sizes),
        mesh=mesh,
        in_specs=(rows, vector) + (columns,) * 6 + (vector,) * 6 + (rows,),
        out_specs=(rows, rows) + (columns,) * 6 + (vector,) * 6,
        check_vma=False,
    )
```

```python
import functools

import jax
import jax.numpy as jnp
import numpy as np
from jax import lax
from jax.experimental import pallas as pl
from jax.experimental.pallas import tpu as pltpu
from jax.sharding import PartitionSpec as P

D = 512
H = 8
DH = 64
FF = 2048
BLOCK = 16
LEVELS = 6
LEN = 1024
AXES = ("dp", "fsdp")
BF16 = jnp.bfloat16
F32 = jnp.float32

STARTS = (32, 1072, 1600, 1872, 2016, 2096)
SIZES = tuple(LEN >> level for level in range(LEVELS))
ROWS = 2192
GAPS = ((0, 32), (1056, 16), (1584, 16), (1856, 16), (2000, 16), (2080, 16), (2128, 64))
WINDOWS = 32
QUERIES = 64
KEYS = 128
POOL_CHUNK = 256
SHARE = 16
FIRST_ROWS = 3 * SHARE + 8
SECOND_ROWS = 9 * SHARE + 8
SCORE = 0.125 * 1.4426950408889634


def nn(left, right):
    return lax.dot_general(left, right, (((1,), (0,)), ((), ())), preferred_element_type=F32)


def nt(left, right):
    return lax.dot_general(left, right, (((1,), (1,)), ((), ())), preferred_element_type=F32)


def tn(left, right):
    return lax.dot_general(left, right, (((0,), (0,)), ((), ())), preferred_element_type=F32)


def score_bias():
    query = (np.arange(2 * QUERIES) % QUERIES)[:, None]
    key = np.arange(KEYS)[None, :] - 32
    near = np.abs(query // 16 - key // 16) <= 1
    apart = np.abs(query // 8 - key // 8) > 1
    return np.where(np.stack([near, near & apart]), 0.0, -1e30).astype(np.float32)


def pool_matrix():
    matrix = np.zeros((POOL_CHUNK, POOL_CHUNK), np.float32)
    first = 0
    for level in range(1, LEVELS):
        count = POOL_CHUNK >> level
        for row in range(count):
            matrix[first + row, row << level : (row + 1) << level] = 0.5**level
        first += count
    return matrix


def halves():
    lane = np.arange(128)
    return np.stack([lane < DH, lane >= DH]).astype(np.float32)


def window_loop(step):
    for window in range(WINDOWS):
        gaps = sum(window >= first for first in (16, 24, 28, 30, 31))
        row = STARTS[0] + QUERIES * window + 16 * gaps
        step(
            pl.ds(row, QUERIES),
            pl.ds(row - 32, KEYS),
            pl.ds(window * 2 * QUERIES, 2 * QUERIES),
            int(window >= 16),
        )


def row_loop(total, size, step):
    for first in range(0, total, size):
        step(first)


def pair_lanes(pair):
    return slice(128 * pair, 128 * pair + 128)


def by_head(values, half):
    return jnp.concatenate([values * half[0:1, :], values * half[1:2, :]], axis=0)


def joined_heads(values, low_head):
    return jnp.where(low_head, values[:QUERIES], values[QUERIES:])


def fill_counts(counts, length):
    clear_gaps(counts)
    for level in range(LEVELS):
        place = lax.broadcasted_iota(jnp.int32, (SIZES[level], 128), 0)
        span = 1 << level
        number = jnp.clip(length - place * span, 0, span).astype(F32)
        counts[STARTS[level] : STARTS[level] + SIZES[level], :] = number.astype(BF16)


def block_places(place, plain, sign):
    for half in range(2):
        for block in range(16):
            if plain:
                yield half, block, half * 16 + block
            else:
                column = place[1] ^ (half + 2 * (block // 4))
                row = (place[0] + 4 + sign * (block % 4)) % 4
                yield half, block, row * 8 + column


def sixteen(device):
    return pl.ds(pl.multiple_of(device * SHARE, SHARE), SHARE)


def sixty_four(device):
    return pl.ds(pl.multiple_of(device * 4 * SHARE, 4 * SHARE), 4 * SHARE)


def load_first(place, plain, blocks, weights, vectors):
    total = jnp.zeros((8, D), F32)
    for half, block, device in block_places(place, plain, -1):
        source = blocks[half]
        for part in range(3):
            rows = pl.ds(pl.multiple_of(part * D + device * SHARE, SHARE), SHARE)
            weights[rows, :] = source[block, part * SHARE : part * SHARE + SHARE, :]
        total = total + source[block, 3 * SHARE : 3 * SHARE + 8, :].astype(F32)
    vectors[...] = total


def load_second(blocks, w_out, w_up, w_down, vectors):
    total = jnp.zeros((8, D), F32)
    for device in range(32):
        rows = slice(device * SHARE, device * SHARE + SHARE)
        w_out[rows, :] = blocks[device, 0:SHARE, :]
        w_up[4 * rows.start : 4 * rows.stop, :] = blocks[device, SHARE : 5 * SHARE, :]
        for part in range(4):
            at = (5 + part) * SHARE
            w_down[rows, D * part : D * part + D] = blocks[device, at : at + SHARE, :]
        total = total + blocks[device, 9 * SHARE : 9 * SHARE + 8, :].astype(F32)
    vectors[...] = total


def layer_norm(values):
    mean = jnp.mean(values, axis=-1, keepdims=True)
    centred = values - mean
    inverse = lax.rsqrt(jnp.mean(centred * centred, axis=-1, keepdims=True) + 1e-05)
    return centred * inverse, inverse


def norm_back(gradient, normed, inverse, gain):
    scaled = gradient * gain
    return inverse * (
        scaled
        - jnp.mean(scaled, axis=-1, keepdims=True)
        - normed * jnp.mean(scaled * normed, axis=-1, keepdims=True)
    )


def clear_gaps(ref):
    for first, count in GAPS:
        ref[first : first + count, :] = jnp.zeros((count, ref.shape[1]), ref.dtype)


def spread_up(ref, factor):
    for level in range(LEVELS - 2, -1, -1):
        count = SIZES[level + 1]
        size = min(count, 64)

        def step(first, level=level, size=size):
            for pair in range(4):
                above = ref[pair, pl.ds(STARTS[level + 1] + first, size), :]
                if factor != 1.0:
                    above = above * factor
                for odd in (0, 1):
                    below = pl.ds(STARTS[level] + 2 * first + odd, size, stride=2)
                    ref[pair, below, :] = ref[pair, below, :] + above

        row_loop(count, size, step)


def attend_kernel(
    plain,
    lengths,
    place,
    tokens,
    near_blocks,
    far_blocks,
    bias,
    pool,
    half,
    query,
    key,
    value,
    probs,
    attn,
    total,
    weights,
    vectors,
    normed,
    joined,
    top,
    counts,
    numer,
    denom,
):
    @pl.when(pl.program_id(0) == 0)
    def _():
        load_first(place, plain, (near_blocks, far_blocks), weights, vectors)

    length = lengths[pl.program_id(0)]
    gain = vectors[0:1, :]
    shift = vectors[1:2, :]

    def norm_step(first):
        rows = pl.ds(first, 64)
        values, _ = layer_norm(tokens[rows, :].astype(F32))
        normed[rows, :] = (values * gain + shift).astype(BF16)

    row_loop(LEN, 64, norm_step)
    for ref in (query, key, value):
        clear_gaps(ref)
    fill_counts(counts, length)
    targets = ((query, 0), (key, D), (value, 2 * D))
    for first in range(0, LEN, POOL_CHUNK):
        rows = slice(first, first + POOL_CHUNK)
        chunk = first // POOL_CHUNK
        values = nt(normed[rows, :], weights[...])
        valid = (lax.broadcasted_iota(jnp.int32, (POOL_CHUNK, 1), 0) + first < length).astype(F32)
        joined[rows, : 2 * D] = values[:, : 2 * D].astype(BF16)
        joined[rows, 2 * D :] = (values[:, 2 * D :] * valid).astype(BF16)
        pooled = nn(pool[...], joined[rows, :])
        for ref, lane in targets:
            start = STARTS[0] + first
            ref[start : start + POOL_CHUNK, :] = joined[rows, lane : lane + D]
            at = 0
            for level in range(1, LEVELS):
                count = POOL_CHUNK >> level
                part = pooled[at : at + count, lane : lane + D]
                at += count
                if ref is value:
                    part = part * float(1 << level)
                if level < LEVELS - 1:
                    start = STARTS[level] + chunk * count
                    ref[start : start + count, :] = part.astype(BF16)
                else:
                    top[chunk * count : chunk * count + count, lane : lane + D] = part
    for ref, lane in targets:
        ref[STARTS[-1] : STARTS[-1] + SIZES[-1], :] = top[:, lane : lane + D].astype(BF16)

    def score_step(rows, near, flat, kind):
        allowed = bias[kind]
        for pair in range(4):
            lanes = pair_lanes(pair)
            scores = nt(by_head(query[rows, lanes], half), key[near, lanes])
            probs[flat, lanes] = jnp.exp2(scores * SCORE + allowed).astype(BF16)

    window_loop(score_step)
    low_head = lax.broadcasted_iota(jnp.int32, (QUERIES, 128), 1) < DH

    def value_step(rows, near, flat, kind):
        number = counts[near, :]
        for pair in range(4):
            lanes = pair_lanes(pair)
            both = nn(probs[flat, lanes], jnp.concatenate([value[near, lanes], number], axis=1))
            numer[pair, rows, :] = joined_heads(both[:, :128], low_head)
            denom[pair, rows, :] = joined_heads(both[:, 128:], low_head)

    window_loop(value_step)
    spread_up(numer, 1.0)
    spread_up(denom, 1.0)

    def join_step(first):
        rows = pl.ds(first, 64)
        inner = pl.ds(STARTS[0] + first, 64)
        for pair in range(4):
            lanes = pair_lanes(pair)
            below = denom[pair, inner, :]
            attn[rows, lanes] = (numer[pair, inner, :] / below).astype(BF16)
            total[rows, lanes] = below

    row_loop(LEN, 64, join_step)


def feed_kernel(
    plain,
    place,
    tokens,
    attn,
    total,
    cotangent,
    blocks,
    output,
    middle_grad,
    numer_grad,
    total_grad,
    near_grads,
    far_grads,
    w_out,
    w_up,
    w_down,
    vectors,
    middle,
    normed,
    inverse,
    normed_low,
    hidden,
    result,
    gathered,
    active,
    back,
    sums,
    acc_out,
    acc_up,
    acc_down,
):
    @pl.when(pl.program_id(0) == 0)
    def _():
        acc_out[...] = jnp.zeros_like(acc_out)
        acc_up[...] = jnp.zeros_like(acc_up)
        acc_down[...] = jnp.zeros_like(acc_down)
        sums[...] = jnp.zeros_like(sums)
        load_second(blocks, w_out, w_up, w_down, vectors)

    gain = vectors[0:1, :]
    shift = vectors[1:2, :]
    bias_down = vectors[2:3, :]
    middle[...] = nt(attn[...], w_out[...])

    def norm_step(first):
        rows = pl.ds(first, 64)
        values = middle[rows, :] + tokens[rows, :].astype(F32)
        middle[rows, :] = values
        norm, factor = layer_norm(values)
        normed[rows, :] = norm
        inverse[rows, :] = jnp.broadcast_to(factor, (64, 128))
        normed_low[rows, :] = (norm * gain + shift).astype(BF16)

    row_loop(LEN, 64, norm_step)
    def lanes_of(part):
        return slice(D * part, D * part + D)

    def enter(part):
        slot = part % 2
        hidden[slot] = nt(normed_low[...], w_up[lanes_of(part), :])
        result[slot] = nn(cotangent[...], w_down[:, lanes_of(part)])

    def act(part):
        slot = part % 2
        bias_up = vectors[3 + part : 4 + part, :]
        at = 8 * (3 + part)
        count = jnp.zeros((8, D), F32)
        for first in range(0, LEN, 64):
            rows = slice(first, first + 64)
            value = hidden[slot, rows, :] + bias_up
            gate = 0.5 * jnp.tanh(0.5 * value) + 0.5
            active[slot, rows, :] = (value * gate).astype(BF16)
            slope = gate * (1.0 + value * (1.0 - gate))
            gradient = (result[slot, rows, :] * slope).astype(BF16)
            back[slot, rows, :] = gradient
            count = count + jnp.sum(gradient.astype(F32).reshape(8, 8, D), axis=0)
        sums[at : at + 8, :] += count

    def leave(part):
        slot = part % 2
        lanes = lanes_of(part)
        acc_down[:, lanes] += tn(cotangent[...], active[slot])
        acc_up[lanes, :] += tn(back[slot], normed_low[...])
        middle[...] += nt(active[slot], w_down[:, lanes])
        gathered[...] += nn(back[slot], w_up[lanes, :])

    gathered[...] = jnp.zeros_like(gathered)
    enter(0)
    for part in range(FF // D):
        act(part)
        if part + 1 < FF // D:
            enter(part + 1)
        leave(part)

    def back_step(first):
        rows = pl.ds(first, 64)
        output[rows, :] = (middle[rows, :] + bias_down).astype(BF16)
        gradient = gathered[rows, :]
        norm = normed[rows, :]
        value = cotangent[rows, :].astype(F32)
        sums[0:8, :] += jnp.sum((gradient * norm).reshape(8, 8, D), axis=0)
        sums[8:16, :] += jnp.sum(gradient.reshape(8, 8, D), axis=0)
        sums[16:24, :] += jnp.sum(value.reshape(8, 8, D), axis=0)
        value = value + norm_back(gradient, norm, inverse[rows, 0:1], gain)
        middle_grad[rows, :] = value.astype(BF16)

    row_loop(LEN, 64, back_step)
    acc_out[...] += tn(middle_grad[...], attn[...])
    gathered[...] = nn(middle_grad[...], w_out[...])

    def numer_step(first):
        rows = pl.ds(first, 64)
        gradient = gathered[rows, :].astype(BF16).astype(F32) / total[rows, :]
        numer_grad[rows, :] = gradient.astype(BF16)
        total_grad[rows, :] = (-gradient * attn[rows, :].astype(F32)).astype(BF16)

    row_loop(LEN, 64, numer_step)

    @pl.when(pl.program_id(0) == pl.num_programs(0) - 1)
    def _():
        small = jnp.sum(sums[...].reshape(7, 8, D), axis=1)
        small = jnp.concatenate([small, jnp.zeros((1, D), F32)], axis=0).astype(BF16)
        for half, block, device in block_places(place, plain, 1):
            target = (near_grads, far_grads)[half]
            target[block, 0:SHARE, :] = acc_out[sixteen(device), :].astype(BF16)
            target[block, SHARE : 5 * SHARE, :] = acc_up[sixty_four(device), :].astype(BF16)
            for part in range(4):
                at = (5 + part) * SHARE
                grads = acc_down[sixteen(device), D * part : D * part + D]
                target[block, at : at + SHARE, :] = grads.astype(BF16)
            target[block, 9 * SHARE : 9 * SHARE + 8, :] = small


def attend_back_kernel(
    plain,
    lengths,
    place,
    tokens,
    middle_grad,
    numer_grad,
    total_grad,
    query,
    key,
    value,
    probs,
    weights,
    vectors,
    pool,
    half,
    grad_tokens,
    near_grads,
    far_grads,
    numer,
    denom,
    score_grad,
    total,
    joined,
    normed,
    counts,
    top,
    sums,
    acc,
):
    step_index = pl.program_id(0)
    length = lengths[step_index]

    @pl.when(step_index == 0)
    def _():
        acc[...] = jnp.zeros_like(acc)
        sums[...] = jnp.zeros_like(sums)

    gain = vectors[0:1, :]
    shift = vectors[1:2, :]
    clear_gaps(numer)
    clear_gaps(denom)
    fill_counts(counts, length)
    for source, target in ((numer_grad, numer), (total_grad, denom)):
        target[STARTS[0] : STARTS[0] + LEN, :] = source[...]
        for first in range(0, LEN, POOL_CHUNK):
            chunk = first // POOL_CHUNK
            pooled = nn(pool[...], source[first : first + POOL_CHUNK, :])
            at = 0
            for level in range(1, LEVELS):
                count = POOL_CHUNK >> level
                part = pooled[at : at + count] * float(1 << level)
                at += count
                if level < LEVELS - 1:
                    start = STARTS[level] + chunk * count
                    target[start : start + count, :] = part.astype(BF16)
                else:
                    top[chunk * count : chunk * count + count, :] = part
        target[STARTS[-1] : STARTS[-1] + SIZES[-1], :] = top[...].astype(BF16)

    def score_step(rows, near, flat, kind):
        number = counts[near, :]
        for pair in range(4):
            lanes = pair_lanes(pair)
            left = jnp.concatenate(
                [by_head(numer[rows, lanes], half), by_head(denom[rows, lanes], half)], axis=1
            )
            right = jnp.concatenate([value[near, lanes], number], axis=1)
            score_grad[flat, lanes] = (nt(left, right) * probs[flat, lanes].astype(F32)).astype(BF16)

    window_loop(score_step)
    low_head = lax.broadcasted_iota(jnp.int32, (QUERIES, 128), 1) < DH

    def query_step(rows, near, flat, kind):
        for pair in range(4):
            lanes = pair_lanes(pair)
            both = nn(score_grad[flat, lanes], key[near, lanes])
            total[pair, rows, :] = joined_heads(both, low_head)

    window_loop(query_step)
    spread_up(total, 0.5)

    def take(at, scale, masked):
        def take_step(first):
            rows = pl.ds(first, 64)
            if masked:
                place = lax.broadcasted_iota(jnp.int32, (64, 1), 0) + first
                valid = (place < length).astype(F32)
            for pair in range(4):
                values = total[pair, pl.ds(STARTS[0] + first, 64), :]
                if scale != 1.0:
                    values = values * scale
                if masked:
                    values = values * valid
                joined[rows, at + 128 * pair : at + 128 * pair + 128] = values.astype(BF16)

        row_loop(LEN, 64, take_step)

    take(0, 0.125, False)
    for at, left, right, factor, scale, masked in (
        (D, score_grad, query, 0.5, 0.125, False),
        (2 * D, probs, numer, 1.0, 1.0, True),
    ):
        total[...] = jnp.zeros_like(total)

        def near_step(rows, near, flat, kind, left=left, right=right):
            for pair in range(4):
                lanes = pair_lanes(pair)
                total[pair, near, :] += tn(left[flat, lanes], by_head(right[rows, lanes], half))

        window_loop(near_step)
        spread_up(total, factor)
        take(at, scale, masked)

    def norm_step(first):
        rows = pl.ds(first, 64)
        values, _ = layer_norm(tokens[rows, :].astype(F32))
        normed[rows, :] = (values * gain + shift).astype(BF16)

    row_loop(LEN, 64, norm_step)
    for part in range(3):
        lanes = slice(D * part, D * part + D)
        acc[lanes, :] += tn(joined[:, lanes], normed[...])
    for first in range(0, LEN, POOL_CHUNK):
        rows = slice(first, first + POOL_CHUNK)
        passed = nn(joined[rows, :], weights[...])
        for pair in range(4):
            total[pair, rows, :] = passed[:, pair_lanes(pair)]

    def back_step(first):
        rows = pl.ds(first, 64)
        norm, inverse = layer_norm(tokens[rows, :].astype(F32))
        gradient = jnp.concatenate([total[pair, rows, :] for pair in range(4)], axis=1)
        sums[0:8, :] += jnp.sum((gradient * norm).reshape(8, 8, D), axis=0)
        sums[8:16, :] += jnp.sum(gradient.reshape(8, 8, D), axis=0)
        value = middle_grad[rows, :].astype(F32) + norm_back(gradient, norm, inverse, gain)
        grad_tokens[rows, :] = value.astype(BF16)

    row_loop(LEN, 64, back_step)

    @pl.when(step_index == pl.num_programs(0) - 1)
    def _():
        small = jnp.sum(sums[...].reshape(2, 8, D), axis=1)
        small = jnp.concatenate([small, jnp.zeros((6, D), F32)], axis=0).astype(BF16)
        for side, block, device in block_places(place, plain, 1):
            target = (near_grads, far_grads)[side]
            for part in range(3):
                rows = pl.ds(pl.multiple_of(part * D + device * SHARE, SHARE), SHARE)
                target[block, part * SHARE : part * SHARE + SHARE, :] = acc[rows, :].astype(BF16)
            target[block, 3 * SHARE : 3 * SHARE + 8, :] = small


SMEM = pl.BlockSpec(memory_space=pltpu.SMEM)


def whole(*shape):
    return pl.BlockSpec(shape, lambda i: (0,) * len(shape), pipeline_mode=pl.Buffered(1))


def per_sequence(rows, columns):
    return pl.BlockSpec((rows, columns), lambda i: (i, 0))


def vmem(rows, columns, dtype):
    return pltpu.VMEM((rows, columns), dtype)


def shape_of(rows, columns, dtype):
    return jax.ShapeDtypeStruct((rows, columns), dtype)


PARAMS = pltpu.CompilerParams(
    dimension_semantics=("arbitrary",), vmem_limit_bytes=63 * 1024 * 1024
)


def cost(microseconds):
    return pl.CostEstimate(
        flops=int(microseconds * 1.0e9), bytes_accessed=int(microseconds * 1.0e6), transcendentals=0
    )


def attend(lengths, place, plain, tokens, blocks):
    count = lengths.shape[0]
    levels = shape_of(count * ROWS, D, BF16)
    one = per_sequence(LEN, D)
    all_levels = per_sequence(ROWS, D)
    flat = WINDOWS * 2 * QUERIES
    return pl.pallas_call(
        functools.partial(attend_kernel, plain),
        grid=(count,),
        in_specs=[
            SMEM,
            SMEM,
            one,
            whole(16, FIRST_ROWS, D),
            whole(16, FIRST_ROWS, D),
            whole(2, 2 * QUERIES, KEYS),
            whole(POOL_CHUNK, POOL_CHUNK),
            whole(2, 128),
        ],
        out_specs=[all_levels] * 3
        + [per_sequence(flat, D), one, one, whole(3 * D, D), whole(8, D)],
        out_shape=[levels] * 3
        + [
            shape_of(count * flat, D, BF16),
            shape_of(count * LEN, D, BF16),
            shape_of(count * LEN, D, F32),
            shape_of(3 * D, D, BF16),
            shape_of(8, D, F32),
        ],
        scratch_shapes=[
            vmem(LEN, D, BF16),
            vmem(LEN, 3 * D, BF16),
            vmem(SIZES[-1], 3 * D, F32),
            vmem(ROWS, 128, BF16),
            pltpu.VMEM((4, ROWS, 128), F32),
            pltpu.VMEM((4, ROWS, 128), F32),
        ],
        compiler_params=PARAMS,
        cost_estimate=cost(40),
        name="attend",
    )(
        lengths,
        place,
        tokens,
        *blocks,
        jnp.asarray(score_bias()),
        jnp.asarray(pool_matrix(), BF16),
        jnp.asarray(halves(), BF16),
    )


def feed(place, plain, tokens, attn, total, cotangent, blocks):
    rows = tokens.shape[0]
    one = per_sequence(LEN, D)
    low = shape_of(rows, D, BF16)
    grads = whole(16, SECOND_ROWS, D)
    return pl.pallas_call(
        functools.partial(feed_kernel, plain),
        grid=(rows // LEN,),
        in_specs=[SMEM] + [one] * 4 + [whole(32, SECOND_ROWS, D)],
        out_specs=[one] * 4 + [grads, grads],
        out_shape=[low] * 4 + [jax.ShapeDtypeStruct((16, SECOND_ROWS, D), BF16)] * 2,
        scratch_shapes=[
            vmem(D, D, BF16),
            vmem(FF, D, BF16),
            vmem(D, FF, BF16),
            vmem(8, D, F32),
            vmem(LEN, D, F32),
            vmem(LEN, D, F32),
            vmem(LEN, 128, F32),
            vmem(LEN, D, BF16),
            pltpu.VMEM((2, LEN, D), F32),
            pltpu.VMEM((2, LEN, D), F32),
            vmem(LEN, D, F32),
            pltpu.VMEM((2, LEN, D), BF16),
            pltpu.VMEM((2, LEN, D), BF16),
            vmem(56, D, F32),
            vmem(D, D, F32),
            vmem(FF, D, F32),
            vmem(D, FF, F32),
        ],
        compiler_params=PARAMS,
        cost_estimate=cost(75),
        name="feed",
    )(place, tokens, attn, total, cotangent, blocks)


def attend_back(lengths, place, plain, tokens, middle_grad, numer_grad, total_grad, kept):
    count = lengths.shape[0]
    one = per_sequence(LEN, D)
    all_levels = per_sequence(ROWS, D)
    flat = WINDOWS * 2 * QUERIES
    grads = whole(16, FIRST_ROWS, D)
    return pl.pallas_call(
        functools.partial(attend_back_kernel, plain),
        grid=(count,),
        in_specs=[SMEM, SMEM]
        + [one] * 4
        + [all_levels] * 3
        + [per_sequence(flat, D)]
        + [whole(3 * D, D), whole(8, D), whole(POOL_CHUNK, POOL_CHUNK), whole(2, 128)],
        out_specs=[one, grads, grads],
        out_shape=[shape_of(count * LEN, D, BF16)]
        + [jax.ShapeDtypeStruct((16, FIRST_ROWS, D), BF16)] * 2,
        scratch_shapes=[
            vmem(ROWS, D, BF16),
            vmem(ROWS, D, BF16),
            vmem(flat, D, BF16),
            pltpu.VMEM((4, ROWS, 128), F32),
            vmem(LEN, 3 * D, BF16),
            vmem(LEN, D, BF16),
            vmem(ROWS, 128, BF16),
            vmem(SIZES[-1], D, F32),
            vmem(16, D, F32),
            vmem(3 * D, D, F32),
        ],
        compiler_params=PARAMS,
        cost_estimate=cost(60),
        name="attend_back",
    )(
        lengths,
        place,
        tokens,
        middle_grad,
        numer_grad,
        total_grad,
        *kept,
        jnp.asarray(pool_matrix(), BF16),
        jnp.asarray(halves(), BF16),
    )


def pack_kernel(place, *refs):
    w_query, w_key, w_value, w_out, w_up, w_down, bias_up, bias_down, *norms, first, second = refs
    for part, ref in enumerate((w_query, w_key, w_value)):
        first[part * SHARE : part * SHARE + SHARE, :] = ref[...]
    second[0:SHARE, :] = w_out[...]
    second[SHARE : 5 * SHARE, :] = w_up[...]
    for part in range(4):
        at = (5 + part) * SHARE
        second[at : at + SHARE, :] = w_down[:, D * part : D * part + D]
    device = place[0] * 8 + place[1]
    lane = lax.broadcasted_iota(jnp.int32, (SHARE, D), 1)
    mine = lane == lax.broadcasted_iota(jnp.int32, (SHARE, D), 0) + device * SHARE
    mine = mine.astype(F32).astype(BF16)
    gain_attn, shift_attn, gain_ffn, shift_ffn = norms
    row = lax.broadcasted_iota(jnp.int32, (8, D), 0)

    def rows_of(vectors):
        total = jnp.zeros((8, D), F32)
        for place_of, vector in enumerate(vectors):
            total = jnp.where(row == place_of, nn(vector[...], mine), total)
        return total

    first[3 * SHARE :, :] = rows_of((gain_attn, shift_attn)).astype(BF16)
    lane = lax.broadcasted_iota(jnp.int32, (4 * SHARE, D), 1)
    mine_up = lane == lax.broadcasted_iota(jnp.int32, (4 * SHARE, D), 0) + (device % 8) * 4 * SHARE
    wide = nn(bias_up[...], mine_up.astype(F32).astype(BF16))
    vectors = rows_of((gain_ffn, shift_ffn, bias_down))
    second[9 * SHARE :, :] = jnp.where(row == 3 + device // 8, wide, vectors).astype(BF16)


def pack(place, weights, vectors):
    operands = [w.T for w in weights] + [v.reshape(1, -1) for v in vectors]
    return pl.pallas_call(
        pack_kernel,
        in_specs=[SMEM] + [pl.BlockSpec(memory_space=pltpu.VMEM)] * len(operands),
        out_specs=[pl.BlockSpec(memory_space=pltpu.VMEM)] * 2,
        out_shape=[shape_of(FIRST_ROWS, D, BF16), shape_of(SECOND_ROWS, D, BF16)],
        cost_estimate=cost(2),
        name="pack",
    )(place, *operands)


def across(values, bits):
    return lax.ppermute(values, "fsdp", [(i, i ^ bits) for i in range(8)])


def along(values, step):
    return lax.ppermute(values, "dp", [(i, (i + step) % 4) for i in range(4)])


def gather_rows(packed):
    return jnp.stack([packed] + [along(packed, step) for step in (1, 2, 3)])


def shares_along(blocks):
    return [blocks[0]] + [along(blocks[step], step) for step in (1, 2, 3)]


def added(parts):
    return sum(part.astype(F32) for part in parts)


def spread(vector, index, devices):
    share = vector.shape[0]
    full = jnp.tile(vector, devices)
    mine = lax.broadcasted_iota(jnp.int32, full.shape, 0) // share == index
    return jnp.where(mine, full, jnp.zeros_like(full)).reshape(-1, D)


def exchange_permutes(place, tokens, lengths, weights, vectors, cotangent):
    first, second = pack(place, weights, vectors)
    rows = gather_rows(first)
    in_x, in_y = across(rows, 2), across(rows, 4)
    diagonal = jnp.concatenate([across(in_x[:2], 4), across(in_y[2:], 2)])
    near = jnp.concatenate([rows, in_x, in_y, diagonal])
    first_blocks = (near, across(near, 1))
    second_blocks = lax.all_gather(second, AXES, axis=0, tiled=False)
    *kept, attn, total, weights, gains = attend(lengths, place, False, tokens, first_blocks)
    kept += [weights, gains]
    output, middle_grad, numer_grad, total_grad, near, far = feed(
        place, False, tokens, attn, total, cotangent, second_blocks
    )
    mine = added([near, across(far, 1)]).astype(BF16).reshape(4, 4, SECOND_ROWS, D)
    others = [across(mine[block], bits) for block, bits in ((1, 2), (2, 4), (3, 6))]
    grad_tokens, near, far = attend_back(
        lengths, place, False, tokens, middle_grad, numer_grad, total_grad, kept
    )
    near, far, others = lax.optimization_barrier((near, far, others))
    second_parts = shares_along(added([mine[0]] + others).astype(BF16))
    mine = added([near, across(far, 1)]).astype(BF16).reshape(4, 4, FIRST_ROWS, D)
    mine = added([mine[:2], across(mine[2:], 4)]).astype(BF16)
    mine = added([mine[0], across(mine[1], 2)]).astype(BF16)
    mine, second_parts = lax.optimization_barrier((mine, second_parts))
    first_share = added(shares_along(mine))
    second_share = added(second_parts)
    return output, grad_tokens, first_share, second_share


def exchange_plain(index, devices, tokens, lengths, weights, vectors, cotangent):
    w_query, w_key, w_value, w_out, w_up, w_down = weights
    bias_up, bias_down, gain_attn, shift_attn, gain_ffn, shift_ffn = vectors
    share = D // devices

    def gathered(rows):
        return lax.all_gather(rows, AXES, axis=0, tiled=True).reshape(32, SHARE, D)

    def vector_rows(parts):
        rows = jnp.concatenate([spread(part, index, devices) for part in parts])
        rows = lax.psum(rows, AXES)
        pad = jnp.zeros((8 - rows.shape[0], D), rows.dtype)
        rows = jnp.concatenate([rows, pad])[None]
        return jnp.concatenate([rows, jnp.zeros((31, 8, D), rows.dtype)])

    def halved(parts):
        blocks = jnp.concatenate(parts, axis=1)
        return blocks[:16], blocks[16:]

    place = jnp.zeros((2,), jnp.int32)
    first_blocks = halved(
        [gathered(w.T) for w in (w_query, w_key, w_value)]
        + [vector_rows([gain_attn, shift_attn])]
    )
    up = lax.all_gather(w_up.T, AXES, axis=0, tiled=True).reshape(32, 4 * SHARE, D)
    down = lax.all_gather(w_down.T, AXES, axis=0, tiled=True).reshape(32, SHARE, 4, D)
    down = jnp.transpose(down, (0, 2, 1, 3)).reshape(32, 4 * SHARE, D)
    vectors = vector_rows([gain_ffn, shift_ffn, bias_down, bias_up])
    second_blocks = jnp.concatenate([gathered(w_out.T), up, down, vectors], axis=1)
    *kept, attn, total, weights, gains = attend(lengths, place, True, tokens, first_blocks)
    kept += [weights, gains]
    output, middle_grad, numer_grad, total_grad, near, far = feed(
        place, True, tokens, attn, total, cotangent, second_blocks
    )
    second = jnp.concatenate([near, far])
    grad_tokens, near, far = attend_back(
        lengths, place, True, tokens, middle_grad, numer_grad, total_grad, kept
    )
    first = jnp.concatenate([near, far])

    def scattered(rows):
        rows = rows.reshape(devices, -1, D)
        return lax.psum_scatter(rows, AXES, scatter_dimension=0, tiled=False).astype(F32)

    down = second[:, 5 * SHARE : 9 * SHARE].reshape(32, 4, SHARE, D)
    down = scattered(jnp.transpose(down, (0, 2, 1, 3)).reshape(32, 4 * SHARE, D))
    down = jnp.transpose(down.reshape(share, 4, D), (1, 0, 2)).reshape(4 * share, D)
    first_vectors = lax.psum(first[0, 3 * SHARE :].astype(F32), AXES)
    second_vectors = lax.psum(second[0, 9 * SHARE :].astype(F32), AXES)
    first_share = [scattered(first[:, p * SHARE : p * SHARE + SHARE]) for p in range(3)]
    second_share = [scattered(second[:, :SHARE]), scattered(second[:, SHARE : 5 * SHARE]), down]
    return (
        output,
        grad_tokens,
        jnp.concatenate(first_share + [first_vectors]),
        jnp.concatenate(second_share + [second_vectors]),
    )


def on_device(sizes, tokens, lengths, *rest):
    weights, vectors, cotangent = rest[:6], rest[6:12], rest[12]
    devices = sizes[0] * sizes[1]
    share = D // devices
    index = lax.axis_index(AXES)
    if sizes == (4, 8):
        place = jnp.stack([lax.axis_index("dp"), lax.axis_index("fsdp")]).astype(jnp.int32)
        output, grad_tokens, first, second = exchange_permutes(
            place, tokens, lengths, weights, vectors, cotangent
        )
    else:
        output, grad_tokens, first, second = exchange_plain(
            index, devices, tokens, lengths, weights, vectors, cotangent
        )

    def own(row):
        return lax.dynamic_slice(row, (index * share,), (share,))

    first_vectors = first[3 * share :]
    second_vectors = second[9 * share :]
    down = jnp.transpose(second[5 * share : 9 * share].reshape(4, share, D), (0, 2, 1))
    return (
        output,
        grad_tokens,
        first[:share].T,
        first[share : 2 * share].T,
        first[2 * share : 3 * share].T,
        second[:share].T,
        second[share : 5 * share].T,
        down.reshape(FF, share),
        lax.dynamic_slice(second_vectors[3:7].reshape(FF), (index * 4 * share,), (4 * share,)),
        own(second_vectors[2]),
        own(first_vectors[0]),
        own(first_vectors[1]),
        own(second_vectors[0]),
        own(second_vectors[1]),
    )


def solution(mesh):
    rows = P(AXES, None)
    columns = P(None, AXES)
    vector = P(AXES)
    sizes = (mesh.shape["dp"], mesh.shape["fsdp"])
    return jax.shard_map(
        functools.partial(on_device, sizes),
        mesh=mesh,
        in_specs=(rows, vector) + (columns,) * 6 + (vector,) * 6 + (rows,),
        out_specs=(rows, rows) + (columns,) * 6 + (vector,) * 6,
        check_vma=False,
    )
```

```python
import functools

import jax
import jax.numpy as jnp
import numpy as np
from jax import lax
from jax.experimental import pallas as pl
from jax.experimental.pallas import tpu as pltpu
from jax.sharding import PartitionSpec as P

D = 512
H = 8
DH = 64
FF = 2048
BLOCK = 16
LEVELS = 6
LEN = 1024
AXES = ("dp", "fsdp")
BF16 = jnp.bfloat16
F32 = jnp.float32

STARTS = (32, 1072, 1600, 1872, 2016, 2096)
SIZES = tuple(LEN >> level for level in range(LEVELS))
ROWS = 2192
GAPS = ((0, 32), (1056, 16), (1584, 16), (1856, 16), (2000, 16), (2080, 16), (2128, 64))
WINDOWS = 32
QUERIES = 64
KEYS = 128
POOL_CHUNK = 256
SHARE = 16
FIRST_ROWS = 3 * SHARE + 8
SECOND_ROWS = 9 * SHARE + 8
SCORE = 0.125 * 1.4426950408889634


def nn(left, right):
    return lax.dot_general(left, right, (((1,), (0,)), ((), ())), preferred_element_type=F32)


def nt(left, right):
    return lax.dot_general(left, right, (((1,), (1,)), ((), ())), preferred_element_type=F32)


def tn(left, right):
    return lax.dot_general(left, right, (((0,), (0,)), ((), ())), preferred_element_type=F32)


def score_bias():
    query = (np.arange(2 * QUERIES) % QUERIES)[:, None]
    key = np.arange(KEYS)[None, :] - 32
    near = np.abs(query // 16 - key // 16) <= 1
    apart = np.abs(query // 8 - key // 8) > 1
    return np.where(np.stack([near, near & apart]), 0.0, -1e30).astype(np.float32)


def pool_matrix():
    matrix = np.zeros((POOL_CHUNK, POOL_CHUNK), np.float32)
    first = 0
    for level in range(1, LEVELS):
        count = POOL_CHUNK >> level
        for row in range(count):
            matrix[first + row, row << level : (row + 1) << level] = 0.5**level
        first += count
    return matrix


def halves():
    lane = np.arange(128)
    return np.stack([lane < DH, lane >= DH]).astype(np.float32)


def window_loop(step):
    for window in range(WINDOWS):
        gaps = sum(window >= first for first in (16, 24, 28, 30, 31))
        row = STARTS[0] + QUERIES * window + 16 * gaps
        step(
            pl.ds(row, QUERIES),
            pl.ds(row - 32, KEYS),
            pl.ds(window * 2 * QUERIES, 2 * QUERIES),
            int(window >= 16),
        )


def row_loop(total, size, step):
    for first in range(0, total, size):
        step(first)


def row_fori(total, size, step, unroll):
    def body(index, carry):
        for inner in range(unroll):
            step(pl.multiple_of((index * unroll + inner) * size, size))
        return carry

    lax.fori_loop(0, total // (size * unroll), body, 0)


def pair_lanes(pair):
    return slice(128 * pair, 128 * pair + 128)


def by_head(values, half):
    return jnp.concatenate([values * half[0:1, :], values * half[1:2, :]], axis=0)


def joined_heads(values, low_head):
    return jnp.where(low_head, values[:QUERIES], values[QUERIES:])


def fill_counts(counts, length):
    clear_gaps(counts)
    for level in range(LEVELS):
        place = lax.broadcasted_iota(jnp.int32, (SIZES[level], 128), 0)
        span = 1 << level
        number = jnp.clip(length - place * span, 0, span).astype(F32)
        counts[STARTS[level] : STARTS[level] + SIZES[level], :] = number.astype(BF16)


def block_places(place, plain, sign):
    for half in range(2):
        for block in range(16):
            if plain:
                yield half, block, half * 16 + block
            else:
                column = place[1] ^ (half + 2 * (block // 4))
                row = (place[0] + 4 + sign * (block % 4)) % 4
                yield half, block, row * 8 + column


def sixteen(device):
    return pl.ds(pl.multiple_of(device * SHARE, SHARE), SHARE)


def sixty_four(device):
    return pl.ds(pl.multiple_of(device * 4 * SHARE, 4 * SHARE), 4 * SHARE)


def load_first(place, plain, blocks, weights, vectors):
    total = jnp.zeros((8, D), F32)
    for half, block, device in block_places(place, plain, -1):
        source = blocks[half]
        for part in range(3):
            rows = pl.ds(pl.multiple_of(part * D + device * SHARE, SHARE), SHARE)
            weights[rows, :] = source[block, part * SHARE : part * SHARE + SHARE, :]
        total = total + source[block, 3 * SHARE : 3 * SHARE + 8, :].astype(F32)
    vectors[...] = total


def load_second(place, plain, blocks, w_out, w_up, w_down, vectors):
    total = jnp.zeros((8, D), F32)
    for half, block, device in block_places(place, plain, -1):
        source = blocks[half]
        w_out[sixteen(device), :] = source[block, 0:SHARE, :]
        w_up[sixty_four(device), :] = source[block, SHARE : 5 * SHARE, :]
        for part in range(4):
            at = (5 + part) * SHARE
            w_down[part, sixteen(device), :] = source[block, at : at + SHARE, :]
        total = total + source[block, 9 * SHARE : 9 * SHARE + 8, :].astype(F32)
    vectors[...] = total


def layer_norm(values):
    mean = jnp.mean(values, axis=-1, keepdims=True)
    centred = values - mean
    inverse = lax.rsqrt(jnp.mean(centred * centred, axis=-1, keepdims=True) + 1e-05)
    return centred * inverse, inverse


def norm_back(gradient, normed, inverse, gain):
    scaled = gradient * gain
    return inverse * (
        scaled
        - jnp.mean(scaled, axis=-1, keepdims=True)
        - normed * jnp.mean(scaled * normed, axis=-1, keepdims=True)
    )


def clear_gaps(ref):
    for first, count in GAPS:
        ref[first : first + count, :] = jnp.zeros((count, ref.shape[1]), ref.dtype)


def spread_up(ref, factor):
    for level in range(LEVELS - 2, -1, -1):
        count = SIZES[level + 1]
        size = min(count, 64)

        def step(first, level=level, size=size):
            for pair in range(4):
                above = ref[pair, pl.ds(STARTS[level + 1] + first, size), :]
                if factor != 1.0:
                    above = above * factor
                for odd in (0, 1):
                    below = pl.ds(STARTS[level] + 2 * first + odd, size, stride=2)
                    ref[pair, below, :] = ref[pair, below, :] + above

        row_loop(count, size, step)


def attend_kernel(
    plain,
    lengths,
    place,
    tokens,
    near_blocks,
    far_blocks,
    bias,
    pool,
    half,
    query,
    key,
    value,
    probs,
    attn,
    total,
    weights,
    vectors,
    normed,
    joined,
    top,
    counts,
    numer,
    denom,
):
    @pl.when(pl.program_id(0) == 0)
    def _():
        load_first(place, plain, (near_blocks, far_blocks), weights, vectors)

    length = lengths[pl.program_id(0)]
    gain = vectors[0:1, :]
    shift = vectors[1:2, :]

    def norm_step(first):
        rows = pl.ds(first, 64)
        values, _ = layer_norm(tokens[rows, :].astype(F32))
        normed[rows, :] = (values * gain + shift).astype(BF16)

    row_loop(LEN, 64, norm_step)
    for ref in (query, key, value):
        clear_gaps(ref)
    fill_counts(counts, length)
    targets = ((query, 0), (key, D), (value, 2 * D))
    for first in range(0, LEN, POOL_CHUNK):
        rows = slice(first, first + POOL_CHUNK)
        chunk = first // POOL_CHUNK
        values = nt(normed[rows, :], weights[...])
        valid = (lax.broadcasted_iota(jnp.int32, (POOL_CHUNK, 1), 0) + first < length).astype(F32)
        joined[rows, : 2 * D] = values[:, : 2 * D].astype(BF16)
        joined[rows, 2 * D :] = (values[:, 2 * D :] * valid).astype(BF16)
        pooled = nn(pool[...], joined[rows, :])
        for ref, lane in targets:
            start = STARTS[0] + first
            ref[start : start + POOL_CHUNK, :] = joined[rows, lane : lane + D]
            at = 0
            for level in range(1, LEVELS):
                count = POOL_CHUNK >> level
                part = pooled[at : at + count, lane : lane + D]
                at += count
                if ref is value:
                    part = part * float(1 << level)
                if level < LEVELS - 1:
                    start = STARTS[level] + chunk * count
                    ref[start : start + count, :] = part.astype(BF16)
                else:
                    top[chunk * count : chunk * count + count, lane : lane + D] = part
    for ref, lane in targets:
        ref[STARTS[-1] : STARTS[-1] + SIZES[-1], :] = top[:, lane : lane + D].astype(BF16)

    def score_step(rows, near, flat, kind):
        allowed = bias[kind]
        for pair in range(4):
            lanes = pair_lanes(pair)
            scores = nt(by_head(query[rows, lanes], half), key[near, lanes])
            probs[flat, lanes] = jnp.exp2(scores * SCORE + allowed).astype(BF16)

    window_loop(score_step)
    low_head = lax.broadcasted_iota(jnp.int32, (QUERIES, 128), 1) < DH

    def value_step(rows, near, flat, kind):
        number = counts[near, :]
        for pair in range(4):
            lanes = pair_lanes(pair)
            both = nn(probs[flat, lanes], jnp.concatenate([value[near, lanes], number], axis=1))
            numer[pair, rows, :] = joined_heads(both[:, :128], low_head)
            denom[pair, rows, :] = joined_heads(both[:, 128:], low_head)

    window_loop(value_step)
    spread_up(numer, 1.0)
    spread_up(denom, 1.0)

    def join_step(first):
        rows = pl.ds(first, 64)
        inner = pl.ds(STARTS[0] + first, 64)
        for pair in range(4):
            lanes = pair_lanes(pair)
            below = denom[pair, inner, :]
            attn[rows, lanes] = (numer[pair, inner, :] / below).astype(BF16)
            total[rows, lanes] = below

    row_loop(LEN, 64, join_step)


def feed_kernel(
    plain,
    place,
    tokens,
    attn,
    total,
    cotangent,
    near_blocks,
    far_blocks,
    output,
    middle_grad,
    numer_grad,
    total_grad,
    grads_0,
    grads_1,
    grads_2,
    grads_3,
    w_out,
    w_up,
    w_down,
    vectors,
    middle,
    normed,
    inverse,
    normed_low,
    hidden,
    result,
    gathered,
    active,
    back,
    sums,
    acc_out,
    acc_up,
    acc_down,
):
    @pl.when(pl.program_id(0) == 0)
    def _():
        acc_out[...] = jnp.zeros_like(acc_out)
        acc_up[...] = jnp.zeros_like(acc_up)
        acc_down[...] = jnp.zeros_like(acc_down)
        sums[...] = jnp.zeros_like(sums)
        load_second(place, plain, (near_blocks, far_blocks), w_out, w_up, w_down, vectors)

    gain = vectors[0:1, :]
    shift = vectors[1:2, :]
    bias_down = vectors[2:3, :]
    middle[...] = nt(attn[...], w_out[...])

    def norm_step(first):
        rows = pl.ds(first, 64)
        values = middle[rows, :] + tokens[rows, :].astype(F32)
        middle[rows, :] = values
        norm, factor = layer_norm(values)
        normed[rows, :] = norm
        inverse[rows, :] = jnp.broadcast_to(factor, (64, 128))
        normed_low[rows, :] = (norm * gain + shift).astype(BF16)

    row_loop(LEN, 64, norm_step)
    gathered[...] = jnp.zeros_like(gathered)

    def part_step(part, carry):
        up = w_up[pl.ds(pl.multiple_of(part * D, D), D), :]
        down = w_down[part]
        bias_up = vectors[pl.ds(3 + part, 1), :]
        count = jnp.zeros((8, D), F32)
        for start in range(0, LEN, 512):
            wide = slice(start, start + 512)
            hidden[wide, :] = nt(normed_low[wide, :], up)
            result[wide, :] = nn(cotangent[wide, :], down)
            for first in range(start, start + 512, 64):
                rows = slice(first, first + 64)
                value = hidden[rows, :] + bias_up
                gate = 0.5 * jnp.tanh(0.5 * value) + 0.5
                active[rows, :] = (value * gate).astype(BF16)
                slope = gate * (1.0 + value * (1.0 - gate))
                gradient = (result[rows, :] * slope).astype(BF16)
                back[rows, :] = gradient
                count = count + jnp.sum(gradient.astype(F32).reshape(8, 8, D), axis=0)
        for start in range(0, LEN, 512):
            wide = slice(start, start + 512)
            middle[wide, :] += nt(active[wide, :], down)
            gathered[wide, :] += nn(back[wide, :], up)
        sums[pl.ds(pl.multiple_of(24 + 8 * part, 8), 8), :] += count
        acc_down[part] += tn(cotangent[...], active[...])
        acc_up[pl.ds(pl.multiple_of(part * D, D), D), :] += tn(back[...], normed_low[...])
        return carry

    lax.fori_loop(0, FF // D, part_step, 0)

    def back_step(first):
        rows = pl.ds(first, 64)
        output[rows, :] = (middle[rows, :] + bias_down).astype(BF16)
        gradient = gathered[rows, :]
        norm = normed[rows, :]
        value = cotangent[rows, :].astype(F32)
        sums[0:8, :] += jnp.sum((gradient * norm).reshape(8, 8, D), axis=0)
        sums[8:16, :] += jnp.sum(gradient.reshape(8, 8, D), axis=0)
        sums[16:24, :] += jnp.sum(value.reshape(8, 8, D), axis=0)
        value = value + norm_back(gradient, norm, inverse[rows, 0:1], gain)
        middle_grad[rows, :] = value.astype(BF16)

    row_loop(LEN, 64, back_step)
    acc_out[...] += tn(middle_grad[...], attn[...])
    gathered[...] = nn(middle_grad[...], w_out[...])

    def numer_step(first):
        rows = pl.ds(first, 64)
        gradient = gathered[rows, :].astype(BF16).astype(F32) / total[rows, :]
        numer_grad[rows, :] = gradient.astype(BF16)
        total_grad[rows, :] = (-gradient * attn[rows, :].astype(F32)).astype(BF16)

    row_loop(LEN, 64, numer_step)

    @pl.when(pl.program_id(0) == pl.num_programs(0) - 1)
    def _():
        small = jnp.sum(sums[...].reshape(7, 8, D), axis=1)
        small = jnp.concatenate([small, jnp.zeros((1, D), F32)], axis=0).astype(BF16)
        for half, block, device in block_places(place, plain, 1):
            target = (grads_0, grads_1, grads_2, grads_3)[block // 4]
            into = 4 * half + block % 4
            target[into, 0:SHARE, :] = acc_out[sixteen(device), :].astype(BF16)
            target[into, SHARE : 5 * SHARE, :] = acc_up[sixty_four(device), :].astype(BF16)
            for part in range(4):
                at = (5 + part) * SHARE
                target[into, at : at + SHARE, :] = acc_down[part, sixteen(device), :].astype(BF16)
            target[into, 9 * SHARE : 9 * SHARE + 8, :] = small


def attend_back_kernel(
    plain,
    lengths,
    place,
    tokens,
    middle_grad,
    numer_grad,
    total_grad,
    query,
    key,
    value,
    probs,
    weights,
    vectors,
    pool,
    half,
    grad_tokens,
    near_grads,
    far_grads,
    numer,
    denom,
    score_grad,
    total,
    joined,
    normed,
    counts,
    top,
    sums,
    acc,
):
    step_index = pl.program_id(0)
    length = lengths[step_index]

    @pl.when(step_index == 0)
    def _():
        acc[...] = jnp.zeros_like(acc)
        sums[...] = jnp.zeros_like(sums)

    gain = vectors[0:1, :]
    shift = vectors[1:2, :]
    clear_gaps(numer)
    clear_gaps(denom)
    fill_counts(counts, length)
    for source, target in ((numer_grad, numer), (total_grad, denom)):
        target[STARTS[0] : STARTS[0] + LEN, :] = source[...]
        for first in range(0, LEN, POOL_CHUNK):
            chunk = first // POOL_CHUNK
            pooled = nn(pool[...], source[first : first + POOL_CHUNK, :])
            at = 0
            for level in range(1, LEVELS):
                count = POOL_CHUNK >> level
                part = pooled[at : at + count] * float(1 << level)
                at += count
                if level < LEVELS - 1:
                    start = STARTS[level] + chunk * count
                    target[start : start + count, :] = part.astype(BF16)
                else:
                    top[chunk * count : chunk * count + count, :] = part
        target[STARTS[-1] : STARTS[-1] + SIZES[-1], :] = top[...].astype(BF16)

    def score_step(rows, near, flat, kind):
        number = counts[near, :]
        for pair in range(4):
            lanes = pair_lanes(pair)
            left = jnp.concatenate(
                [by_head(numer[rows, lanes], half), by_head(denom[rows, lanes], half)], axis=1
            )
            right = jnp.concatenate([value[near, lanes], number], axis=1)
            score_grad[flat, lanes] = (nt(left, right) * probs[flat, lanes].astype(F32)).astype(BF16)

    window_loop(score_step)
    low_head = lax.broadcasted_iota(jnp.int32, (QUERIES, 128), 1) < DH

    def query_step(rows, near, flat, kind):
        for pair in range(4):
            lanes = pair_lanes(pair)
            both = nn(score_grad[flat, lanes], key[near, lanes])
            total[pair, rows, :] = joined_heads(both, low_head)

    window_loop(query_step)
    spread_up(total, 0.5)

    def take(at, scale, masked):
        def take_step(first):
            rows = pl.ds(first, 64)
            if masked:
                place = lax.broadcasted_iota(jnp.int32, (64, 1), 0) + first
                valid = (place < length).astype(F32)
            for pair in range(4):
                values = total[pair, pl.ds(STARTS[0] + first, 64), :]
                if scale != 1.0:
                    values = values * scale
                if masked:
                    values = values * valid
                joined[rows, at + 128 * pair : at + 128 * pair + 128] = values.astype(BF16)

        row_loop(LEN, 64, take_step)

    take(0, 0.125, False)
    for at, left, right, factor, scale, masked in (
        (D, score_grad, query, 0.5, 0.125, False),
        (2 * D, probs, numer, 1.0, 1.0, True),
    ):
        total[...] = jnp.zeros_like(total)

        def near_step(rows, near, flat, kind, left=left, right=right):
            for pair in range(4):
                lanes = pair_lanes(pair)
                total[pair, near, :] += tn(left[flat, lanes], by_head(right[rows, lanes], half))

        window_loop(near_step)
        spread_up(total, factor)
        take(at, scale, masked)

    def norm_step(first):
        rows = pl.ds(first, 64)
        values, _ = layer_norm(tokens[rows, :].astype(F32))
        normed[rows, :] = (values * gain + shift).astype(BF16)

    row_loop(LEN, 64, norm_step)
    for part in range(3):
        lanes = slice(D * part, D * part + D)
        acc[lanes, :] += tn(joined[:, lanes], normed[...])
    for first in range(0, LEN, POOL_CHUNK):
        rows = slice(first, first + POOL_CHUNK)
        passed = nn(joined[rows, :], weights[...])
        for pair in range(4):
            total[pair, rows, :] = passed[:, pair_lanes(pair)]

    def back_step(first):
        rows = pl.ds(first, 64)
        norm, inverse = layer_norm(tokens[rows, :].astype(F32))
        gradient = jnp.concatenate([total[pair, rows, :] for pair in range(4)], axis=1)
        sums[0:8, :] += jnp.sum((gradient * norm).reshape(8, 8, D), axis=0)
        sums[8:16, :] += jnp.sum(gradient.reshape(8, 8, D), axis=0)
        value = middle_grad[rows, :].astype(F32) + norm_back(gradient, norm, inverse, gain)
        grad_tokens[rows, :] = value.astype(BF16)

    row_loop(LEN, 64, back_step)

    @pl.when(step_index == pl.num_programs(0) - 1)
    def _():
        small = jnp.sum(sums[...].reshape(2, 8, D), axis=1)
        small = jnp.concatenate([small, jnp.zeros((6, D), F32)], axis=0).astype(BF16)
        for side, block, device in block_places(place, plain, 1):
            target = (near_grads, far_grads)[side]
            for part in range(3):
                rows = pl.ds(pl.multiple_of(part * D + device * SHARE, SHARE), SHARE)
                target[block, part * SHARE : part * SHARE + SHARE, :] = acc[rows, :].astype(BF16)
            target[block, 3 * SHARE : 3 * SHARE + 8, :] = small


SMEM = pl.BlockSpec(memory_space=pltpu.SMEM)


def whole(*shape):
    return pl.BlockSpec(shape, lambda i: (0,) * len(shape), pipeline_mode=pl.Buffered(1))


def per_sequence(rows, columns):
    return pl.BlockSpec((rows, columns), lambda i: (i, 0))


def vmem(rows, columns, dtype):
    return pltpu.VMEM((rows, columns), dtype)


def shape_of(rows, columns, dtype):
    return jax.ShapeDtypeStruct((rows, columns), dtype)


PARAMS = pltpu.CompilerParams(
    dimension_semantics=("arbitrary",), vmem_limit_bytes=63 * 1024 * 1024
)


def cost(microseconds):
    return pl.CostEstimate(
        flops=int(microseconds * 1.0e9), bytes_accessed=int(microseconds * 1.0e6), transcendentals=0
    )


def attend(lengths, place, plain, tokens, blocks):
    count = lengths.shape[0]
    levels = shape_of(count * ROWS, D, BF16)
    one = per_sequence(LEN, D)
    all_levels = per_sequence(ROWS, D)
    flat = WINDOWS * 2 * QUERIES
    return pl.pallas_call(
        functools.partial(attend_kernel, plain),
        grid=(count,),
        in_specs=[
            SMEM,
            SMEM,
            one,
            whole(16, FIRST_ROWS, D),
            whole(16, FIRST_ROWS, D),
            whole(2, 2 * QUERIES, KEYS),
            whole(POOL_CHUNK, POOL_CHUNK),
            whole(2, 128),
        ],
        out_specs=[all_levels] * 3
        + [per_sequence(flat, D), one, one, whole(3 * D, D), whole(8, D)],
        out_shape=[levels] * 3
        + [
            shape_of(count * flat, D, BF16),
            shape_of(count * LEN, D, BF16),
            shape_of(count * LEN, D, F32),
            shape_of(3 * D, D, BF16),
            shape_of(8, D, F32),
        ],
        scratch_shapes=[
            vmem(LEN, D, BF16),
            vmem(LEN, 3 * D, BF16),
            vmem(SIZES[-1], 3 * D, F32),
            vmem(ROWS, 128, BF16),
            pltpu.VMEM((4, ROWS, 128), F32),
            pltpu.VMEM((4, ROWS, 128), F32),
        ],
        compiler_params=PARAMS,
        cost_estimate=cost(40),
        name="attend",
    )(
        lengths,
        place,
        tokens,
        *blocks,
        jnp.asarray(score_bias()),
        jnp.asarray(pool_matrix(), BF16),
        jnp.asarray(halves(), BF16),
    )


def feed(place, plain, tokens, attn, total, cotangent, blocks):
    rows = tokens.shape[0]
    one = per_sequence(LEN, D)
    low = shape_of(rows, D, BF16)
    grads = whole(8, SECOND_ROWS, D)
    return pl.pallas_call(
        functools.partial(feed_kernel, plain),
        grid=(rows // LEN,),
        in_specs=[SMEM] + [one] * 4 + [whole(16, SECOND_ROWS, D)] * 2,
        out_specs=[one] * 4 + [grads] * 4,
        out_shape=[low] * 4 + [jax.ShapeDtypeStruct((8, SECOND_ROWS, D), BF16)] * 4,
        scratch_shapes=[
            vmem(D, D, BF16),
            vmem(FF, D, BF16),
            pltpu.VMEM((4, D, D), BF16),
            vmem(8, D, F32),
            vmem(LEN, D, F32),
            vmem(LEN, D, F32),
            vmem(LEN, 128, F32),
            vmem(LEN, D, BF16),
            vmem(LEN, D, F32),
            vmem(LEN, D, F32),
            vmem(LEN, D, F32),
            vmem(LEN, D, BF16),
            vmem(LEN, D, BF16),
            vmem(56, D, F32),
            vmem(D, D, F32),
            vmem(FF, D, F32),
            pltpu.VMEM((4, D, D), F32),
        ],
        compiler_params=PARAMS,
        cost_estimate=cost(75),
        name="feed",
    )(place, tokens, attn, total, cotangent, *blocks)


def attend_back(lengths, place, plain, tokens, middle_grad, numer_grad, total_grad, kept):
    count = lengths.shape[0]
    one = per_sequence(LEN, D)
    all_levels = per_sequence(ROWS, D)
    flat = WINDOWS * 2 * QUERIES
    grads = whole(16, FIRST_ROWS, D)
    return pl.pallas_call(
        functools.partial(attend_back_kernel, plain),
        grid=(count,),
        in_specs=[SMEM, SMEM]
        + [one] * 4
        + [all_levels] * 3
        + [per_sequence(flat, D)]
        + [whole(3 * D, D), whole(8, D), whole(POOL_CHUNK, POOL_CHUNK), whole(2, 128)],
        out_specs=[one, grads, grads],
        out_shape=[shape_of(count * LEN, D, BF16)]
        + [jax.ShapeDtypeStruct((16, FIRST_ROWS, D), BF16)] * 2,
        scratch_shapes=[
            vmem(ROWS, D, BF16),
            vmem(ROWS, D, BF16),
            vmem(flat, D, BF16),
            pltpu.VMEM((4, ROWS, 128), F32),
            vmem(LEN, 3 * D, BF16),
            vmem(LEN, D, BF16),
            vmem(ROWS, 128, BF16),
            vmem(SIZES[-1], D, F32),
            vmem(16, D, F32),
            vmem(3 * D, D, F32),
        ],
        compiler_params=PARAMS,
        cost_estimate=cost(60),
        name="attend_back",
    )(
        lengths,
        place,
        tokens,
        middle_grad,
        numer_grad,
        total_grad,
        *kept,
        jnp.asarray(pool_matrix(), BF16),
        jnp.asarray(halves(), BF16),
    )


def pack_kernel(place, *refs):
    w_query, w_key, w_value, w_out, w_up, w_down, bias_up, bias_down, *norms, first, second = refs
    for part, ref in enumerate((w_query, w_key, w_value)):
        first[part * SHARE : part * SHARE + SHARE, :] = ref[...]
    second[0:SHARE, :] = w_out[...]
    second[SHARE : 5 * SHARE, :] = w_up[...]
    for part in range(4):
        at = (5 + part) * SHARE
        second[at : at + SHARE, :] = w_down[:, D * part : D * part + D]
    device = place[0] * 8 + place[1]
    lane = lax.broadcasted_iota(jnp.int32, (SHARE, D), 1)
    mine = lane == lax.broadcasted_iota(jnp.int32, (SHARE, D), 0) + device * SHARE
    mine = mine.astype(F32).astype(BF16)
    gain_attn, shift_attn, gain_ffn, shift_ffn = norms
    row = lax.broadcasted_iota(jnp.int32, (8, D), 0)

    def rows_of(vectors):
        total = jnp.zeros((8, D), F32)
        for place_of, vector in enumerate(vectors):
            total = jnp.where(row == place_of, nn(vector[...], mine), total)
        return total

    first[3 * SHARE :, :] = rows_of((gain_attn, shift_attn)).astype(BF16)
    lane = lax.broadcasted_iota(jnp.int32, (4 * SHARE, D), 1)
    mine_up = lane == lax.broadcasted_iota(jnp.int32, (4 * SHARE, D), 0) + (device % 8) * 4 * SHARE
    wide = nn(bias_up[...], mine_up.astype(F32).astype(BF16))
    vectors = rows_of((gain_ffn, shift_ffn, bias_down))
    second[9 * SHARE :, :] = jnp.where(row == 3 + device // 8, wide, vectors).astype(BF16)


def pack(place, weights, vectors):
    operands = [w.T for w in weights] + [v.reshape(1, -1) for v in vectors]
    return pl.pallas_call(
        pack_kernel,
        in_specs=[SMEM] + [pl.BlockSpec(memory_space=pltpu.VMEM)] * len(operands),
        out_specs=[pl.BlockSpec(memory_space=pltpu.VMEM)] * 2,
        out_shape=[shape_of(FIRST_ROWS, D, BF16), shape_of(SECOND_ROWS, D, BF16)],
        cost_estimate=cost(2),
        name="pack",
    )(place, *operands)


def across(values, bits):
    return lax.ppermute(values, "fsdp", [(i, i ^ bits) for i in range(8)])


def along(values, step):
    return lax.ppermute(values, "dp", [(i, (i + step) % 4) for i in range(4)])


def gather_rows(packed):
    return jnp.stack([packed] + [along(packed, step) for step in (1, 2, 3)])


def shares_along(blocks):
    return [blocks[0]] + [along(blocks[step], step) for step in (1, 2, 3)]


def added(parts):
    return sum(part.astype(F32) for part in parts)


def spread(vector, index, devices):
    share = vector.shape[0]
    full = jnp.tile(vector, devices)
    mine = lax.broadcasted_iota(jnp.int32, full.shape, 0) // share == index
    return jnp.where(mine, full, jnp.zeros_like(full)).reshape(-1, D)


def finish_kernel(place, *refs):
    first, second, outs = refs[:4], refs[4:8], refs[8:]
    query, key, value, out, up, down, bias_up, bias_down, *norms = outs

    def summed(parts, rows):
        return sum(part[rows, :].astype(F32) for part in parts)

    for place_of, ref in enumerate((query, key, value)):
        ref[...] = summed(first, slice(place_of * SHARE, place_of * SHARE + SHARE))
    out[...] = summed(second, slice(0, SHARE))
    up[...] = summed(second, slice(SHARE, 5 * SHARE))
    for part in range(4):
        at = (5 + part) * SHARE
        down[:, D * part : D * part + D] = summed(second, slice(at, at + SHARE))
    device = place[0] * 8 + place[1]
    shift = lax.rem(D - device * SHARE, D)
    mine_first = pltpu.roll(summed(first, slice(3 * SHARE, FIRST_ROWS)), shift, 1)
    vectors = summed(second, slice(9 * SHARE, SECOND_ROWS))
    mine_second = pltpu.roll(vectors, shift, 1)
    row = lax.broadcasted_iota(jnp.int32, (8, D), 0)
    wide = jnp.sum(jnp.where(row == 3 + device // 8, vectors, 0.0), axis=0, keepdims=True)
    wide = pltpu.roll(jnp.broadcast_to(wide, (8, D)), lax.rem(D - (device % 8) * 4 * SHARE, D), 1)
    bias_up[...] = wide[0:1, : 4 * SHARE]
    bias_down[...] = mine_second[2:3, :SHARE]
    gain_attn, shift_attn, gain_ffn, shift_ffn = norms
    gain_attn[...] = mine_first[0:1, :SHARE]
    shift_attn[...] = mine_first[1:2, :SHARE]
    gain_ffn[...] = mine_second[0:1, :SHARE]
    shift_ffn[...] = mine_second[1:2, :SHARE]


def finish(place, first, second):
    shapes = [(SHARE, D)] * 4 + [(4 * SHARE, D), (SHARE, FF), (1, 4 * SHARE)] + [(1, SHARE)] * 5
    grads = pl.pallas_call(
        finish_kernel,
        in_specs=[SMEM] + [pl.BlockSpec(memory_space=pltpu.VMEM)] * 8,
        out_specs=[pl.BlockSpec(memory_space=pltpu.VMEM)] * 12,
        out_shape=[shape_of(rows, columns, F32) for rows, columns in shapes],
        cost_estimate=cost(2),
        name="finish",
    )(place, *first, *second)
    return [grad.T for grad in grads[:6]] + [grad.reshape(-1) for grad in grads[6:]]


def exchange_permutes(place, tokens, lengths, weights, vectors, cotangent):
    first, second = pack(place, weights, vectors)
    rows = gather_rows(first)
    in_x, in_y = across(rows, 2), across(rows, 4)
    diagonal = jnp.concatenate([across(in_x[:2], 4), across(in_y[2:], 2)])
    near = jnp.concatenate([rows, in_x, in_y, diagonal])
    second_rows = gather_rows(second)
    near, second_rows = lax.optimization_barrier((near, second_rows))
    first_blocks = (near, across(near, 1))
    first_blocks, second_rows = lax.optimization_barrier((first_blocks, second_rows))
    others = [across(second_rows, bits) for bits in (2, 4, 6)]
    *kept, attn, total, weights, gains = attend(lengths, place, False, tokens, first_blocks)
    kept += [weights, gains]
    attn, total, others = lax.optimization_barrier((attn, total, others))
    near = jnp.concatenate([second_rows] + others)
    second_blocks = (near, across(near, 1))
    output, middle_grad, numer_grad, total_grad, *parts = feed(
        place, False, tokens, attn, total, cotangent, second_blocks
    )
    others = [across(parts[chip], bits) for chip, bits in ((1, 2), (2, 4), (3, 6))]
    grad_tokens, near, far = attend_back(
        lengths, place, False, tokens, middle_grad, numer_grad, total_grad, kept
    )
    near, far, others = lax.optimization_barrier((near, far, others))
    second = added([parts[0]] + others).astype(BF16)
    second = added([second[:4], across(second[4:], 1)]).astype(BF16)
    first = added([near, across(far, 1)]).astype(BF16).reshape(4, 4, FIRST_ROWS, D)
    by_x, by_y = first[:, :2], first[:, 2:]
    sent_x = across(jnp.stack([by_x[1], by_x[3]]), 2)
    sent_y = across(jnp.stack([by_y[2], by_y[3]]), 4)
    by_x = added([jnp.stack([by_x[0], by_x[2]]), sent_x]).astype(BF16)
    by_y = added([jnp.stack([by_y[0], by_y[1]]), sent_y]).astype(BF16)
    by_x = added([by_x[0], across(by_x[1], 4)]).astype(BF16)
    by_y = added([by_y[0], across(by_y[1], 2)]).astype(BF16)
    first = shares_along([by_x[0], by_x[1], by_y[0], by_y[1]])
    second = shares_along(second)
    return output, grad_tokens, finish(place, first, second)


def exchange_plain(index, devices, tokens, lengths, weights, vectors, cotangent):
    w_query, w_key, w_value, w_out, w_up, w_down = weights
    bias_up, bias_down, gain_attn, shift_attn, gain_ffn, shift_ffn = vectors
    share = D // devices

    def gathered(rows):
        return lax.all_gather(rows, AXES, axis=0, tiled=True).reshape(32, SHARE, D)

    def vector_rows(parts):
        rows = jnp.concatenate([spread(part, index, devices) for part in parts])
        rows = lax.psum(rows, AXES)
        pad = jnp.zeros((8 - rows.shape[0], D), rows.dtype)
        rows = jnp.concatenate([rows, pad])[None]
        return jnp.concatenate([rows, jnp.zeros((31, 8, D), rows.dtype)])

    def halved(parts):
        blocks = jnp.concatenate(parts, axis=1)
        return blocks[:16], blocks[16:]

    place = jnp.zeros((2,), jnp.int32)
    first_blocks = halved(
        [gathered(w.T) for w in (w_query, w_key, w_value)]
        + [vector_rows([gain_attn, shift_attn])]
    )
    up = lax.all_gather(w_up.T, AXES, axis=0, tiled=True).reshape(32, 4 * SHARE, D)
    down = lax.all_gather(w_down.T, AXES, axis=0, tiled=True).reshape(32, SHARE, 4, D)
    down = jnp.transpose(down, (0, 2, 1, 3)).reshape(32, 4 * SHARE, D)
    second_blocks = halved(
        [gathered(w_out.T), up, down, vector_rows([gain_ffn, shift_ffn, bias_down, bias_up])]
    )
    *kept, attn, total, weights, gains = attend(lengths, place, True, tokens, first_blocks)
    kept += [weights, gains]
    output, middle_grad, numer_grad, total_grad, *parts = feed(
        place, True, tokens, attn, total, cotangent, second_blocks
    )
    second = jnp.stack(parts).reshape(4, 2, 4, SECOND_ROWS, D)
    second = jnp.transpose(second, (1, 0, 2, 3, 4)).reshape(32, SECOND_ROWS, D)
    grad_tokens, near, far = attend_back(
        lengths, place, True, tokens, middle_grad, numer_grad, total_grad, kept
    )
    first = jnp.concatenate([near, far])

    def scattered(rows):
        rows = rows.reshape(devices, -1, D)
        return lax.psum_scatter(rows, AXES, scatter_dimension=0, tiled=False).astype(F32)

    down = second[:, 5 * SHARE : 9 * SHARE].reshape(32, 4, SHARE, D)
    down = scattered(jnp.transpose(down, (0, 2, 1, 3)).reshape(32, 4 * SHARE, D))
    down = jnp.transpose(down.reshape(share, 4, D), (1, 0, 2)).reshape(4 * share, D)
    first_vectors = lax.psum(first[0, 3 * SHARE :].astype(F32), AXES)
    second_vectors = lax.psum(second[0, 9 * SHARE :].astype(F32), AXES)
    down = jnp.transpose(down.reshape(4, share, D), (0, 2, 1)).reshape(FF, share)

    def own(row):
        return lax.dynamic_slice(row, (index * share,), (share,))

    return (
        output,
        grad_tokens,
        [
            *[scattered(first[:, p * SHARE : p * SHARE + SHARE]).T for p in range(3)],
            scattered(second[:, :SHARE]).T,
            scattered(second[:, SHARE : 5 * SHARE]).T,
            down,
            lax.dynamic_slice(second_vectors[3:7].reshape(FF), (index * 4 * share,), (4 * share,)),
            own(second_vectors[2]),
            own(first_vectors[0]),
            own(first_vectors[1]),
            own(second_vectors[0]),
            own(second_vectors[1]),
        ],
    )


def on_device(sizes, tokens, lengths, *rest):
    weights, vectors, cotangent = rest[:6], rest[6:12], rest[12]
    if sizes == (4, 8):
        place = jnp.stack([lax.axis_index("dp"), lax.axis_index("fsdp")]).astype(jnp.int32)
        output, grad_tokens, grads = exchange_permutes(
            place, tokens, lengths, weights, vectors, cotangent
        )
    else:
        index = lax.axis_index(AXES)
        output, grad_tokens, grads = exchange_plain(
            index, sizes[0] * sizes[1], tokens, lengths, weights, vectors, cotangent
        )
    return (output, grad_tokens, *grads)


def solution(mesh):
    rows = P(AXES, None)
    columns = P(None, AXES)
    vector = P(AXES)
    sizes = (mesh.shape["dp"], mesh.shape["fsdp"])
    return jax.shard_map(
        functools.partial(on_device, sizes),
        mesh=mesh,
        in_specs=(rows, vector) + (columns,) * 6 + (vector,) * 6 + (rows,),
        out_specs=(rows, rows) + (columns,) * 6 + (vector,) * 6,
        check_vma=False,
    )
```

```python
import functools

import jax
import jax.numpy as jnp
import numpy as np
from jax import lax
from jax.experimental import pallas as pl
from jax.experimental.pallas import tpu as pltpu
from jax.sharding import PartitionSpec as P

D = 512
H = 8
DH = 64
FF = 2048
BLOCK = 16
LEVELS = 6
LEN = 1024
AXES = ("dp", "fsdp")
BF16 = jnp.bfloat16
F32 = jnp.float32

STARTS = (32, 1072, 1600, 1872, 2016, 2096)
SIZES = tuple(LEN >> level for level in range(LEVELS))
ROWS = 2192
GAPS = ((0, 32), (1056, 16), (1584, 16), (1856, 16), (2000, 16), (2080, 16), (2128, 64))
WINDOWS = 32
QUERIES = 64
KEYS = 128
POOL_CHUNK = 256
SHARE = 16
FIRST_ROWS = 3 * SHARE + 8
SECOND_ROWS = 9 * SHARE + 8
SCORE = 0.125 * 1.4426950408889634


def nn(left, right):
    return lax.dot_general(left, right, (((1,), (0,)), ((), ())), preferred_element_type=F32)


def nt(left, right):
    return lax.dot_general(left, right, (((1,), (1,)), ((), ())), preferred_element_type=F32)


def tn(left, right):
    return lax.dot_general(left, right, (((0,), (0,)), ((), ())), preferred_element_type=F32)


def score_bias():
    query = (np.arange(2 * QUERIES) % QUERIES)[:, None]
    key = np.arange(KEYS)[None, :] - 32
    near = np.abs(query // 16 - key // 16) <= 1
    apart = np.abs(query // 8 - key // 8) > 1
    return np.where(np.stack([near, near & apart]), 0.0, -1e30).astype(np.float32)


def pool_matrix():
    matrix = np.zeros((POOL_CHUNK, POOL_CHUNK), np.float32)
    first = 0
    for level in range(1, LEVELS):
        count = POOL_CHUNK >> level
        for row in range(count):
            matrix[first + row, row << level : (row + 1) << level] = 0.5**level
        first += count
    return matrix


def halves():
    lane = np.arange(128)
    return np.stack([lane < DH, lane >= DH]).astype(np.float32)


def window_loop(step):
    for window in range(WINDOWS):
        gaps = sum(window >= first for first in (16, 24, 28, 30, 31))
        row = STARTS[0] + QUERIES * window + 16 * gaps
        step(
            pl.ds(row, QUERIES),
            pl.ds(row - 32, KEYS),
            pl.ds(window * 2 * QUERIES, 2 * QUERIES),
            int(window >= 16),
        )


def row_loop(total, size, step):
    for first in range(0, total, size):
        step(first)


def row_fori(total, size, step, unroll):
    def body(index, carry):
        for inner in range(unroll):
            step(pl.multiple_of((index * unroll + inner) * size, size))
        return carry

    lax.fori_loop(0, total // (size * unroll), body, 0)


def pair_lanes(pair):
    return slice(128 * pair, 128 * pair + 128)


def by_head(values, half):
    return jnp.concatenate([values * half[0:1, :], values * half[1:2, :]], axis=0)


def joined_heads(values, low_head):
    return jnp.where(low_head, values[:QUERIES], values[QUERIES:])


def fill_counts(counts, length):
    clear_gaps(counts)
    for level in range(LEVELS):
        place = lax.broadcasted_iota(jnp.int32, (SIZES[level], 128), 0)
        span = 1 << level
        number = jnp.clip(length - place * span, 0, span).astype(F32)
        counts[STARTS[level] : STARTS[level] + SIZES[level], :] = number.astype(BF16)


def block_places(place, plain, sign):
    for half in range(2):
        for block in range(16):
            if plain:
                yield half, block, half * 16 + block
            else:
                column = place[1] ^ (half + 2 * (block // 4))
                row = (place[0] + 4 + sign * (block % 4)) % 4
                yield half, block, row * 8 + column


def sixteen(device):
    return pl.ds(pl.multiple_of(device * SHARE, SHARE), SHARE)


def sixty_four(device):
    return pl.ds(pl.multiple_of(device * 4 * SHARE, 4 * SHARE), 4 * SHARE)


def load_first(place, plain, blocks, weights, vectors):
    total = jnp.zeros((8, D), F32)
    for half, block, device in block_places(place, plain, -1):
        source = blocks[half]
        for part in range(3):
            rows = pl.ds(pl.multiple_of(part * D + device * SHARE, SHARE), SHARE)
            weights[rows, :] = source[block, part * SHARE : part * SHARE + SHARE, :]
        total = total + source[block, 3 * SHARE : 3 * SHARE + 8, :].astype(F32)
    vectors[...] = total


def load_second(place, plain, blocks, w_out, w_up, w_down, vectors):
    total = jnp.zeros((8, D), F32)
    for half, block, device in block_places(place, plain, -1):
        source = blocks[4 * half + block // 4].at[block % 4]
        w_out[sixteen(device), :] = source[0:SHARE, :]
        w_up[sixty_four(device), :] = source[SHARE : 5 * SHARE, :]
        for part in range(4):
            at = (5 + part) * SHARE
            w_down[part, sixteen(device), :] = source[at : at + SHARE, :]
        total = total + source[9 * SHARE : 9 * SHARE + 8, :].astype(F32)
    vectors[...] = total


def layer_norm(values):
    mean = jnp.mean(values, axis=-1, keepdims=True)
    centred = values - mean
    inverse = lax.rsqrt(jnp.mean(centred * centred, axis=-1, keepdims=True) + 1e-05)
    return centred * inverse, inverse


def norm_back(gradient, normed, inverse, gain):
    scaled = gradient * gain
    return inverse * (
        scaled
        - jnp.mean(scaled, axis=-1, keepdims=True)
        - normed * jnp.mean(scaled * normed, axis=-1, keepdims=True)
    )


def clear_gaps(ref):
    for first, count in GAPS:
        ref[first : first + count, :] = jnp.zeros((count, ref.shape[1]), ref.dtype)


def spread_up(ref, factor):
    for level in range(LEVELS - 2, -1, -1):
        count = SIZES[level + 1]
        size = min(count, 64)

        def step(first, level=level, size=size):
            for pair in range(4):
                above = ref[pair, pl.ds(STARTS[level + 1] + first, size), :]
                if factor != 1.0:
                    above = above * factor
                for odd in (0, 1):
                    below = pl.ds(STARTS[level] + 2 * first + odd, size, stride=2)
                    ref[pair, below, :] = ref[pair, below, :] + above

        row_loop(count, size, step)


def attend_kernel(
    plain,
    lengths,
    place,
    tokens,
    near_blocks,
    far_blocks,
    bias,
    pool,
    half,
    query_out,
    key_out,
    value_out,
    probs_out,
    attn,
    total,
    weights,
    vectors,
    query,
    key,
    value,
    probs,
    normed,
    joined,
    top,
    counts,
    numer,
    denom,
    done,
):
    def copy_out(index):
        source = (query, key, value, probs)[index]
        target = (query_out, key_out, value_out, probs_out)[index]
        return pltpu.make_async_copy(source, target.at[pl.program_id(0)], done.at[index])

    @pl.when(pl.program_id(0) == 0)
    def _():
        load_first(place, plain, (near_blocks, far_blocks), weights, vectors)

    length = lengths[pl.program_id(0)]
    gain = vectors[0:1, :]
    shift = vectors[1:2, :]

    def norm_step(first):
        rows = pl.ds(first, 64)
        values, _ = layer_norm(tokens[rows, :].astype(F32))
        normed[rows, :] = (values * gain + shift).astype(BF16)

    row_loop(LEN, 64, norm_step)
    for ref in (query, key, value):
        clear_gaps(ref)
    fill_counts(counts, length)
    targets = ((query, 0), (key, D), (value, 2 * D))
    for first in range(0, LEN, POOL_CHUNK):
        rows = slice(first, first + POOL_CHUNK)
        chunk = first // POOL_CHUNK
        values = nt(normed[rows, :], weights[...])
        valid = (lax.broadcasted_iota(jnp.int32, (POOL_CHUNK, 1), 0) + first < length).astype(F32)
        joined[rows, : 2 * D] = values[:, : 2 * D].astype(BF16)
        joined[rows, 2 * D :] = (values[:, 2 * D :] * valid).astype(BF16)
        pooled = nn(pool[...], joined[rows, :])
        for ref, lane in targets:
            start = STARTS[0] + first
            ref[start : start + POOL_CHUNK, :] = joined[rows, lane : lane + D]
            at = 0
            for level in range(1, LEVELS):
                count = POOL_CHUNK >> level
                part = pooled[at : at + count, lane : lane + D]
                at += count
                if ref is value:
                    part = part * float(1 << level)
                if level < LEVELS - 1:
                    start = STARTS[level] + chunk * count
                    ref[start : start + count, :] = part.astype(BF16)
                else:
                    top[chunk * count : chunk * count + count, lane : lane + D] = part
    for ref, lane in targets:
        ref[STARTS[-1] : STARTS[-1] + SIZES[-1], :] = top[:, lane : lane + D].astype(BF16)
    for index in range(3):
        copy_out(index).start()

    def score_step(rows, near, flat, kind):
        allowed = bias[kind]
        for pair in range(4):
            lanes = pair_lanes(pair)
            scores = nt(by_head(query[rows, lanes], half), key[near, lanes])
            probs[flat, lanes] = jnp.exp2(scores * SCORE + allowed).astype(BF16)

    window_loop(score_step)
    copy_out(3).start()
    low_head = lax.broadcasted_iota(jnp.int32, (QUERIES, 128), 1) < DH

    def value_step(rows, near, flat, kind):
        number = counts[near, :]
        for pair in range(4):
            lanes = pair_lanes(pair)
            both = nn(probs[flat, lanes], jnp.concatenate([value[near, lanes], number], axis=1))
            numer[pair, rows, :] = joined_heads(both[:, :128], low_head)
            denom[pair, rows, :] = joined_heads(both[:, 128:], low_head)

    window_loop(value_step)
    spread_up(numer, 1.0)
    spread_up(denom, 1.0)

    def join_step(first):
        rows = pl.ds(first, 64)
        inner = pl.ds(STARTS[0] + first, 64)
        for pair in range(4):
            lanes = pair_lanes(pair)
            below = denom[pair, inner, :]
            attn[rows, lanes] = (numer[pair, inner, :] / below).astype(BF16)
            total[rows, lanes] = below

    row_loop(LEN, 64, join_step)
    for index in range(4):
        copy_out(index).wait()


def feed_kernel(plain, place, tokens, attn, total, cotangent, *refs):
    blocks, (output, middle_grad, numer_grad, total_grad), grads = refs[:8], refs[8:12], refs[12:16]
    w_out, w_up, w_down, vectors, middle, normed, inverse, normed_low = refs[16:24]
    hidden, result, gathered, active, back, sums, acc_out, acc_up, acc_down = refs[24:]

    @pl.when(pl.program_id(0) == 0)
    def _():
        acc_out[...] = jnp.zeros_like(acc_out)
        acc_up[...] = jnp.zeros_like(acc_up)
        acc_down[...] = jnp.zeros_like(acc_down)
        sums[...] = jnp.zeros_like(sums)
        load_second(place, plain, blocks, w_out, w_up, w_down, vectors)

    gain = vectors[0:1, :]
    shift = vectors[1:2, :]
    bias_down = vectors[2:3, :]
    middle[...] = nt(attn[...], w_out[...])

    def norm_step(first):
        rows = pl.ds(first, 64)
        values = middle[rows, :] + tokens[rows, :].astype(F32)
        middle[rows, :] = values
        norm, factor = layer_norm(values)
        normed[rows, :] = norm
        inverse[rows, :] = jnp.broadcast_to(factor, (64, 128))
        normed_low[rows, :] = (norm * gain + shift).astype(BF16)

    row_loop(LEN, 64, norm_step)
    gathered[...] = jnp.zeros_like(gathered)

    def part_step(part, carry):
        up = w_up[pl.ds(pl.multiple_of(part * D, D), D), :]
        down = w_down[part]
        bias_up = vectors[pl.ds(3 + part, 1), :]
        count = jnp.zeros((8, D), F32)
        for start in range(0, LEN, 512):
            wide = slice(start, start + 512)
            hidden[wide, :] = nt(normed_low[wide, :], up)
            result[wide, :] = nn(cotangent[wide, :], down)
            for first in range(start, start + 512, 64):
                rows = slice(first, first + 64)
                value = hidden[rows, :] + bias_up
                gate = 0.5 * jnp.tanh(0.5 * value) + 0.5
                active[rows, :] = (value * gate).astype(BF16)
                slope = gate * (1.0 + value * (1.0 - gate))
                gradient = (result[rows, :] * slope).astype(BF16)
                back[rows, :] = gradient
                count = count + jnp.sum(gradient.astype(F32).reshape(8, 8, D), axis=0)
        for start in range(0, LEN, 512):
            wide = slice(start, start + 512)
            middle[wide, :] += nt(active[wide, :], down)
            gathered[wide, :] += nn(back[wide, :], up)
        sums[pl.ds(pl.multiple_of(24 + 8 * part, 8), 8), :] += count
        acc_down[part] += tn(cotangent[...], active[...])
        acc_up[pl.ds(pl.multiple_of(part * D, D), D), :] += tn(back[...], normed_low[...])
        return carry

    lax.fori_loop(0, FF // D, part_step, 0)

    def back_step(first):
        rows = pl.ds(first, 64)
        output[rows, :] = (middle[rows, :] + bias_down).astype(BF16)
        gradient = gathered[rows, :]
        norm = normed[rows, :]
        value = cotangent[rows, :].astype(F32)
        sums[0:8, :] += jnp.sum((gradient * norm).reshape(8, 8, D), axis=0)
        sums[8:16, :] += jnp.sum(gradient.reshape(8, 8, D), axis=0)
        sums[16:24, :] += jnp.sum(value.reshape(8, 8, D), axis=0)
        value = value + norm_back(gradient, norm, inverse[rows, 0:1], gain)
        middle_grad[rows, :] = value.astype(BF16)

    row_loop(LEN, 64, back_step)
    acc_out[...] += tn(middle_grad[...], attn[...])
    gathered[...] = nn(middle_grad[...], w_out[...])

    def numer_step(first):
        rows = pl.ds(first, 64)
        gradient = gathered[rows, :].astype(BF16).astype(F32) / total[rows, :]
        numer_grad[rows, :] = gradient.astype(BF16)
        total_grad[rows, :] = (-gradient * attn[rows, :].astype(F32)).astype(BF16)

    row_loop(LEN, 64, numer_step)

    @pl.when(pl.program_id(0) == pl.num_programs(0) - 1)
    def _():
        small = jnp.sum(sums[...].reshape(7, 8, D), axis=1)
        small = jnp.concatenate([small, jnp.zeros((1, D), F32)], axis=0).astype(BF16)
        for half, block, device in block_places(place, plain, 1):
            target = grads[block // 4]
            into = 4 * half + block % 4
            target[into, 0:SHARE, :] = acc_out[sixteen(device), :].astype(BF16)
            target[into, SHARE : 5 * SHARE, :] = acc_up[sixty_four(device), :].astype(BF16)
            for part in range(4):
                at = (5 + part) * SHARE
                target[into, at : at + SHARE, :] = acc_down[part, sixteen(device), :].astype(BF16)
            target[into, 9 * SHARE : 9 * SHARE + 8, :] = small


def attend_back_kernel(
    plain,
    lengths,
    place,
    tokens,
    middle_grad,
    numer_grad,
    total_grad,
    query_in,
    key_in,
    value_in,
    probs_in,
    weights,
    vectors,
    pool,
    half,
    grad_tokens,
    near_grads,
    far_grads,
    numer,
    denom,
    score_grad,
    total,
    joined,
    normed,
    counts,
    top,
    sums,
    acc,
    query,
    key,
    value,
    probs,
    arrived,
):
    step_index = pl.program_id(0)
    last = pl.num_programs(0) - 1
    length = lengths[step_index]

    def copy_in(index, step):
        source = (value_in, probs_in, key_in, query_in)[index]
        target = (value, probs, key, query)[index]
        return pltpu.make_async_copy(source.at[step], target, arrived.at[index])

    following = jnp.minimum(step_index + 1, last)

    @pl.when(step_index == 0)
    def _():
        for index in range(4):
            copy_in(index, 0).start()
        acc[...] = jnp.zeros_like(acc)
        sums[...] = jnp.zeros_like(sums)

    gain = vectors[0:1, :]
    shift = vectors[1:2, :]
    clear_gaps(numer)
    clear_gaps(denom)
    fill_counts(counts, length)
    for source, target in ((numer_grad, numer), (total_grad, denom)):
        target[STARTS[0] : STARTS[0] + LEN, :] = source[...]
        for first in range(0, LEN, POOL_CHUNK):
            chunk = first // POOL_CHUNK
            pooled = nn(pool[...], source[first : first + POOL_CHUNK, :])
            at = 0
            for level in range(1, LEVELS):
                count = POOL_CHUNK >> level
                part = pooled[at : at + count] * float(1 << level)
                at += count
                if level < LEVELS - 1:
                    start = STARTS[level] + chunk * count
                    target[start : start + count, :] = part.astype(BF16)
                else:
                    top[chunk * count : chunk * count + count, :] = part
        target[STARTS[-1] : STARTS[-1] + SIZES[-1], :] = top[...].astype(BF16)

    def score_step(rows, near, flat, kind):
        number = counts[near, :]
        for pair in range(4):
            lanes = pair_lanes(pair)
            left = jnp.concatenate(
                [by_head(numer[rows, lanes], half), by_head(denom[rows, lanes], half)], axis=1
            )
            right = jnp.concatenate([value[near, lanes], number], axis=1)
            score_grad[flat, lanes] = (nt(left, right) * probs[flat, lanes].astype(F32)).astype(BF16)

    copy_in(0, step_index).wait()
    copy_in(1, step_index).wait()
    window_loop(score_step)
    copy_in(0, following).start()
    copy_in(2, step_index).wait()
    low_head = lax.broadcasted_iota(jnp.int32, (QUERIES, 128), 1) < DH

    def query_step(rows, near, flat, kind):
        for pair in range(4):
            lanes = pair_lanes(pair)
            both = nn(score_grad[flat, lanes], key[near, lanes])
            total[pair, rows, :] = joined_heads(both, low_head)

    window_loop(query_step)
    copy_in(2, following).start()
    copy_in(3, step_index).wait()
    spread_up(total, 0.5)

    def take(at, scale, masked):
        def take_step(first):
            rows = pl.ds(first, 64)
            if masked:
                place = lax.broadcasted_iota(jnp.int32, (64, 1), 0) + first
                valid = (place < length).astype(F32)
            for pair in range(4):
                values = total[pair, pl.ds(STARTS[0] + first, 64), :]
                if scale != 1.0:
                    values = values * scale
                if masked:
                    values = values * valid
                joined[rows, at + 128 * pair : at + 128 * pair + 128] = values.astype(BF16)

        row_loop(LEN, 64, take_step)

    take(0, 0.125, False)
    for at, left, right, factor, scale, masked, index in (
        (D, score_grad, query, 0.5, 0.125, False, 3),
        (2 * D, probs, numer, 1.0, 1.0, True, 1),
    ):
        total[...] = jnp.zeros_like(total)

        def near_step(rows, near, flat, kind, left=left, right=right):
            for pair in range(4):
                lanes = pair_lanes(pair)
                total[pair, near, :] += tn(left[flat, lanes], by_head(right[rows, lanes], half))

        window_loop(near_step)
        copy_in(index, following).start()
        spread_up(total, factor)
        take(at, scale, masked)

    def norm_step(first):
        rows = pl.ds(first, 64)
        values, _ = layer_norm(tokens[rows, :].astype(F32))
        normed[rows, :] = (values * gain + shift).astype(BF16)

    row_loop(LEN, 64, norm_step)
    for part in range(3):
        lanes = slice(D * part, D * part + D)
        acc[lanes, :] += tn(joined[:, lanes], normed[...])
    for first in range(0, LEN, POOL_CHUNK):
        rows = slice(first, first + POOL_CHUNK)
        passed = nn(joined[rows, :], weights[...])
        for pair in range(4):
            total[pair, rows, :] = passed[:, pair_lanes(pair)]

    def back_step(first):
        rows = pl.ds(first, 64)
        norm, inverse = layer_norm(tokens[rows, :].astype(F32))
        gradient = jnp.concatenate([total[pair, rows, :] for pair in range(4)], axis=1)
        sums[0:8, :] += jnp.sum((gradient * norm).reshape(8, 8, D), axis=0)
        sums[8:16, :] += jnp.sum(gradient.reshape(8, 8, D), axis=0)
        value = middle_grad[rows, :].astype(F32) + norm_back(gradient, norm, inverse, gain)
        grad_tokens[rows, :] = value.astype(BF16)

    row_loop(LEN, 64, back_step)

    @pl.when(step_index == last)
    def _():
        for index in range(4):
            copy_in(index, last).wait()
        small = jnp.sum(sums[...].reshape(2, 8, D), axis=1)
        small = jnp.concatenate([small, jnp.zeros((6, D), F32)], axis=0).astype(BF16)
        for side, block, device in block_places(place, plain, 1):
            target = (near_grads, far_grads)[side]
            for part in range(3):
                rows = pl.ds(pl.multiple_of(part * D + device * SHARE, SHARE), SHARE)
                target[block, part * SHARE : part * SHARE + SHARE, :] = acc[rows, :].astype(BF16)
            target[block, 3 * SHARE : 3 * SHARE + 8, :] = small


SMEM = pl.BlockSpec(memory_space=pltpu.SMEM)


def whole(*shape):
    return pl.BlockSpec(shape, lambda i: (0,) * len(shape), pipeline_mode=pl.Buffered(1))


def per_sequence(rows, columns):
    return pl.BlockSpec((rows, columns), lambda i: (i, 0))


def vmem(rows, columns, dtype):
    return pltpu.VMEM((rows, columns), dtype)


def shape_of(rows, columns, dtype):
    return jax.ShapeDtypeStruct((rows, columns), dtype)


PARAMS = pltpu.CompilerParams(
    dimension_semantics=("arbitrary",), vmem_limit_bytes=63 * 1024 * 1024
)


def cost(microseconds):
    return pl.CostEstimate(
        flops=int(microseconds * 1.0e9), bytes_accessed=int(microseconds * 1.0e6), transcendentals=0
    )


def attend(lengths, place, plain, tokens, blocks):
    count = lengths.shape[0]
    one = per_sequence(LEN, D)
    flat = WINDOWS * 2 * QUERIES
    return pl.pallas_call(
        functools.partial(attend_kernel, plain),
        grid=(count,),
        in_specs=[
            SMEM,
            SMEM,
            one,
            whole(16, FIRST_ROWS, D),
            whole(16, FIRST_ROWS, D),
            whole(2, 2 * QUERIES, KEYS),
            whole(POOL_CHUNK, POOL_CHUNK),
            whole(2, 128),
        ],
        out_specs=[pl.BlockSpec(memory_space=pl.ANY)] * 4
        + [one, one, whole(3 * D, D), whole(8, D)],
        out_shape=[jax.ShapeDtypeStruct((count, ROWS, D), BF16)] * 3
        + [
            jax.ShapeDtypeStruct((count, flat, D), BF16),
            shape_of(count * LEN, D, BF16),
            shape_of(count * LEN, D, F32),
            shape_of(3 * D, D, BF16),
            shape_of(8, D, F32),
        ],
        scratch_shapes=[vmem(ROWS, D, BF16)] * 3
        + [
            vmem(flat, D, BF16),
            vmem(LEN, D, BF16),
            vmem(LEN, 3 * D, BF16),
            vmem(SIZES[-1], 3 * D, F32),
            vmem(ROWS, 128, BF16),
            pltpu.VMEM((4, ROWS, 128), F32),
            pltpu.VMEM((4, ROWS, 128), F32),
            pltpu.SemaphoreType.DMA((4,)),
        ],
        compiler_params=PARAMS,
        cost_estimate=cost(40),
        name="attend",
    )(
        lengths,
        place,
        tokens,
        *blocks,
        jnp.asarray(score_bias()),
        jnp.asarray(pool_matrix(), BF16),
        jnp.asarray(halves(), BF16),
    )


def feed(place, plain, tokens, attn, total, cotangent, blocks):
    rows = tokens.shape[0]
    one = per_sequence(LEN, D)
    low = shape_of(rows, D, BF16)
    grads = whole(8, SECOND_ROWS, D)
    return pl.pallas_call(
        functools.partial(feed_kernel, plain),
        grid=(rows // LEN,),
        in_specs=[SMEM] + [one] * 4 + [whole(4, SECOND_ROWS, D)] * 8,
        out_specs=[one] * 4 + [grads] * 4,
        out_shape=[low] * 4 + [jax.ShapeDtypeStruct((8, SECOND_ROWS, D), BF16)] * 4,
        scratch_shapes=[
            vmem(D, D, BF16),
            vmem(FF, D, BF16),
            pltpu.VMEM((4, D, D), BF16),
            vmem(8, D, F32),
            vmem(LEN, D, F32),
            vmem(LEN, D, F32),
            vmem(LEN, 128, F32),
            vmem(LEN, D, BF16),
            vmem(LEN, D, F32),
            vmem(LEN, D, F32),
            vmem(LEN, D, F32),
            vmem(LEN, D, BF16),
            vmem(LEN, D, BF16),
            vmem(56, D, F32),
            vmem(D, D, F32),
            vmem(FF, D, F32),
            pltpu.VMEM((4, D, D), F32),
        ],
        compiler_params=PARAMS,
        cost_estimate=cost(75),
        name="feed",
    )(place, tokens, attn, total, cotangent, *blocks)


def attend_back(lengths, place, plain, tokens, middle_grad, numer_grad, total_grad, kept):
    count = lengths.shape[0]
    one = per_sequence(LEN, D)
    flat = WINDOWS * 2 * QUERIES
    grads = whole(16, FIRST_ROWS, D)
    return pl.pallas_call(
        functools.partial(attend_back_kernel, plain),
        grid=(count,),
        in_specs=[SMEM, SMEM]
        + [one] * 4
        + [pl.BlockSpec(memory_space=pl.ANY)] * 4
        + [whole(3 * D, D), whole(8, D), whole(POOL_CHUNK, POOL_CHUNK), whole(2, 128)],
        out_specs=[one, grads, grads],
        out_shape=[shape_of(count * LEN, D, BF16)]
        + [jax.ShapeDtypeStruct((16, FIRST_ROWS, D), BF16)] * 2,
        scratch_shapes=[
            vmem(ROWS, D, BF16),
            vmem(ROWS, D, BF16),
            vmem(flat, D, BF16),
            pltpu.VMEM((4, ROWS, 128), F32),
            vmem(LEN, 3 * D, BF16),
            vmem(LEN, D, BF16),
            vmem(ROWS, 128, BF16),
            vmem(SIZES[-1], D, F32),
            vmem(16, D, F32),
            vmem(3 * D, D, F32),
            vmem(ROWS, D, BF16),
            vmem(ROWS, D, BF16),
            vmem(ROWS, D, BF16),
            vmem(flat, D, BF16),
            pltpu.SemaphoreType.DMA((4,)),
        ],
        compiler_params=PARAMS,
        cost_estimate=cost(60),
        name="attend_back",
    )(
        lengths,
        place,
        tokens,
        middle_grad,
        numer_grad,
        total_grad,
        *kept,
        jnp.asarray(pool_matrix(), BF16),
        jnp.asarray(halves(), BF16),
    )


def pack_kernel(place, *refs):
    w_query, w_key, w_value, w_out, w_up, w_down, bias_up, bias_down, *norms, first, second = refs
    for part, ref in enumerate((w_query, w_key, w_value)):
        first[part * SHARE : part * SHARE + SHARE, :] = ref[...]
    second[0:SHARE, :] = w_out[...]
    second[SHARE : 5 * SHARE, :] = w_up[...]
    for part in range(4):
        at = (5 + part) * SHARE
        second[at : at + SHARE, :] = w_down[:, D * part : D * part + D]
    device = place[0] * 8 + place[1]
    lane = lax.broadcasted_iota(jnp.int32, (SHARE, D), 1)
    mine = lane == lax.broadcasted_iota(jnp.int32, (SHARE, D), 0) + device * SHARE
    mine = mine.astype(F32).astype(BF16)
    gain_attn, shift_attn, gain_ffn, shift_ffn = norms
    row = lax.broadcasted_iota(jnp.int32, (8, D), 0)

    def rows_of(vectors):
        total = jnp.zeros((8, D), F32)
        for place_of, vector in enumerate(vectors):
            total = jnp.where(row == place_of, nn(vector[...], mine), total)
        return total

    first[3 * SHARE :, :] = rows_of((gain_attn, shift_attn)).astype(BF16)
    lane = lax.broadcasted_iota(jnp.int32, (4 * SHARE, D), 1)
    mine_up = lane == lax.broadcasted_iota(jnp.int32, (4 * SHARE, D), 0) + (device % 8) * 4 * SHARE
    wide = nn(bias_up[...], mine_up.astype(F32).astype(BF16))
    vectors = rows_of((gain_ffn, shift_ffn, bias_down))
    second[9 * SHARE :, :] = jnp.where(row == 3 + device // 8, wide, vectors).astype(BF16)


def pack(place, weights, vectors):
    operands = [w.T for w in weights] + [v.reshape(1, -1) for v in vectors]
    return pl.pallas_call(
        pack_kernel,
        in_specs=[SMEM] + [pl.BlockSpec(memory_space=pltpu.VMEM)] * len(operands),
        out_specs=[pl.BlockSpec(memory_space=pltpu.VMEM)] * 2,
        out_shape=[shape_of(FIRST_ROWS, D, BF16), shape_of(SECOND_ROWS, D, BF16)],
        cost_estimate=cost(2),
        name="pack",
    )(place, *operands)


def across(values, bits):
    return lax.ppermute(values, "fsdp", [(i, i ^ bits) for i in range(8)])


def along(values, step):
    return lax.ppermute(values, "dp", [(i, (i + step) % 4) for i in range(4)])


def gather_rows(packed):
    return jnp.stack([packed] + [along(packed, step) for step in (1, 2, 3)])


def shares_along(blocks):
    return [blocks[0]] + [along(blocks[step], step) for step in (1, 2, 3)]


def added(parts):
    return sum(part.astype(F32) for part in parts)


def spread(vector, index, devices):
    share = vector.shape[0]
    full = jnp.tile(vector, devices)
    mine = lax.broadcasted_iota(jnp.int32, full.shape, 0) // share == index
    return jnp.where(mine, full, jnp.zeros_like(full)).reshape(-1, D)


def finish_kernel(place, *refs):
    first, second, outs = refs[:4], refs[4:8], refs[8:]
    query, key, value, out, up, down, bias_up, bias_down, *norms = outs

    def summed(parts, rows):
        return sum(part[rows, :].astype(F32) for part in parts)

    for place_of, ref in enumerate((query, key, value)):
        ref[...] = summed(first, slice(place_of * SHARE, place_of * SHARE + SHARE))
    out[...] = summed(second, slice(0, SHARE))
    up[...] = summed(second, slice(SHARE, 5 * SHARE))
    for part in range(4):
        at = (5 + part) * SHARE
        down[:, D * part : D * part + D] = summed(second, slice(at, at + SHARE))
    device = place[0] * 8 + place[1]
    shift = lax.rem(D - device * SHARE, D)
    mine_first = pltpu.roll(summed(first, slice(3 * SHARE, FIRST_ROWS)), shift, 1)
    vectors = summed(second, slice(9 * SHARE, SECOND_ROWS))
    mine_second = pltpu.roll(vectors, shift, 1)
    row = lax.broadcasted_iota(jnp.int32, (8, D), 0)
    wide = jnp.sum(jnp.where(row == 3 + device // 8, vectors, 0.0), axis=0, keepdims=True)
    wide = pltpu.roll(jnp.broadcast_to(wide, (8, D)), lax.rem(D - (device % 8) * 4 * SHARE, D), 1)
    bias_up[...] = wide[0:1, : 4 * SHARE]
    bias_down[...] = mine_second[2:3, :SHARE]
    gain_attn, shift_attn, gain_ffn, shift_ffn = norms
    gain_attn[...] = mine_first[0:1, :SHARE]
    shift_attn[...] = mine_first[1:2, :SHARE]
    gain_ffn[...] = mine_second[0:1, :SHARE]
    shift_ffn[...] = mine_second[1:2, :SHARE]


def finish(place, first, second):
    shapes = [(SHARE, D)] * 4 + [(4 * SHARE, D), (SHARE, FF), (1, 4 * SHARE)] + [(1, SHARE)] * 5
    grads = pl.pallas_call(
        finish_kernel,
        in_specs=[SMEM] + [pl.BlockSpec(memory_space=pltpu.VMEM)] * 8,
        out_specs=[pl.BlockSpec(memory_space=pltpu.VMEM)] * 12,
        out_shape=[shape_of(rows, columns, F32) for rows, columns in shapes],
        cost_estimate=cost(2),
        name="finish",
    )(place, *first, *second)
    return [grad.T for grad in grads[:6]] + [grad.reshape(-1) for grad in grads[6:]]


def exchange_permutes(place, tokens, lengths, weights, vectors, cotangent):
    first, second = pack(place, weights, vectors)
    rows = gather_rows(first)
    near = jnp.concatenate([rows] + [across(rows, bits) for bits in (2, 4, 6)])
    second_rows = gather_rows(second)
    near, second_rows = lax.optimization_barrier((near, second_rows))
    first_blocks = (near, across(near, 1))
    first_blocks, second_rows = lax.optimization_barrier((first_blocks, second_rows))
    others = [across(second_rows, bits) for bits in (2, 4, 6)] + [across(second_rows, 1)]
    *kept, attn, total, weights, gains = attend(lengths, place, False, tokens, first_blocks)
    kept += [weights, gains]
    attn, total, others = lax.optimization_barrier((attn, total, others))
    *others, partner = others
    second_blocks = [second_rows, *others, partner] + [across(other, 1) for other in others]
    output, middle_grad, numer_grad, total_grad, *parts = feed(
        place, False, tokens, attn, total, cotangent, second_blocks
    )
    others = [across(parts[chip], bits) for chip, bits in ((1, 2), (2, 4), (3, 6))]
    grad_tokens, near, far = attend_back(
        lengths, place, False, tokens, middle_grad, numer_grad, total_grad, kept
    )
    partner = across(far, 1)
    near, partner, others = lax.optimization_barrier((near, partner, others))
    second = added([parts[0]] + others).astype(BF16)
    second = added([second[:4], across(second[4:], 1)]).astype(BF16)
    first = added([near, partner]).astype(BF16).reshape(4, 4, FIRST_ROWS, D)
    by_x, by_y = first[:, :2], first[:, 2:]
    sent_x = across(jnp.stack([by_x[1], by_x[3]]), 2)
    sent_y = across(jnp.stack([by_y[2], by_y[3]]), 4)
    by_x = added([jnp.stack([by_x[0], by_x[2]]), sent_x]).astype(BF16)
    by_y = added([jnp.stack([by_y[0], by_y[1]]), sent_y]).astype(BF16)
    by_x = added([by_x[0], across(by_x[1], 4)]).astype(BF16)
    by_y = added([by_y[0], across(by_y[1], 2)]).astype(BF16)
    first = shares_along([by_x[0], by_x[1], by_y[0], by_y[1]])
    second = shares_along(second)
    return output, grad_tokens, finish(place, first, second)


def exchange_plain(index, devices, tokens, lengths, weights, vectors, cotangent):
    w_query, w_key, w_value, w_out, w_up, w_down = weights
    bias_up, bias_down, gain_attn, shift_attn, gain_ffn, shift_ffn = vectors
    share = D // devices

    def gathered(rows):
        return lax.all_gather(rows, AXES, axis=0, tiled=True).reshape(32, SHARE, D)

    def vector_rows(parts):
        rows = jnp.concatenate([spread(part, index, devices) for part in parts])
        rows = lax.psum(rows, AXES)
        pad = jnp.zeros((8 - rows.shape[0], D), rows.dtype)
        rows = jnp.concatenate([rows, pad])[None]
        return jnp.concatenate([rows, jnp.zeros((31, 8, D), rows.dtype)])

    def halved(parts):
        blocks = jnp.concatenate(parts, axis=1)
        return blocks[:16], blocks[16:]

    place = jnp.zeros((2,), jnp.int32)
    first_blocks = halved(
        [gathered(w.T) for w in (w_query, w_key, w_value)]
        + [vector_rows([gain_attn, shift_attn])]
    )
    up = lax.all_gather(w_up.T, AXES, axis=0, tiled=True).reshape(32, 4 * SHARE, D)
    down = lax.all_gather(w_down.T, AXES, axis=0, tiled=True).reshape(32, SHARE, 4, D)
    down = jnp.transpose(down, (0, 2, 1, 3)).reshape(32, 4 * SHARE, D)
    vectors = vector_rows([gain_ffn, shift_ffn, bias_down, bias_up])
    second_blocks = jnp.concatenate([gathered(w_out.T), up, down, vectors], axis=1)
    second_blocks = [second_blocks[at : at + 4] for at in range(0, 32, 4)]
    *kept, attn, total, weights, gains = attend(lengths, place, True, tokens, first_blocks)
    kept += [weights, gains]
    output, middle_grad, numer_grad, total_grad, *parts = feed(
        place, True, tokens, attn, total, cotangent, second_blocks
    )
    second = jnp.stack(parts).reshape(4, 2, 4, SECOND_ROWS, D)
    second = jnp.transpose(second, (1, 0, 2, 3, 4)).reshape(32, SECOND_ROWS, D)
    grad_tokens, near, far = attend_back(
        lengths, place, True, tokens, middle_grad, numer_grad, total_grad, kept
    )
    first = jnp.concatenate([near, far])

    def scattered(rows):
        rows = rows.reshape(devices, -1, D)
        return lax.psum_scatter(rows, AXES, scatter_dimension=0, tiled=False).astype(F32)

    down = second[:, 5 * SHARE : 9 * SHARE].reshape(32, 4, SHARE, D)
    down = scattered(jnp.transpose(down, (0, 2, 1, 3)).reshape(32, 4 * SHARE, D))
    down = jnp.transpose(down.reshape(share, 4, D), (1, 0, 2)).reshape(4 * share, D)
    first_vectors = lax.psum(first[0, 3 * SHARE :].astype(F32), AXES)
    second_vectors = lax.psum(second[0, 9 * SHARE :].astype(F32), AXES)
    down = jnp.transpose(down.reshape(4, share, D), (0, 2, 1)).reshape(FF, share)

    def own(row):
        return lax.dynamic_slice(row, (index * share,), (share,))

    return (
        output,
        grad_tokens,
        [
            *[scattered(first[:, p * SHARE : p * SHARE + SHARE]).T for p in range(3)],
            scattered(second[:, :SHARE]).T,
            scattered(second[:, SHARE : 5 * SHARE]).T,
            down,
            lax.dynamic_slice(second_vectors[3:7].reshape(FF), (index * 4 * share,), (4 * share,)),
            own(second_vectors[2]),
            own(first_vectors[0]),
            own(first_vectors[1]),
            own(second_vectors[0]),
            own(second_vectors[1]),
        ],
    )


def on_device(sizes, tokens, lengths, *rest):
    weights, vectors, cotangent = rest[:6], rest[6:12], rest[12]
    if sizes == (4, 8):
        place = jnp.stack([lax.axis_index("dp"), lax.axis_index("fsdp")]).astype(jnp.int32)
        output, grad_tokens, grads = exchange_permutes(
            place, tokens, lengths, weights, vectors, cotangent
        )
    else:
        index = lax.axis_index(AXES)
        output, grad_tokens, grads = exchange_plain(
            index, sizes[0] * sizes[1], tokens, lengths, weights, vectors, cotangent
        )
    return (output, grad_tokens, *grads)


def solution(mesh):
    rows = P(AXES, None)
    columns = P(None, AXES)
    vector = P(AXES)
    sizes = (mesh.shape["dp"], mesh.shape["fsdp"])
    return jax.shard_map(
        functools.partial(on_device, sizes),
        mesh=mesh,
        in_specs=(rows, vector) + (columns,) * 6 + (vector,) * 6 + (rows,),
        out_specs=(rows, rows) + (columns,) * 6 + (vector,) * 6,
        check_vma=False,
    )
```

```python
import functools

import jax
import jax.numpy as jnp
import numpy as np
from jax import lax
from jax.experimental import pallas as pl
from jax.experimental.pallas import tpu as pltpu
from jax.sharding import PartitionSpec as P

D = 512
H = 8
DH = 64
FF = 2048
BLOCK = 16
LEVELS = 6
LEN = 1024
AXES = ("dp", "fsdp")
BF16 = jnp.bfloat16
F32 = jnp.float32

STARTS = (32, 1072, 1600, 1872, 2016, 2096)
SIZES = tuple(LEN >> level for level in range(LEVELS))
ROWS = 2192
GAPS = ((0, 32), (1056, 16), (1584, 16), (1856, 16), (2000, 16), (2080, 16), (2128, 64))
WINDOWS = 32
QUERIES = 64
KEYS = 128
POOL_CHUNK = 256
SHARE = 16
FIRST_ROWS = 3 * SHARE + 8
SECOND_ROWS = 9 * SHARE + 8
SCORE = 0.125 * 1.4426950408889634


def nn(left, right):
    return lax.dot_general(left, right, (((1,), (0,)), ((), ())), preferred_element_type=F32)


def nt(left, right):
    return lax.dot_general(left, right, (((1,), (1,)), ((), ())), preferred_element_type=F32)


def tn(left, right):
    return lax.dot_general(left, right, (((0,), (0,)), ((), ())), preferred_element_type=F32)


def score_bias():
    query = (np.arange(2 * QUERIES) % QUERIES)[:, None]
    key = np.arange(KEYS)[None, :] - 32
    near = np.abs(query // 16 - key // 16) <= 1
    apart = np.abs(query // 8 - key // 8) > 1
    return np.where(np.stack([near, near & apart]), 0.0, -1e30).astype(np.float32)


def pool_matrix():
    matrix = np.zeros((POOL_CHUNK, POOL_CHUNK), np.float32)
    first = 0
    for level in range(1, LEVELS):
        count = POOL_CHUNK >> level
        for row in range(count):
            matrix[first + row, row << level : (row + 1) << level] = 0.5**level
        first += count
    return matrix


def halves():
    lane = np.arange(128)
    return np.stack([lane < DH, lane >= DH]).astype(np.float32)


def window_loop(step):
    for window in range(WINDOWS):
        gaps = sum(window >= first for first in (16, 24, 28, 30, 31))
        row = STARTS[0] + QUERIES * window + 16 * gaps
        step(
            pl.ds(row, QUERIES),
            pl.ds(row - 32, KEYS),
            pl.ds(window * 2 * QUERIES, 2 * QUERIES),
            int(window >= 16),
        )


def row_loop(total, size, step):
    for first in range(0, total, size):
        step(first)


def row_fori(total, size, step, unroll):
    def body(index, carry):
        for inner in range(unroll):
            step(pl.multiple_of((index * unroll + inner) * size, size))
        return carry

    lax.fori_loop(0, total // (size * unroll), body, 0)


def pair_lanes(pair):
    return slice(128 * pair, 128 * pair + 128)


def by_head(values, half):
    return jnp.concatenate([values * half[0:1, :], values * half[1:2, :]], axis=0)


def joined_heads(values, low_head):
    return jnp.where(low_head, values[:QUERIES], values[QUERIES:])


def fill_counts(counts, length):
    clear_gaps(counts)
    for level in range(LEVELS):
        place = lax.broadcasted_iota(jnp.int32, (SIZES[level], 128), 0)
        span = 1 << level
        number = jnp.clip(length - place * span, 0, span).astype(F32)
        counts[STARTS[level] : STARTS[level] + SIZES[level], :] = number.astype(BF16)


def block_places(place, plain, sign):
    for half in range(2):
        for block in range(16):
            if plain:
                yield half, block, half * 16 + block
            else:
                column = place[1] ^ (half + 2 * (block // 4))
                row = (place[0] + 4 + sign * (block % 4)) % 4
                yield half, block, row * 8 + column


def sixteen(device):
    return pl.ds(pl.multiple_of(device * SHARE, SHARE), SHARE)


def sixty_four(device):
    return pl.ds(pl.multiple_of(device * 4 * SHARE, 4 * SHARE), 4 * SHARE)


def load_first(place, plain, blocks, weights, vectors):
    total = jnp.zeros((8, D), F32)
    for half, block, device in block_places(place, plain, -1):
        source = blocks[half]
        for part in range(3):
            rows = pl.ds(pl.multiple_of(part * D + device * SHARE, SHARE), SHARE)
            weights[rows, :] = source[block, part * SHARE : part * SHARE + SHARE, :]
        total = total + source[block, 3 * SHARE : 3 * SHARE + 8, :].astype(F32)
    vectors[...] = total


def load_second(place, plain, blocks, w_out, w_up, w_down, vectors):
    total = jnp.zeros((8, D), F32)
    for half, block, device in block_places(place, plain, -1):
        source = blocks[4 * half + block // 4].at[block % 4]
        w_out[sixteen(device), :] = source[0:SHARE, :]
        w_up[sixty_four(device), :] = source[SHARE : 5 * SHARE, :]
        for part in range(4):
            at = (5 + part) * SHARE
            w_down[part, sixteen(device), :] = source[at : at + SHARE, :]
        total = total + source[9 * SHARE : 9 * SHARE + 8, :].astype(F32)
    vectors[...] = total


def layer_norm(values):
    mean = jnp.mean(values, axis=-1, keepdims=True)
    centred = values - mean
    inverse = lax.rsqrt(jnp.mean(centred * centred, axis=-1, keepdims=True) + 1e-05)
    return centred * inverse, inverse


def norm_back(gradient, normed, inverse, gain):
    scaled = gradient * gain
    return inverse * (
        scaled
        - jnp.mean(scaled, axis=-1, keepdims=True)
        - normed * jnp.mean(scaled * normed, axis=-1, keepdims=True)
    )


def clear_gaps(ref):
    for first, count in GAPS:
        ref[first : first + count, :] = jnp.zeros((count, ref.shape[1]), ref.dtype)


def spread_up(ref, factor):
    for level in range(LEVELS - 2, -1, -1):
        count = SIZES[level + 1]
        size = min(count, 64)

        def step(first, level=level, size=size):
            for pair in range(4):
                above = ref[pair, pl.ds(STARTS[level + 1] + first, size), :]
                if factor != 1.0:
                    above = above * factor
                for odd in (0, 1):
                    below = pl.ds(STARTS[level] + 2 * first + odd, size, stride=2)
                    ref[pair, below, :] = ref[pair, below, :] + above

        row_loop(count, size, step)


def attend_kernel(
    plain,
    lengths,
    place,
    tokens,
    near_blocks,
    far_blocks,
    bias,
    pool,
    half,
    query_out,
    key_out,
    value_out,
    probs_out,
    attn,
    total,
    weights,
    vectors,
    query,
    key,
    value,
    probs,
    normed,
    joined,
    top,
    counts,
    numer,
    denom,
    done,
):
    def copy_out(index):
        source = (query, key, value, probs)[index]
        target = (query_out, key_out, value_out, probs_out)[index]
        return pltpu.make_async_copy(source, target.at[pl.program_id(0)], done.at[index])

    @pl.when(pl.program_id(0) == 0)
    def _():
        load_first(place, plain, (near_blocks, far_blocks), weights, vectors)

    length = lengths[pl.program_id(0)]
    gain = vectors[0:1, :]
    shift = vectors[1:2, :]

    def norm_step(first):
        rows = pl.ds(first, 64)
        values, _ = layer_norm(tokens[rows, :].astype(F32))
        normed[rows, :] = (values * gain + shift).astype(BF16)

    row_loop(LEN, 64, norm_step)
    for ref in (query, key, value):
        clear_gaps(ref)
    fill_counts(counts, length)
    targets = ((query, 0), (key, D), (value, 2 * D))
    for first in range(0, LEN, POOL_CHUNK):
        rows = slice(first, first + POOL_CHUNK)
        chunk = first // POOL_CHUNK
        values = nt(normed[rows, :], weights[...])
        valid = (lax.broadcasted_iota(jnp.int32, (POOL_CHUNK, 1), 0) + first < length).astype(F32)
        joined[rows, : 2 * D] = values[:, : 2 * D].astype(BF16)
        joined[rows, 2 * D :] = (values[:, 2 * D :] * valid).astype(BF16)
        pooled = nn(pool[...], joined[rows, :])
        for ref, lane in targets:
            start = STARTS[0] + first
            ref[start : start + POOL_CHUNK, :] = joined[rows, lane : lane + D]
            at = 0
            for level in range(1, LEVELS):
                count = POOL_CHUNK >> level
                part = pooled[at : at + count, lane : lane + D]
                at += count
                if ref is value:
                    part = part * float(1 << level)
                if level < LEVELS - 1:
                    start = STARTS[level] + chunk * count
                    ref[start : start + count, :] = part.astype(BF16)
                else:
                    top[chunk * count : chunk * count + count, lane : lane + D] = part
    for ref, lane in targets:
        ref[STARTS[-1] : STARTS[-1] + SIZES[-1], :] = top[:, lane : lane + D].astype(BF16)
    for index in range(3):
        copy_out(index).start()

    def score_step(rows, near, flat, kind):
        allowed = bias[kind]
        for pair in range(4):
            lanes = pair_lanes(pair)
            scores = nt(by_head(query[rows, lanes], half), key[near, lanes])
            probs[flat, lanes] = jnp.exp2(scores * SCORE + allowed).astype(BF16)

    window_loop(score_step)
    copy_out(3).start()
    low_head = lax.broadcasted_iota(jnp.int32, (QUERIES, 128), 1) < DH

    def value_step(rows, near, flat, kind):
        number = counts[near, :]
        for pair in range(4):
            lanes = pair_lanes(pair)
            both = nn(probs[flat, lanes], jnp.concatenate([value[near, lanes], number], axis=1))
            numer[pair, rows, :] = joined_heads(both[:, :128], low_head)
            denom[pair, rows, :] = joined_heads(both[:, 128:], low_head)

    window_loop(value_step)
    spread_up(numer, 1.0)
    spread_up(denom, 1.0)

    def join_step(first):
        rows = pl.ds(first, 64)
        inner = pl.ds(STARTS[0] + first, 64)
        for pair in range(4):
            lanes = pair_lanes(pair)
            below = denom[pair, inner, :]
            attn[rows, lanes] = (numer[pair, inner, :] / below).astype(BF16)
            total[rows, lanes] = below

    row_loop(LEN, 64, join_step)
    for index in range(4):
        copy_out(index).wait()


def feed_kernel(plain, place, tokens, attn, total, cotangent, *refs):
    blocks, (output, middle_grad, numer_grad, total_grad), grads = refs[:8], refs[8:12], refs[12:16]
    w_out, w_up, w_down, vectors, middle, normed, inverse, normed_low = refs[16:24]
    hidden, result, gathered, active, back, sums, acc_out, acc_up, acc_down = refs[24:]

    @pl.when(pl.program_id(0) == 0)
    def _():
        acc_out[...] = jnp.zeros_like(acc_out)
        acc_up[...] = jnp.zeros_like(acc_up)
        acc_down[...] = jnp.zeros_like(acc_down)
        sums[...] = jnp.zeros_like(sums)
        load_second(place, plain, blocks, w_out, w_up, w_down, vectors)

    gain = vectors[0:1, :]
    shift = vectors[1:2, :]
    bias_down = vectors[2:3, :]
    middle[...] = nt(attn[...], w_out[...])

    def norm_step(first):
        rows = pl.ds(first, 64)
        values = middle[rows, :] + tokens[rows, :].astype(F32)
        middle[rows, :] = values
        norm, factor = layer_norm(values)
        normed[rows, :] = norm
        inverse[rows, :] = jnp.broadcast_to(factor, (64, 128))
        normed_low[rows, :] = (norm * gain + shift).astype(BF16)

    row_loop(LEN, 64, norm_step)
    gathered[...] = jnp.zeros_like(gathered)

    def part_step(part, carry):
        up = w_up[pl.ds(pl.multiple_of(part * D, D), D), :]
        down = w_down[part]
        bias_up = vectors[pl.ds(3 + part, 1), :]
        count = jnp.zeros((8, D), F32)
        for start in range(0, LEN, 512):
            wide = slice(start, start + 512)
            hidden[wide, :] = nt(normed_low[wide, :], up)
            result[wide, :] = nn(cotangent[wide, :], down)
            for first in range(start, start + 512, 64):
                rows = slice(first, first + 64)
                value = hidden[rows, :] + bias_up
                gate = 0.5 * jnp.tanh(0.5 * value) + 0.5
                active[rows, :] = (value * gate).astype(BF16)
                slope = gate * (1.0 + value * (1.0 - gate))
                gradient = (result[rows, :] * slope).astype(BF16)
                back[rows, :] = gradient
                count = count + jnp.sum(gradient.astype(F32).reshape(8, 8, D), axis=0)
        for start in range(0, LEN, 512):
            wide = slice(start, start + 512)
            middle[wide, :] += nt(active[wide, :], down)
            gathered[wide, :] += nn(back[wide, :], up)
        sums[pl.ds(pl.multiple_of(24 + 8 * part, 8), 8), :] += count
        acc_down[part] += tn(cotangent[...], active[...])
        acc_up[pl.ds(pl.multiple_of(part * D, D), D), :] += tn(back[...], normed_low[...])
        return carry

    lax.fori_loop(0, FF // D, part_step, 0)

    def back_step(first):
        rows = pl.ds(first, 64)
        output[rows, :] = (middle[rows, :] + bias_down).astype(BF16)
        gradient = gathered[rows, :]
        norm = normed[rows, :]
        value = cotangent[rows, :].astype(F32)
        sums[0:8, :] += jnp.sum((gradient * norm).reshape(8, 8, D), axis=0)
        sums[8:16, :] += jnp.sum(gradient.reshape(8, 8, D), axis=0)
        sums[16:24, :] += jnp.sum(value.reshape(8, 8, D), axis=0)
        value = value + norm_back(gradient, norm, inverse[rows, 0:1], gain)
        middle_grad[rows, :] = value.astype(BF16)

    row_loop(LEN, 64, back_step)
    acc_out[...] += tn(middle_grad[...], attn[...])
    gathered[...] = nn(middle_grad[...], w_out[...])

    def numer_step(first):
        rows = pl.ds(first, 64)
        gradient = gathered[rows, :].astype(BF16).astype(F32) / total[rows, :]
        numer_grad[rows, :] = gradient.astype(BF16)
        total_grad[rows, :] = (-gradient * attn[rows, :].astype(F32)).astype(BF16)

    row_loop(LEN, 64, numer_step)

    @pl.when(pl.program_id(0) == pl.num_programs(0) - 1)
    def _():
        small = jnp.sum(sums[...].reshape(7, 8, D), axis=1)
        small = jnp.concatenate([small, jnp.zeros((1, D), F32)], axis=0).astype(BF16)
        for half, block, device in block_places(place, plain, 1):
            target = grads[block // 4]
            into = 4 * half + block % 4
            target[into, 0:SHARE, :] = acc_out[sixteen(device), :].astype(BF16)
            target[into, SHARE : 5 * SHARE, :] = acc_up[sixty_four(device), :].astype(BF16)
            for part in range(4):
                at = (5 + part) * SHARE
                target[into, at : at + SHARE, :] = acc_down[part, sixteen(device), :].astype(BF16)
            target[into, 9 * SHARE : 9 * SHARE + 8, :] = small


def attend_back_kernel(
    plain,
    lengths,
    place,
    tokens,
    middle_grad,
    numer_grad,
    total_grad,
    query_in,
    key_in,
    value_in,
    probs_in,
    weights,
    vectors,
    pool,
    half,
    grad_tokens,
    near_grads,
    far_grads,
    numer,
    denom,
    score_grad,
    total,
    joined,
    normed,
    counts,
    top,
    sums,
    acc,
    query,
    key,
    value,
    probs,
    arrived,
):
    step_index = pl.program_id(0)
    last = pl.num_programs(0) - 1
    length = lengths[step_index]

    def copy_in(index, step):
        source = (value_in, probs_in, key_in, query_in)[index]
        target = (value, probs, key, query)[index]
        return pltpu.make_async_copy(source.at[step], target, arrived.at[index])

    following = jnp.minimum(step_index + 1, last)

    @pl.when(step_index == 0)
    def _():
        for index in range(4):
            copy_in(index, 0).start()
        acc[...] = jnp.zeros_like(acc)
        sums[...] = jnp.zeros_like(sums)

    gain = vectors[0:1, :]
    shift = vectors[1:2, :]
    clear_gaps(numer)
    clear_gaps(denom)
    fill_counts(counts, length)
    for source, target in ((numer_grad, numer), (total_grad, denom)):
        target[STARTS[0] : STARTS[0] + LEN, :] = source[...]
        for first in range(0, LEN, POOL_CHUNK):
            chunk = first // POOL_CHUNK
            pooled = nn(pool[...], source[first : first + POOL_CHUNK, :])
            at = 0
            for level in range(1, LEVELS):
                count = POOL_CHUNK >> level
                part = pooled[at : at + count] * float(1 << level)
                at += count
                if level < LEVELS - 1:
                    start = STARTS[level] + chunk * count
                    target[start : start + count, :] = part.astype(BF16)
                else:
                    top[chunk * count : chunk * count + count, :] = part
        target[STARTS[-1] : STARTS[-1] + SIZES[-1], :] = top[...].astype(BF16)

    def score_step(rows, near, flat, kind):
        number = counts[near, :]
        for pair in range(4):
            lanes = pair_lanes(pair)
            left = jnp.concatenate(
                [by_head(numer[rows, lanes], half), by_head(denom[rows, lanes], half)], axis=1
            )
            right = jnp.concatenate([value[near, lanes], number], axis=1)
            score_grad[flat, lanes] = (nt(left, right) * probs[flat, lanes].astype(F32)).astype(BF16)

    copy_in(0, step_index).wait()
    copy_in(1, step_index).wait()
    window_loop(score_step)
    copy_in(0, following).start()
    copy_in(2, step_index).wait()
    low_head = lax.broadcasted_iota(jnp.int32, (QUERIES, 128), 1) < DH

    def query_step(rows, near, flat, kind):
        for pair in range(4):
            lanes = pair_lanes(pair)
            both = nn(score_grad[flat, lanes], key[near, lanes])
            total[pair, rows, :] = joined_heads(both, low_head)

    window_loop(query_step)
    copy_in(2, following).start()
    copy_in(3, step_index).wait()
    spread_up(total, 0.5)

    def take(at, scale, masked):
        def take_step(first):
            rows = pl.ds(first, 64)
            if masked:
                place = lax.broadcasted_iota(jnp.int32, (64, 1), 0) + first
                valid = (place < length).astype(F32)
            for pair in range(4):
                values = total[pair, pl.ds(STARTS[0] + first, 64), :]
                if scale != 1.0:
                    values = values * scale
                if masked:
                    values = values * valid
                joined[rows, at + 128 * pair : at + 128 * pair + 128] = values.astype(BF16)

        row_loop(LEN, 64, take_step)

    take(0, 0.125, False)
    for at, left, right, factor, scale, masked, index in (
        (D, score_grad, query, 0.5, 0.125, False, 3),
        (2 * D, probs, numer, 1.0, 1.0, True, 1),
    ):
        total[...] = jnp.zeros_like(total)

        def near_step(rows, near, flat, kind, left=left, right=right):
            for pair in range(4):
                lanes = pair_lanes(pair)
                total[pair, near, :] += tn(left[flat, lanes], by_head(right[rows, lanes], half))

        window_loop(near_step)
        copy_in(index, following).start()
        spread_up(total, factor)
        take(at, scale, masked)

    def norm_step(first):
        rows = pl.ds(first, 64)
        values, _ = layer_norm(tokens[rows, :].astype(F32))
        normed[rows, :] = (values * gain + shift).astype(BF16)

    row_loop(LEN, 64, norm_step)
    for part in range(3):
        lanes = slice(D * part, D * part + D)
        acc[lanes, :] += tn(joined[:, lanes], normed[...])
    for first in range(0, LEN, POOL_CHUNK):
        rows = slice(first, first + POOL_CHUNK)
        passed = nn(joined[rows, :], weights[...])
        for pair in range(4):
            total[pair, rows, :] = passed[:, pair_lanes(pair)]

    def back_step(first):
        rows = pl.ds(first, 64)
        norm, inverse = layer_norm(tokens[rows, :].astype(F32))
        gradient = jnp.concatenate([total[pair, rows, :] for pair in range(4)], axis=1)
        sums[0:8, :] += jnp.sum((gradient * norm).reshape(8, 8, D), axis=0)
        sums[8:16, :] += jnp.sum(gradient.reshape(8, 8, D), axis=0)
        value = middle_grad[rows, :].astype(F32) + norm_back(gradient, norm, inverse, gain)
        grad_tokens[rows, :] = value.astype(BF16)

    row_loop(LEN, 64, back_step)

    @pl.when(step_index == last)
    def _():
        for index in range(4):
            copy_in(index, last).wait()
        small = jnp.sum(sums[...].reshape(2, 8, D), axis=1)
        small = jnp.concatenate([small, jnp.zeros((6, D), F32)], axis=0).astype(BF16)
        for side, block, device in block_places(place, plain, 1):
            target = (near_grads, far_grads)[side]
            for part in range(3):
                rows = pl.ds(pl.multiple_of(part * D + device * SHARE, SHARE), SHARE)
                target[block, part * SHARE : part * SHARE + SHARE, :] = acc[rows, :].astype(BF16)
            target[block, 3 * SHARE : 3 * SHARE + 8, :] = small


SMEM = pl.BlockSpec(memory_space=pltpu.SMEM)


def whole(*shape):
    return pl.BlockSpec(shape, lambda i: (0,) * len(shape), pipeline_mode=pl.Buffered(1))


def per_sequence(rows, columns):
    return pl.BlockSpec((rows, columns), lambda i: (i, 0))


def vmem(rows, columns, dtype):
    return pltpu.VMEM((rows, columns), dtype)


def shape_of(rows, columns, dtype):
    return jax.ShapeDtypeStruct((rows, columns), dtype)


PARAMS = pltpu.CompilerParams(
    dimension_semantics=("arbitrary",), vmem_limit_bytes=63 * 1024 * 1024
)


def cost(microseconds):
    return pl.CostEstimate(
        flops=int(microseconds * 1.0e9), bytes_accessed=int(microseconds * 1.0e6), transcendentals=0
    )


def attend(lengths, place, plain, tokens, blocks):
    count = lengths.shape[0]
    one = per_sequence(LEN, D)
    flat = WINDOWS * 2 * QUERIES
    return pl.pallas_call(
        functools.partial(attend_kernel, plain),
        grid=(count,),
        in_specs=[
            SMEM,
            SMEM,
            one,
            whole(16, FIRST_ROWS, D),
            whole(16, FIRST_ROWS, D),
            whole(2, 2 * QUERIES, KEYS),
            whole(POOL_CHUNK, POOL_CHUNK),
            whole(2, 128),
        ],
        out_specs=[pl.BlockSpec(memory_space=pl.ANY)] * 4
        + [one, one, whole(3 * D, D), whole(8, D)],
        out_shape=[jax.ShapeDtypeStruct((count, ROWS, D), BF16)] * 3
        + [
            jax.ShapeDtypeStruct((count, flat, D), BF16),
            shape_of(count * LEN, D, BF16),
            shape_of(count * LEN, D, F32),
            shape_of(3 * D, D, BF16),
            shape_of(8, D, F32),
        ],
        scratch_shapes=[vmem(ROWS, D, BF16)] * 3
        + [
            vmem(flat, D, BF16),
            vmem(LEN, D, BF16),
            vmem(LEN, 3 * D, BF16),
            vmem(SIZES[-1], 3 * D, F32),
            vmem(ROWS, 128, BF16),
            pltpu.VMEM((4, ROWS, 128), F32),
            pltpu.VMEM((4, ROWS, 128), F32),
            pltpu.SemaphoreType.DMA((4,)),
        ],
        compiler_params=PARAMS,
        cost_estimate=cost(40),
        name="attend",
    )(
        lengths,
        place,
        tokens,
        *blocks,
        jnp.asarray(score_bias()),
        jnp.asarray(pool_matrix(), BF16),
        jnp.asarray(halves(), BF16),
    )


def feed(place, plain, tokens, attn, total, cotangent, blocks):
    rows = tokens.shape[0]
    one = per_sequence(LEN, D)
    low = shape_of(rows, D, BF16)
    grads = whole(8, SECOND_ROWS, D)
    return pl.pallas_call(
        functools.partial(feed_kernel, plain),
        grid=(rows // LEN,),
        in_specs=[SMEM] + [one] * 4 + [whole(4, SECOND_ROWS, D)] * 8,
        out_specs=[one] * 4 + [grads] * 4,
        out_shape=[low] * 4 + [jax.ShapeDtypeStruct((8, SECOND_ROWS, D), BF16)] * 4,
        scratch_shapes=[
            vmem(D, D, BF16),
            vmem(FF, D, BF16),
            pltpu.VMEM((4, D, D), BF16),
            vmem(8, D, F32),
            vmem(LEN, D, F32),
            vmem(LEN, D, F32),
            vmem(LEN, 128, F32),
            vmem(LEN, D, BF16),
            vmem(LEN, D, F32),
            vmem(LEN, D, F32),
            vmem(LEN, D, F32),
            vmem(LEN, D, BF16),
            vmem(LEN, D, BF16),
            vmem(56, D, F32),
            vmem(D, D, F32),
            vmem(FF, D, F32),
            pltpu.VMEM((4, D, D), F32),
        ],
        compiler_params=PARAMS,
        cost_estimate=cost(75),
        name="feed",
    )(place, tokens, attn, total, cotangent, *blocks)


def attend_back(lengths, place, plain, tokens, middle_grad, numer_grad, total_grad, kept):
    count = lengths.shape[0]
    one = per_sequence(LEN, D)
    flat = WINDOWS * 2 * QUERIES
    grads = whole(16, FIRST_ROWS, D)
    return pl.pallas_call(
        functools.partial(attend_back_kernel, plain),
        grid=(count,),
        in_specs=[SMEM, SMEM]
        + [one] * 4
        + [pl.BlockSpec(memory_space=pl.ANY)] * 4
        + [whole(3 * D, D), whole(8, D), whole(POOL_CHUNK, POOL_CHUNK), whole(2, 128)],
        out_specs=[one, grads, grads],
        out_shape=[shape_of(count * LEN, D, BF16)]
        + [jax.ShapeDtypeStruct((16, FIRST_ROWS, D), BF16)] * 2,
        scratch_shapes=[
            vmem(ROWS, D, BF16),
            vmem(ROWS, D, BF16),
            vmem(flat, D, BF16),
            pltpu.VMEM((4, ROWS, 128), F32),
            vmem(LEN, 3 * D, BF16),
            vmem(LEN, D, BF16),
            vmem(ROWS, 128, BF16),
            vmem(SIZES[-1], D, F32),
            vmem(16, D, F32),
            vmem(3 * D, D, F32),
            vmem(ROWS, D, BF16),
            vmem(ROWS, D, BF16),
            vmem(ROWS, D, BF16),
            vmem(flat, D, BF16),
            pltpu.SemaphoreType.DMA((4,)),
        ],
        compiler_params=PARAMS,
        cost_estimate=cost(60),
        name="attend_back",
    )(
        lengths,
        place,
        tokens,
        middle_grad,
        numer_grad,
        total_grad,
        *kept,
        jnp.asarray(pool_matrix(), BF16),
        jnp.asarray(halves(), BF16),
    )


def pack_kernel(place, *refs):
    w_query, w_key, w_value, w_out, w_up, w_down, bias_up, bias_down, *norms, first, second = refs
    for part, ref in enumerate((w_query, w_key, w_value)):
        first[part * SHARE : part * SHARE + SHARE, :] = ref[...]
    second[0:SHARE, :] = w_out[...]
    second[SHARE : 5 * SHARE, :] = w_up[...]
    for part in range(4):
        at = (5 + part) * SHARE
        second[at : at + SHARE, :] = w_down[:, D * part : D * part + D]
    device = place[0] * 8 + place[1]
    lane = lax.broadcasted_iota(jnp.int32, (SHARE, D), 1)
    mine = lane == lax.broadcasted_iota(jnp.int32, (SHARE, D), 0) + device * SHARE
    mine = mine.astype(F32).astype(BF16)
    gain_attn, shift_attn, gain_ffn, shift_ffn = norms
    row = lax.broadcasted_iota(jnp.int32, (8, D), 0)

    def rows_of(vectors):
        total = jnp.zeros((8, D), F32)
        for place_of, vector in enumerate(vectors):
            total = jnp.where(row == place_of, nn(vector[...], mine), total)
        return total

    first[3 * SHARE :, :] = rows_of((gain_attn, shift_attn)).astype(BF16)
    lane = lax.broadcasted_iota(jnp.int32, (4 * SHARE, D), 1)
    mine_up = lane == lax.broadcasted_iota(jnp.int32, (4 * SHARE, D), 0) + (device % 8) * 4 * SHARE
    wide = nn(bias_up[...], mine_up.astype(F32).astype(BF16))
    vectors = rows_of((gain_ffn, shift_ffn, bias_down))
    second[9 * SHARE :, :] = jnp.where(row == 3 + device // 8, wide, vectors).astype(BF16)


def pack(place, weights, vectors):
    operands = [w.T for w in weights] + [v.reshape(1, -1) for v in vectors]
    return pl.pallas_call(
        pack_kernel,
        in_specs=[SMEM] + [pl.BlockSpec(memory_space=pltpu.VMEM)] * len(operands),
        out_specs=[pl.BlockSpec(memory_space=pltpu.VMEM)] * 2,
        out_shape=[shape_of(FIRST_ROWS, D, BF16), shape_of(SECOND_ROWS, D, BF16)],
        cost_estimate=cost(2),
        name="pack",
    )(place, *operands)


def across(values, bits):
    return lax.ppermute(values, "fsdp", [(i, i ^ bits) for i in range(8)])


def along(values, step):
    return lax.ppermute(values, "dp", [(i, (i + step) % 4) for i in range(4)])


def gather_rows(packed):
    return jnp.stack([packed] + [along(packed, step) for step in (1, 2, 3)])


def shares_along(blocks):
    return [blocks[0]] + [along(blocks[step], step) for step in (1, 2, 3)]


def added(parts):
    return sum(part.astype(F32) for part in parts)


def spread(vector, index, devices):
    share = vector.shape[0]
    full = jnp.tile(vector, devices)
    mine = lax.broadcasted_iota(jnp.int32, full.shape, 0) // share == index
    return jnp.where(mine, full, jnp.zeros_like(full)).reshape(-1, D)


def finish_kernel(place, *refs):
    first, second, outs = refs[:4], refs[4:8], refs[8:]
    query, key, value, out, up, down, bias_up, bias_down, *norms = outs

    def summed(parts, rows):
        return sum(part[rows, :].astype(F32) for part in parts)

    for place_of, ref in enumerate((query, key, value)):
        ref[...] = summed(first, slice(place_of * SHARE, place_of * SHARE + SHARE))
    out[...] = summed(second, slice(0, SHARE))
    up[...] = summed(second, slice(SHARE, 5 * SHARE))
    for part in range(4):
        at = (5 + part) * SHARE
        down[:, D * part : D * part + D] = summed(second, slice(at, at + SHARE))
    device = place[0] * 8 + place[1]
    shift = lax.rem(D - device * SHARE, D)
    mine_first = pltpu.roll(summed(first, slice(3 * SHARE, FIRST_ROWS)), shift, 1)
    vectors = summed(second, slice(9 * SHARE, SECOND_ROWS))
    mine_second = pltpu.roll(vectors, shift, 1)
    row = lax.broadcasted_iota(jnp.int32, (8, D), 0)
    wide = jnp.sum(jnp.where(row == 3 + device // 8, vectors, 0.0), axis=0, keepdims=True)
    wide = pltpu.roll(jnp.broadcast_to(wide, (8, D)), lax.rem(D - (device % 8) * 4 * SHARE, D), 1)
    bias_up[...] = wide[0:1, : 4 * SHARE]
    bias_down[...] = mine_second[2:3, :SHARE]
    gain_attn, shift_attn, gain_ffn, shift_ffn = norms
    gain_attn[...] = mine_first[0:1, :SHARE]
    shift_attn[...] = mine_first[1:2, :SHARE]
    gain_ffn[...] = mine_second[0:1, :SHARE]
    shift_ffn[...] = mine_second[1:2, :SHARE]


def finish(place, first, second):
    shapes = [(SHARE, D)] * 4 + [(4 * SHARE, D), (SHARE, FF), (1, 4 * SHARE)] + [(1, SHARE)] * 5
    grads = pl.pallas_call(
        finish_kernel,
        in_specs=[SMEM] + [pl.BlockSpec(memory_space=pltpu.VMEM)] * 8,
        out_specs=[pl.BlockSpec(memory_space=pltpu.VMEM)] * 12,
        out_shape=[shape_of(rows, columns, F32) for rows, columns in shapes],
        cost_estimate=cost(2),
        name="finish",
    )(place, *first, *second)
    return [grad.T for grad in grads[:6]] + [grad.reshape(-1) for grad in grads[6:]]


def exchange_permutes(place, tokens, lengths, weights, vectors, cotangent):
    first, second = pack(place, weights, vectors)
    rows = gather_rows(first)
    near = jnp.concatenate([rows] + [across(rows, bits) for bits in (2, 4, 6)])
    second_rows = gather_rows(second)
    near, second_rows = lax.optimization_barrier((near, second_rows))
    first_blocks = (near, across(near, 1))
    first_blocks, second_rows = lax.optimization_barrier((first_blocks, second_rows))
    diagonal = across(second_rows, 6)
    others = [across(second_rows, bits) for bits in (2, 4)] + [diagonal, across(second_rows, 1)]
    *kept, attn, total, weights, gains = attend(lengths, place, False, tokens, first_blocks)
    kept += [weights, gains]
    attn, total, others = lax.optimization_barrier((attn, total, others))
    *others, partner = others
    second_blocks = [second_rows, *others, partner] + [across(other, 1) for other in others]
    output, middle_grad, numer_grad, total_grad, *parts = feed(
        place, False, tokens, attn, total, cotangent, second_blocks
    )
    others = [across(parts[chip], bits) for chip, bits in ((3, 6), (2, 4), (1, 2))]
    grad_tokens, near, far = attend_back(
        lengths, place, False, tokens, middle_grad, numer_grad, total_grad, kept
    )
    partner = across(far, 1)
    near, partner, others = lax.optimization_barrier((near, partner, others))
    second = added([parts[0]] + others).astype(BF16)
    second = added([second[:4], across(second[4:], 1)]).astype(BF16)
    first = added([near, partner]).astype(BF16).reshape(4, 4, FIRST_ROWS, D)
    by_x, by_y = first[:, :2], first[:, 2:]
    sent_x = across(jnp.stack([by_x[1], by_x[3]]), 2)
    sent_y = across(jnp.stack([by_y[2], by_y[3]]), 4)
    by_x = added([jnp.stack([by_x[0], by_x[2]]), sent_x]).astype(BF16)
    by_y = added([jnp.stack([by_y[0], by_y[1]]), sent_y]).astype(BF16)
    by_x = added([by_x[0], across(by_x[1], 4)]).astype(BF16)
    by_y = added([by_y[0], across(by_y[1], 2)]).astype(BF16)
    first = shares_along([by_x[0], by_x[1], by_y[0], by_y[1]])
    second = shares_along(second)
    return output, grad_tokens, finish(place, first, second)


def exchange_plain(index, devices, tokens, lengths, weights, vectors, cotangent):
    w_query, w_key, w_value, w_out, w_up, w_down = weights
    bias_up, bias_down, gain_attn, shift_attn, gain_ffn, shift_ffn = vectors
    share = D // devices

    def gathered(rows):
        return lax.all_gather(rows, AXES, axis=0, tiled=True).reshape(32, SHARE, D)

    def vector_rows(parts):
        rows = jnp.concatenate([spread(part, index, devices) for part in parts])
        rows = lax.psum(rows, AXES)
        pad = jnp.zeros((8 - rows.shape[0], D), rows.dtype)
        rows = jnp.concatenate([rows, pad])[None]
        return jnp.concatenate([rows, jnp.zeros((31, 8, D), rows.dtype)])

    def halved(parts):
        blocks = jnp.concatenate(parts, axis=1)
        return blocks[:16], blocks[16:]

    place = jnp.zeros((2,), jnp.int32)
    first_blocks = halved(
        [gathered(w.T) for w in (w_query, w_key, w_value)]
        + [vector_rows([gain_attn, shift_attn])]
    )
    up = lax.all_gather(w_up.T, AXES, axis=0, tiled=True).reshape(32, 4 * SHARE, D)
    down = lax.all_gather(w_down.T, AXES, axis=0, tiled=True).reshape(32, SHARE, 4, D)
    down = jnp.transpose(down, (0, 2, 1, 3)).reshape(32, 4 * SHARE, D)
    vectors = vector_rows([gain_ffn, shift_ffn, bias_down, bias_up])
    second_blocks = jnp.concatenate([gathered(w_out.T), up, down, vectors], axis=1)
    second_blocks = [second_blocks[at : at + 4] for at in range(0, 32, 4)]
    *kept, attn, total, weights, gains = attend(lengths, place, True, tokens, first_blocks)
    kept += [weights, gains]
    output, middle_grad, numer_grad, total_grad, *parts = feed(
        place, True, tokens, attn, total, cotangent, second_blocks
    )
    second = jnp.stack(parts).reshape(4, 2, 4, SECOND_ROWS, D)
    second = jnp.transpose(second, (1, 0, 2, 3, 4)).reshape(32, SECOND_ROWS, D)
    grad_tokens, near, far = attend_back(
        lengths, place, True, tokens, middle_grad, numer_grad, total_grad, kept
    )
    first = jnp.concatenate([near, far])

    def scattered(rows):
        rows = rows.reshape(devices, -1, D)
        return lax.psum_scatter(rows, AXES, scatter_dimension=0, tiled=False).astype(F32)

    down = second[:, 5 * SHARE : 9 * SHARE].reshape(32, 4, SHARE, D)
    down = scattered(jnp.transpose(down, (0, 2, 1, 3)).reshape(32, 4 * SHARE, D))
    down = jnp.transpose(down.reshape(share, 4, D), (1, 0, 2)).reshape(4 * share, D)
    first_vectors = lax.psum(first[0, 3 * SHARE :].astype(F32), AXES)
    second_vectors = lax.psum(second[0, 9 * SHARE :].astype(F32), AXES)
    down = jnp.transpose(down.reshape(4, share, D), (0, 2, 1)).reshape(FF, share)

    def own(row):
        return lax.dynamic_slice(row, (index * share,), (share,))

    return (
        output,
        grad_tokens,
        [
            *[scattered(first[:, p * SHARE : p * SHARE + SHARE]).T for p in range(3)],
            scattered(second[:, :SHARE]).T,
            scattered(second[:, SHARE : 5 * SHARE]).T,
            down,
            lax.dynamic_slice(second_vectors[3:7].reshape(FF), (index * 4 * share,), (4 * share,)),
            own(second_vectors[2]),
            own(first_vectors[0]),
            own(first_vectors[1]),
            own(second_vectors[0]),
            own(second_vectors[1]),
        ],
    )


def on_device(sizes, tokens, lengths, *rest):
    weights, vectors, cotangent = rest[:6], rest[6:12], rest[12]
    if sizes == (4, 8):
        place = jnp.stack([lax.axis_index("dp"), lax.axis_index("fsdp")]).astype(jnp.int32)
        output, grad_tokens, grads = exchange_permutes(
            place, tokens, lengths, weights, vectors, cotangent
        )
    else:
        index = lax.axis_index(AXES)
        output, grad_tokens, grads = exchange_plain(
            index, sizes[0] * sizes[1], tokens, lengths, weights, vectors, cotangent
        )
    return (output, grad_tokens, *grads)


def solution(mesh):
    rows = P(AXES, None)
    columns = P(None, AXES)
    vector = P(AXES)
    sizes = (mesh.shape["dp"], mesh.shape["fsdp"])
    return jax.shard_map(
        functools.partial(on_device, sizes),
        mesh=mesh,
        in_specs=(rows, vector) + (columns,) * 6 + (vector,) * 6 + (rows,),
        out_specs=(rows, rows) + (columns,) * 6 + (vector,) * 6,
        check_vma=False,
    )
```
